32 devices in a mesh: res: 8 (over z, x), samp: 4 (over y, core).
Axes of the slice: x: 2, y: 2, z: 4, core: 2. Of those that a mesh axis runs over, the one named last changes fastest.
Arguments:
- coords_pred: float32 [16, 3, 24576], P('samp', None, 'res'), may hold values from -130 to 130
- coords_true: float32 [3, 24576], P(None, 'res'), may hold values from -55 to 55
- atom_kind: int32 [24576], P('res'), may hold values from 0 to 2
- partners: int32 [192, 5], P('res'), may hold values from 0 to 191, as said below
- noise_level: float32 [16], P('samp'), may hold values from 2 to 32
Outputs:
- copy_loss: float32 [16], P('samp')
- mean_loss: float32 [], replicated
- coord_grad: float32 [16, 3, 24576], P('samp', None, 'res')
The draws below stay inside these ranges and needn't reach their ends.
Inputs may be any that keep to these rules, and one draw needn't show every extreme that they name: `partners`: slot 0 of tile g holds g; the other used slots hold distinct tiles g' with 0 < |g' - g| <= 2, and unused slots hold g again; the pairing is symmetric (g' is listed for g exactly when g is listed for g'); some tile uses all 5 slots.
All inputs are finite; a program needn't handle non-finite values.
Results may differ from the reference program's by a relative error of at most 0.0005.
Values sent between devices are 32-bit elements; how exact they have to be, the bound alone decides.
No kernel may reach another device: no remote copies, remote signals or barrier semaphores. Data moves between devices by JAX's collectives and lax.ppermute only.
A program may use at most 64 MiB of HBM per device.

```python
import math
import jax
import jax.numpy as jnp
from jax import lax

TILE = 128
BAND = 2
SLOTS = 5
NTILES = 192
ATOMS = 24576
COPIES = 16


def tile_chain(seed_key):
    tile_pos = (jnp.arange(ATOMS) // TILE).astype(jnp.float32)
    centre = 40.0 * jnp.stack([jnp.sin(0.11 * tile_pos), jnp.sin(0.13 * tile_pos + 1.0), jnp.sin(0.17 * tile_pos + 2.0)], axis=0)
    offsets = jnp.clip(5.0 * jax.random.normal(seed_key, (3, ATOMS), jnp.float32), -15.0, 15.0)
    return centre + offsets


def draw_coords_true(key, part):
    return tile_chain(jax.random.fold_in(key, 11)).astype(jnp.float32)


def draw_coords_pred(key, part):
    true_coords = tile_chain(jax.random.fold_in(key, 11))
    base_key = jax.random.fold_in(key, 23)
    key_axis, key_angle, key_move, key_size, key_noise = jax.random.split(base_key, 5)
    spin_axis = jax.random.normal(key_axis, (COPIES, 3), jnp.float32)
    spin_axis = spin_axis / jnp.sqrt(jnp.sum(spin_axis * spin_axis, axis=1, keepdims=True) + 1e-06)
    spin_angle = jax.random.uniform(key_angle, (COPIES,), jnp.float32, -math.pi, math.pi)
    cosine = jnp.cos(spin_angle)
    sine = jnp.sin(spin_angle)
    ux = spin_axis[:, 0]
    uy = spin_axis[:, 1]
    uz = spin_axis[:, 2]
    rest = 1.0 - cosine
    row_one = jnp.stack([cosine + ux * ux * rest, ux * uy * rest - uz * sine, ux * uz * rest + uy * sine], axis=1)
    row_two = jnp.stack([uy * ux * rest + uz * sine, cosine + uy * uy * rest, uy * uz * rest - ux * sine], axis=1)
    row_three = jnp.stack([uz * ux * rest - uy * sine, uz * uy * rest + ux * sine, cosine + uz * uz * rest], axis=1)
    spin = jnp.stack([row_one, row_two, row_three], axis=1)
    rotated = spin[:, :, 0, None] * true_coords[0] + spin[:, :, 1, None] * true_coords[1] + spin[:, :, 2, None] * true_coords[2]
    translation = jax.random.uniform(key_move, (COPIES, 3), jnp.float32, -20.0, 20.0)
    amplitude = jnp.exp(jax.random.uniform(key_size, (COPIES,), jnp.float32, math.log(0.5), math.log(3.0)))
    noise_field = jnp.clip(jax.random.normal(key_noise, (COPIES, 3, ATOMS), jnp.float32), -4.0, 4.0)
    return (rotated + translation[:, :, None] + amplitude[:, None, None] * noise_field).astype(jnp.float32)


def partner_table(seed_key):
    pair_bits = jax.random.randint(seed_key, (NTILES, BAND), 0, 2)
    full_tile = jax.random.randint(jax.random.fold_in(seed_key, 1), (), BAND, NTILES - BAND)
    tile_index = jnp.arange(NTILES, dtype=jnp.int32)[:, None]
    offset_index = jnp.arange(BAND, dtype=jnp.int32)[None, :]
    forced = (tile_index == full_tile) | (tile_index == full_tile - offset_index - 1)
    pair_bits = jnp.where(forced, 1, pair_bits)
    upper_ok = (pair_bits == 1) & (tile_index + offset_index + 1 < NTILES)
    lower_rows = jnp.clip(tile_index - offset_index - 1, 0, NTILES - 1)
    lower_bits = pair_bits[lower_rows, jnp.broadcast_to(offset_index, (NTILES, BAND))]
    lower_ok = (lower_bits == 1) & (tile_index - offset_index - 1 >= 0)
    candidates = jnp.concatenate([tile_index, tile_index + offset_index + 1, tile_index - offset_index - 1], axis=1)
    present = jnp.concatenate([jnp.ones((NTILES, 1), jnp.int32), upper_ok.astype(jnp.int32), lower_ok.astype(jnp.int32)], axis=1)
    sort_keys = (1 - present) * SLOTS + jnp.arange(SLOTS, dtype=jnp.int32)[None, :]
    slot_order = jnp.argsort(sort_keys, axis=1)
    sorted_tiles = jnp.take_along_axis(candidates, slot_order, axis=1)
    sorted_present = jnp.take_along_axis(present, slot_order, axis=1)
    return jnp.where(sorted_present == 1, sorted_tiles, tile_index).astype(jnp.int32)


def draw_partners(key, part):
    return partner_table(jax.random.fold_in(key, 5))


def place_ends(drawn, rng, least, high):
    shape = drawn.shape
    index_at = [jax.random.randint(jax.random.fold_in(rng, axis), (), 0, shape[axis]) for axis in range(len(shape))]
    drawn = drawn.at[tuple(index_at)].set(least)
    longest = shape.index(max(shape))
    index_at[longest] = (index_at[longest] + 1) % shape[longest]
    return drawn.at[tuple(index_at)].set(high)


def block_scale(stream_key, extent, shards, least, top_value):
    gain, own = 1.0, jax.random.fold_in(stream_key, 6)
    for dim, blocks in shards:
        heights = jnp.exp(jax.random.uniform(jax.random.fold_in(own, dim), (blocks,), jnp.float32, least / len(shards), top_value / len(shards)))
        gain = gain * jnp.repeat(heights, extent[dim] // blocks).reshape([-1 if axis == dim else 1 for axis in range(len(extent))])
    return gain


def setup_inputs(seed: int = 0) -> dict:
    seeds = jax.random.split(jax.random.key(seed), 6)
    return {
        "coords_pred": draw_coords_pred(jax.random.fold_in(seeds[5], 71), 0),
        "coords_true": draw_coords_true(jax.random.fold_in(seeds[5], 71), 0),
        "atom_kind": place_ends(jax.random.randint(seeds[2], (ATOMS,), 0, 3), jax.random.fold_in(seeds[2], 1), 0, 2).astype(jnp.int32),
        "partners": draw_partners(jax.random.fold_in(seeds[5], 71), 0),
        "noise_level": jnp.clip(jnp.exp(math.log(32.0) - 2.7725887 * jax.random.uniform(seeds[4], (COPIES,), jnp.float32) ** block_scale(seeds[4], (COPIES,), ((0, 4),), -0.2, 0.2)), 2.0, 32.0),
    }


precise = lax.Precision.HIGHEST
thresholds = (0.5, 1.0, 2.0, 4.0)
sigma_data = 16.0

def atom_weight(atom_kind):
    return jnp.where(atom_kind == 1, 5.0, jnp.where(atom_kind == 2, 10.0, 1.0)).astype(jnp.float32)

def atom_cutoff(atom_kind):
    return jnp.where(atom_kind == 1, 30.0, 15.0).astype(jnp.float32)

def moments(coords_pred, coords_true, weight):
    weight_sum = jnp.sum(weight)
    pred_sum = jnp.einsum('sca,a->sc', coords_pred, weight, precision=precise)
    true_sum = jnp.einsum('ca,a->c', coords_true, weight, precision=precise)
    cross = jnp.einsum('sca,da->scd', coords_pred * weight, coords_true, precision=precise)
    return (weight_sum, pred_sum, true_sum, cross)

def rotation_of(weight_sum, pred_sum, true_sum, cross):
    pred_mean = pred_sum / weight_sum
    true_mean = true_sum / weight_sum
    covariance = cross - pred_sum[:, :, None] * true_mean[None, None, :]
    frobenius = jnp.sqrt(lax.optimization_barrier(jnp.sum(covariance * covariance, axis=(1, 2))))
    polar_factor = covariance / frobenius[:, None, None]
    for sweep_index in range(20):
        gram_matrix = jnp.einsum('sab,scb->sac', polar_factor, polar_factor, precision=precise)
        polar_factor = 1.5 * polar_factor - 0.5 * jnp.einsum('sac,scd->sad', gram_matrix, polar_factor, precision=precise)
    return (polar_factor, pred_mean, true_mean)

def aligned_truth(rotation, pred_mean, true_mean, coords_true):
    centred = coords_true - true_mean[:, None]
    return jnp.einsum('scd,da->sca', rotation, centred, precision=precise) + pred_mean[:, :, None]

def pair_terms(own_rows, partner_rows, own_tile, partner_tiles, copies):
    tile_len = own_rows.shape[-1]
    slot_count = partner_tiles.shape[0]
    own_pred = own_rows[:3 * copies].reshape(copies, 3, tile_len)
    own_true = own_rows[3 * copies:3 * copies + 3]
    own_cut = own_rows[3 * copies + 3]
    far_pred = partner_rows[:3 * copies].reshape(copies, 3, slot_count, tile_len)
    far_true = partner_rows[3 * copies:3 * copies + 3]
    far_cut = partner_rows[3 * copies + 3]
    pred_terms = []
    true_terms = []
    for component in range(3):
        coord_gap = own_pred[:, component, None, :, None] - far_pred[:, component, :, None, :]
        pred_terms.append(coord_gap * coord_gap)
        true_gap = own_true[component][None, :, None] - far_true[component][:, None, :]
        true_terms.append(true_gap * true_gap)
    pred_dist = jnp.sqrt(pred_terms[0] + pred_terms[1] + pred_terms[2] + 1e-06)
    true_dist = jnp.sqrt(true_terms[0] + true_terms[1] + true_terms[2] + 1e-06)
    slot_used = (jnp.arange(slot_count) == 0) | (partner_tiles != own_tile)
    same_atom = jnp.arange(tile_len)[:, None] == jnp.arange(tile_len)[None, :]
    diagonal = (partner_tiles == own_tile)[:, None, None] & same_atom[None]
    usable = slot_used[:, None, None] & jnp.logical_not(diagonal)
    mask_fwd = jnp.where(usable & (true_dist < far_cut[:, None, :]), 1.0, 0.0).astype(jnp.float32)
    mask_back = jnp.where(usable & (true_dist < own_cut[None, :, None]), 1.0, 0.0).astype(jnp.float32)
    spread = jnp.abs(pred_dist - true_dist)
    score_parts = []
    slope_parts = []
    for threshold in thresholds:
        squash = jax.nn.sigmoid(threshold - spread)
        score_parts.append(squash)
        slope_parts.append(squash * (1.0 - squash))
    pair_score = 0.25 * (score_parts[0] + score_parts[1] + score_parts[2] + score_parts[3])
    pair_slope = -0.25 * (slope_parts[0] + slope_parts[1] + slope_parts[2] + slope_parts[3])
    pair_count = jnp.sum(mask_fwd)
    score_sum = lax.optimization_barrier(jnp.sum(mask_fwd * pair_score, axis=(1, 2, 3)))
    factor = (mask_fwd + mask_back) * pair_slope * jnp.sign(pred_dist - true_dist) / pred_dist
    weight_row = lax.optimization_barrier(jnp.sum(factor, axis=(1, 3)))
    pull_parts = []
    for component in range(3):
        remote = jnp.einsum('skij,skj->si', factor, far_pred[:, component], precision=precise)
        pull_parts.append(own_pred[:, component] * weight_row - remote)
    return (pair_count, score_sum, jnp.stack(pull_parts, axis=1))

def reference(coords_pred, coords_true, atom_kind, partners, noise_level):
    copies = coords_pred.shape[0]
    atom_total = coords_pred.shape[2]
    weight = atom_weight(atom_kind)
    cutoff = atom_cutoff(atom_kind)
    weight_sum, pred_sum, true_sum, cross = moments(coords_pred, coords_true, weight)
    rotation, pred_mean, true_mean = rotation_of(weight_sum, pred_sum, true_sum, cross)
    target = aligned_truth(rotation, pred_mean, true_mean, coords_true)
    deviation = coords_pred - target
    square_err = lax.optimization_barrier(jnp.sum(weight * deviation * deviation, axis=(1, 2)))
    packed = jnp.concatenate([coords_pred.reshape(3 * copies, atom_total), coords_true, cutoff[None]], axis=0)
    tile_rows = packed.reshape(packed.shape[0], NTILES, TILE)

    def one_tile(tile_id):
        own_rows = lax.dynamic_index_in_dim(tile_rows, tile_id, 1, keepdims=False)
        partner_tiles = lax.dynamic_index_in_dim(partners, tile_id, 0, keepdims=False)
        partner_rows = jnp.take(tile_rows, partner_tiles, axis=1)
        return pair_terms(own_rows, partner_rows, tile_id, partner_tiles, copies)
    counts, scores, pull_tiles = lax.map(one_tile, jnp.arange(NTILES, dtype=jnp.int32))
    pair_total = jnp.sum(counts)
    score_total = lax.optimization_barrier(jnp.sum(scores, axis=0))
    pull_field = jnp.moveaxis(pull_tiles, 0, 2).reshape(copies, 3, atom_total)
    loss_weight = (noise_level * noise_level + sigma_data * sigma_data) / (noise_level * sigma_data * (noise_level * sigma_data))
    mean_square = square_err / (3.0 * weight_sum)
    copy_loss = loss_weight * mean_square + 1.0 - score_total / pair_total
    mean_loss = jnp.mean(copy_loss)
    grad_scale = 16.0 * atom_total
    coord_grad = grad_scale * (2.0 * loss_weight[:, None, None] * weight * deviation / (3.0 * weight_sum) - pull_field / pair_total)
    return (copy_loss, mean_loss, coord_grad)
```

```python
import functools

import jax
import jax.numpy as jnp
from jax import lax
from jax.experimental import pallas as pl
from jax.experimental.pallas import tpu as pltpu
from jax.sharding import PartitionSpec as P

LANES = 128
BAND = 2
SWEEPS = 20
SIGMA = 16.0
HALF_THRESHOLDS = (0.25, 0.5, 1.0, 2.0)
EPS = 0.25e-6
F32 = jnp.float32


def roll(x, shift, axis=1):
    return pltpu.roll(x, shift, axis)


def two_sum(a, b):
    s = a + b
    t = s - a
    return s, (a - (s - t)) + (b - t)


def two_prod(a, b):
    def halves(x):
        t = x * 4097.0
        h = t - (t - x)
        return h, x - h

    p = a * b
    ah, al = halves(a)
    bh, bl = halves(b)
    return p, ((ah * bh - p) + ah * bl + al * bh) + al * bl


def pair_add(x, y):
    s, e = two_sum(x[0], y[0])
    return two_sum(s, e + (x[1] + y[1]))


def pair_neg(x):
    return -x[0], -x[1]


def pair_mul(x, y):
    p, e = two_prod(x[0], y[0])
    return two_sum(p, e + (x[0] * y[1] + x[1] * y[0]))


def pair_div(x, w):
    q = x[0] / w
    p, e = two_prod(q, w)
    return two_sum(q, (((x[0] - p) - e) + x[1]) / w)


def pair_kernel(base_ref, part_ref, pred_ref, true_ref, kind_ref, lo_ref, hi_ref, pull_ref, stat_ref,
                x_ref, xr_ref, s_ref, td_ref, w_ref, pi_ref, aj_ref, sc_ref, cn_ref, *, copies, tiles):
    base = base_ref[0]
    rows = 3 * copies
    window = tiles + 2 * BAND
    for q in range(BAND):
        x_ref[q] = lo_ref[:, q * LANES:(q + 1) * LANES]
        x_ref[window - BAND + q] = hi_ref[:, q * LANES:(q + 1) * LANES]

    @pl.loop(0, tiles)
    def _(t):
        sl = pl.ds(pl.multiple_of(t * LANES, LANES), LANES)
        kind = kind_ref[:, sl]
        for s in range(copies):
            x_ref[t + BAND, 3 * s:3 * s + 3, :] = pred_ref[s, :, sl] * 0.5
        x_ref[t + BAND, rows:rows + 3, :] = true_ref[:, sl] * 0.5
        x_ref[t + BAND, rows + 3:rows + 4, :] = jnp.where(kind == 1, 15.0, 7.5)

    @pl.loop(0, window)
    def _(t):
        x = x_ref[t]
        for b in range(16):
            xr_ref[t, b] = roll(x, 127 - 8 * b)
        pi_ref[t] = jnp.zeros(pi_ref.shape[1:], F32)

    sc_ref[...] = jnp.zeros_like(sc_ref)
    cn_ref[...] = jnp.zeros_like(cn_ref)
    row = lax.broadcasted_iota(jnp.int32, (8, LANES), 0)

    zero = jnp.zeros((16, LANES), F32)

    def add_tile(t, carry):
        acc, total = carry
        x = x_ref[t + BAND]
        kind = kind_ref[:, pl.ds(pl.multiple_of(t * LANES, LANES), LANES)]
        weight = jnp.where(kind == 1, 5.0, jnp.where(kind == 2, 10.0, 1.0))
        wx = x * weight
        terms = [wx * x[rows + c:rows + c + 1] for c in range(3)] + [wx, wx * x]
        out = []
        for (high, low), term in zip(acc, terms):
            s, e = two_sum(high, term)
            out.append((s, low + e))
        return tuple(out), total + weight

    acc, total = lax.fori_loop(0, tiles, add_tile, (tuple((zero, zero) for _ in range(5)), jnp.zeros((1, LANES), F32)))
    lane = lax.broadcasted_iota(jnp.int32, (16, LANES), 1)
    row16 = lax.broadcasted_iota(jnp.int32, (16, LANES), 0)
    for k in (64, 32, 16, 8, 4, 2, 1):
        acc = tuple(pair_add(a, (roll(a[0], k), roll(a[1], k))) for a in acc)
    high, low = zero, zero
    for q in range(5):
        high = jnp.where(lane == q, acc[q][0], high)
        low = jnp.where(lane == q, acc[q][1], low)

    def body(g, blocks, share):
        st = [s_ref[rows + c] for c in range(3)]
        cut_j = s_ref[rows + 3]
        count = jnp.zeros((8, LANES), F32)
        for b in range(blocks):
            d2 = None
            for c in range(3):
                gap = xr_ref[g, b, rows + c:rows + c + 1, :] - st[c]
                d2 = gap * gap if d2 is None else d2 + gap * gap
            d2 = d2 + EPS
            td = d2 * lax.rsqrt(d2)
            cut_i = xr_ref[g, b, rows + 3:rows + 4, :]
            w = jnp.where(td < cut_j, 0.0625, 0.0) + jnp.where(td < cut_i, 0.0625, 0.0)
            if blocks == 8 and b == 7:
                w = jnp.where(row == 7, w * 0.5, w)
            td_ref[b] = td
            w_ref[b] = w
            count = count + w
        cn_ref[...] += count * share
        for s in range(copies):
            sj = [s_ref[3 * s + c] for c in range(3)]
            to_i = [jnp.zeros((8, LANES), F32) for _ in range(3)]
            to_j = [jnp.zeros((8, LANES), F32) for _ in range(3)]
            score = jnp.zeros((8, LANES), F32)
            for b in range(blocks):
                gap = [xr_ref[g, b, 3 * s + c:3 * s + c + 1, :] - sj[c] for c in range(3)]
                d2 = gap[0] * gap[0] + gap[1] * gap[1] + gap[2] * gap[2] + EPS
                r = lax.rsqrt(d2)
                diff = d2 * r - td_ref[b]
                spread = jnp.abs(diff)
                u = [jnp.tanh(t - spread) for t in HALF_THRESHOLDS]
                w = w_ref[b]
                score = score + w * ((u[0] + u[1]) + (u[2] + u[3]))
                slope = ((u[0] * u[0] + u[1] * u[1]) + (u[2] * u[2] + u[3] * u[3])) - 4.0
                sign = jnp.maximum(jnp.minimum(diff * 1e30, w), -w)
                f = slope * r * sign
                for c in range(3):
                    h = f * gap[c]
                    to_j[c] = to_j[c] + h
                    to_i[c] = to_i[c] + roll(h, 8 * b + 1)
            sc_ref[s] += score * share
            for c in range(3):
                pi_ref[g, 3 * s + c] += to_i[c]
                aj_ref[3 * s + c] -= to_j[c]

    @pl.loop(0, tiles + BAND)
    def _(t):
        j = t + BAND
        aj_ref[...] = jnp.zeros_like(aj_ref)
        for m in range(rows + 4):
            s_ref[m] = pltpu.roll(jnp.broadcast_to(x_ref[j, m:m + 1, :], (8, LANES)), 0, 1, stride=1, stride_axis=0)

        @pl.when(t < tiles)
        def _():
            body(j, 8, 1.0)

        @pl.loop(1, BAND + 1)
        def _(o):
            g = t - o
            owner = jnp.clip(jnp.where(t < tiles, t, g), 0, tiles - 1)
            other = base + jnp.where(t < tiles, g, t)
            hit = jnp.bool_(False)
            for k in range(1, part_ref.shape[1]):
                hit = hit | (part_ref[owner, k] == other)

            @pl.when(hit & ((t < tiles) | (g < tiles)))
            def _():
                body(j - o, 16, jnp.where((t >= tiles) | (g < 0), 0.5, 1.0))

        for m in range(rows):
            a = aj_ref[m]
            for k in (4, 2, 1):
                a = a + roll(roll(a, 8 - k, 0), LANES - k, 1)
            pi_ref[j, m] += jnp.where(row == 0, a, 0.0)

    @pl.loop(0, tiles)
    def _(t):
        sl = pl.ds(pl.multiple_of(t * LANES, LANES), LANES)
        for s in range(copies):
            for c in range(3):
                pull_ref[s, c:c + 1, sl] = jnp.sum(pi_ref[t + BAND, 3 * s + c], axis=0, keepdims=True)

    sums = [jnp.sum(sc_ref[s], keepdims=True) for s in range(copies)]
    sums += [jnp.sum(cn_ref[...], keepdims=True), jnp.sum(total, keepdims=True)]
    column = zero
    for i, value in enumerate(sums):
        column = jnp.where(row16 == i, value, column)
    stat_ref[0] = jnp.where(lane == 5, column, high)
    stat_ref[1] = low


def finish_kernel(stat_ref, noise_ref, pred_ref, true_ref, kind_ref, pull_ref, loss_ref, grad_ref, m_ref, k_ref, *, copies, tiles, atoms):
    rows = 3 * copies
    stats = [stat_ref[0], stat_ref[1]]

    def per_copy(c, q, scale):
        return tuple(stat_ref[part, pl.ds(c, copies, stride=3), :][:, q:q + 1] * scale for part in range(2))

    def shared(r, q, scale):
        return tuple(stats[part][r:r + 1, q:q + 1] * scale for part in range(2))

    def wide(x):
        return tuple(jnp.broadcast_to(v, (copies, LANES)) for v in x)

    weight_sum = jnp.broadcast_to(stats[0][copies + 1:copies + 2, 5:6], (copies, LANES))
    count = jnp.broadcast_to(stats[0][copies:copies + 1, 5:6], (copies, LANES)) * 16.0
    score = jnp.broadcast_to(stats[0][0:copies, 5:6], (copies, LANES)) * 2.0 + 0.5 * count
    pred_sum = [wide(per_copy(c, 3, 2.0)) for c in range(3)]
    true_sum = [wide(shared(rows + c, 3, 2.0)) for c in range(3)]
    pred_mean = [pair_div(x, weight_sum) for x in pred_sum]
    true_mean = [pair_div(x, weight_sum) for x in true_sum]
    cov = [[pair_add(wide(per_copy(c, d, 4.0)), pair_neg(pair_mul(pred_sum[c], true_mean[d]))) for d in range(3)] for c in range(3)]
    ct = {}
    for d in range(3):
        for e in range(d + 1):
            ct[d, e] = pair_add(wide(shared(rows + d, e, 4.0)), pair_neg(pair_mul(true_sum[d], true_mean[e])))
    var = None
    for c in range(3):
        term = pair_add(wide(per_copy(c, 4, 4.0)), pair_neg(pair_mul(pred_sum[c], pred_mean[c])))
        var = term if var is None else pair_add(var, term)

    x = [[cov[c][d][0] for d in range(3)] for c in range(3)]
    frobenius = jnp.sqrt(sum(x[c][d] * x[c][d] for c in range(3) for d in range(3)))
    x = [[x[c][d] / frobenius for d in range(3)] for c in range(3)]

    def sweep(_, flat):
        x = [flat[0:3], flat[3:6], flat[6:9]]
        gram = {}
        for a in range(3):
            for b in range(a + 1):
                gram[a, b] = gram[b, a] = x[a][0] * x[b][0] + x[a][1] * x[b][1] + x[a][2] * x[b][2]
        return tuple(1.5 * x[a][d] - 0.5 * (gram[a, 0] * x[0][d] + gram[a, 1] * x[1][d] + gram[a, 2] * x[2][d])
                     for a in range(3) for d in range(3))

    flat = lax.fori_loop(0, SWEEPS, sweep, tuple(v for line in x for v in line))
    x = [flat[0:3], flat[3:6], flat[6:9]]

    square = var
    nothing = jnp.zeros((copies, LANES), F32)
    for c in range(3):
        for d in range(3):
            square = pair_add(square, pair_mul((-2.0 * x[c][d], nothing), cov[c][d]))
    for d in range(3):
        for e in range(d + 1):
            gram = None
            for c in range(3):
                term = two_prod(x[c][d], x[c][e])
                gram = term if gram is None else pair_add(gram, term)
            if d != e:
                gram = (2.0 * gram[0], 2.0 * gram[1])
            square = pair_add(square, pair_mul(gram, ct[d, e]))

    row = lax.broadcasted_iota(jnp.int32, (copies, LANES), 0)
    noise = nothing
    for s in range(copies):
        noise = jnp.where(row == s, noise_ref[s], noise)
    loss_weight = (noise * noise + SIGMA * SIGMA) / (noise * SIGMA * (noise * SIGMA))
    mean_square = (square[0] + square[1]) / (3.0 * weight_sum)
    loss_ref[...] = loss_weight * mean_square + 1.0 - score / count

    grad_scale = 16.0 * atoms
    for c in range(3):
        for d in range(3):
            m_ref[d, pl.ds(c, copies, stride=3), :] = x[c][d]
        m_ref[3, pl.ds(c, copies, stride=3), :] = pred_mean[c][0]
        m_ref[4, pl.ds(c, copies, stride=3), :] = grad_scale * 2.0 * loss_weight / (3.0 * weight_sum)
        m_ref[5, pl.ds(c, copies, stride=3), :] = grad_scale / count
        k_ref[c:c + 1, :] = true_mean[c][0][0:1]

    @pl.loop(0, tiles)
    def _(t):
        sl = pl.ds(pl.multiple_of(t * LANES, LANES), LANES)
        kind = kind_ref[:, sl]
        weight = jnp.where(kind == 1, 5.0, jnp.where(kind == 2, 10.0, 1.0))
        centred = true_ref[:, sl] - k_ref[0:3, :]
        for s in range(copies):
            r = slice(3 * s, 3 * s + 3)
            target = m_ref[0, r, :] * centred[0:1] + m_ref[1, r, :] * centred[1:2] + m_ref[2, r, :] * centred[2:3] + m_ref[3, r, :]
            deviation = pred_ref[s, :, sl] - target
            grad_ref[s, :, sl] = m_ref[4, r, :] * weight * deviation - m_ref[5, r, :] * pull_ref[s, :, sl]


VMEM = pl.BlockSpec(memory_space=pltpu.VMEM)
SMEM = pl.BlockSpec(memory_space=pltpu.SMEM)


def swap(x, axis, step):
    return lax.ppermute(x, axis, [(i, i ^ step) for i in range(lax.axis_size(axis))])


def shards(coords_pred, coords_true, atom_kind, partners, noise_level):
    copies, _, local = coords_pred.shape
    tiles = partners.shape[0]
    rows = 3 * copies
    window = tiles + 2 * BAND
    size = lax.axis_size("res")
    kind = atom_kind[None]
    base = (lax.axis_index("res") * tiles)[None].astype(jnp.int32)

    def edge(start):
        take = lambda a: lax.slice_in_dim(a, start, start + BAND * LANES, axis=a.ndim - 1)
        cut = jnp.where(take(atom_kind) == 1, 15.0, 7.5).astype(F32)
        return jnp.concatenate([take(coords_pred).reshape(rows, -1) * 0.5, take(coords_true) * 0.5, cut[None]], axis=0)

    forward = [(i, i + 1) for i in range(size - 1)]
    low = lax.ppermute(edge(local - BAND * LANES), "res", forward)
    high = lax.ppermute(edge(0), "res", [(b, a) for a, b in forward])

    pull, stats = pl.pallas_call(
        functools.partial(pair_kernel, copies=copies, tiles=tiles),
        in_specs=[SMEM, SMEM] + [VMEM] * 5,
        out_specs=[VMEM, VMEM],
        out_shape=[jax.ShapeDtypeStruct((copies, 3, local), F32), jax.ShapeDtypeStruct((2, 16, LANES), F32)],
        scratch_shapes=[
            pltpu.VMEM((window, 16, LANES), F32),
            pltpu.VMEM((window, 16, 16, LANES), F32),
            pltpu.VMEM((16, 8, LANES), F32),
            pltpu.VMEM((16, 8, LANES), F32),
            pltpu.VMEM((16, 8, LANES), F32),
            pltpu.VMEM((window, rows, 8, LANES), F32),
            pltpu.VMEM((rows, 8, LANES), F32),
            pltpu.VMEM((copies, 8, LANES), F32),
            pltpu.VMEM((8, LANES), F32),
        ],
        compiler_params=pltpu.CompilerParams(vmem_limit_bytes=40 * 2**20),
        name="pairs",
    )(base, partners, coords_pred, coords_true, kind, low, high)

    step = 1
    while step < size:
        other = swap(stats, "res", step)
        total, error = two_sum(stats[0], other[0])
        stats = jnp.stack([total, (stats[1] + other[1]) + error])
        step *= 2

    loss, grad = pl.pallas_call(
        functools.partial(finish_kernel, copies=copies, tiles=tiles, atoms=local * size),
        in_specs=[VMEM, SMEM] + [VMEM] * 4,
        out_specs=[VMEM, VMEM],
        out_shape=[jax.ShapeDtypeStruct((copies, LANES), F32), jax.ShapeDtypeStruct((copies, 3, local), F32)],
        scratch_shapes=[pltpu.VMEM((6, rows, LANES), F32), pltpu.VMEM((8, LANES), F32)],
        compiler_params=pltpu.CompilerParams(vmem_limit_bytes=40 * 2**20),
        name="finish",
    )(stats, noise_level, coords_pred, coords_true, kind, pull)
    copy_loss = loss[:, 0]
    total = jnp.sum(copy_loss)[None]
    step = 1
    while step < lax.axis_size("samp"):
        total = total + swap(total, "samp", step)
        step *= 2
    mean_loss = total[0] / (copies * lax.axis_size("samp"))
    return copy_loss, mean_loss, grad


def solution(mesh):
    in_specs = (P("samp", None, "res"), P(None, "res"), P("res"), P("res", None), P("samp"))
    out_specs = (P("samp"), P(), P("samp", None, "res"))
    return jax.shard_map(shards, mesh=mesh, in_specs=in_specs, out_specs=out_specs, check_vma=False)
```

```python
import functools

import jax
import jax.numpy as jnp
from jax import lax
from jax.experimental import pallas as pl
from jax.experimental.pallas import tpu as pltpu
from jax.sharding import PartitionSpec as P

LANES = 128
BAND = 2
SWEEPS = 20
SIGMA = 16.0
HALF_THRESHOLDS = (0.25, 0.5, 1.0, 2.0)
EPS = 0.25e-6
F32 = jnp.float32
BF16 = jnp.bfloat16


def roll(x, shift, axis=1):
    return pltpu.roll(x, shift, axis)


def two_sum(a, b):
    s = a + b
    t = s - a
    return s, (a - (s - t)) + (b - t)


def two_prod(a, b):
    def halves(x):
        t = x * 4097.0
        h = t - (t - x)
        return h, x - h

    p = a * b
    ah, al = halves(a)
    bh, bl = halves(b)
    return p, ((ah * bh - p) + ah * bl + al * bh) + al * bl


def pair_add(x, y):
    s, e = two_sum(x[0], y[0])
    return two_sum(s, e + (x[1] + y[1]))


def pair_neg(x):
    return -x[0], -x[1]


def pair_mul(x, y):
    p, e = two_prod(x[0], y[0])
    return two_sum(p, e + (x[0] * y[1] + x[1] * y[0]))


def pair_div(x, w):
    q = x[0] / w
    p, e = two_prod(q, w)
    return two_sum(q, (((x[0] - p) - e) + x[1]) / w)


def dot(a, b):
    return jnp.dot(a, b, preferred_element_type=F32)


def dot_nt(a, b):
    return lax.dot_general(a, b, (((1,), (1,)), ((), ())), preferred_element_type=F32)


def split3(x):
    a = x.astype(BF16).astype(F32)
    rest = x - a
    b = rest.astype(BF16).astype(F32)
    return a, b, (rest - b).astype(BF16).astype(F32)


def stack(a, b, axis):
    return jnp.concatenate([a, b], axis=axis)


def listed(part_ref, owner, other):
    hit = jnp.bool_(False)
    for k in range(1, part_ref.shape[1]):
        hit = hit | (part_ref[owner, k] == other)
    return hit


class Engine:
    names = ("v", "cut", "centre", "left", "point", "right", "true", "weight", "d", "f", "acc", "score", "count", "tri", "items")

    def __init__(self, copies, refs):
        self.copies = copies
        self.twos = copies // 2
        for name, ref in zip(self.names, refs):
            setattr(self, name, ref)

    @staticmethod
    def scratch(tiles, copies, items):
        n, twos = tiles + 1, copies // 2
        return [
            pltpu.VMEM((n, copies + 1, 8, LANES), F32),
            pltpu.VMEM((n, 1, LANES), F32),
            pltpu.VMEM((n, copies + 1, 8, LANES), F32),
            pltpu.VMEM((n, twos + 1, LANES, LANES), BF16),
            pltpu.VMEM((n, twos, 64, 2 * LANES), BF16),
            [pltpu.VMEM((2, twos + 1, LANES, 2 * LANES), BF16)] * 2,
            [pltpu.VMEM((LANES, LANES), F32)] * 2,
            [pltpu.VMEM((LANES, LANES), F32)] * 2,
            [pltpu.VMEM((twos + 1, LANES, 2 * LANES), F32)] * 2,
            [pltpu.VMEM((twos, 2 * LANES, 2 * LANES), BF16)] * 2,
            pltpu.VMEM((n, copies, 8, LANES), F32),
            pltpu.VMEM((copies, 8, LANES), F32),
            pltpu.VMEM((8, LANES), F32),
            pltpu.VMEM((2, LANES, LANES), BF16),
            pltpu.SMEM((4, items + 2), jnp.int32),
        ]

    def begin(self, tiles):
        for ref in [self.v, self.acc, self.score, self.count, *self.right, *self.f]:
            ref[...] = jnp.zeros_like(ref)
        self.cut[tiles] = jnp.zeros((1, LANES), F32)
        row = lax.broadcasted_iota(jnp.int32, (LANES, LANES), 0)
        lane = lax.broadcasted_iota(jnp.int32, (LANES, LANES), 1)
        self.tri[0] = jnp.where(lane > row, 1.0, 0.0).astype(BF16)
        self.tri[1] = jnp.where(lane < row, 1.0, 0.0).astype(BF16)
        pick = jnp.where(row == 7, 1.0, 0.0).astype(BF16)
        for ref in self.right:
            for k in range(2):
                ref[k, self.twos, :, LANES:] = pick

    @staticmethod
    def unit(k):
        return jnp.where(lax.broadcasted_iota(jnp.int32, (8, LANES), 0) == k, 1.0, 0.0)

    def prep(self, t):
        groups = []
        for s in range(self.copies + 1):
            v = self.v[t, s]
            centre = jnp.broadcast_to(jnp.sum(v, axis=1, keepdims=True) * (1.0 / LANES), (8, LANES))
            self.centre[t, s] = centre
            y = v - centre
            norm = jnp.sum(y * y, axis=0, keepdims=True)
            x = y + (self.unit(4) + EPS * self.unit(5)) + norm * self.unit(3)
            if s == self.copies:
                x = x + self.unit(7) * self.cut[t]
            a, b, c = split3(x)
            groups.append(jnp.concatenate([a, a, b, a, b, c, b, c], axis=0))
            if s < self.copies:
                a, b, c = split3(v + self.unit(3))
                p = jnp.concatenate([a, b, c, jnp.zeros_like(a)], axis=0).astype(BF16)
                q = 32 * (s % 2)
                self.point[t, s // 2, q:q + 32, :LANES] = p
                self.point[t, s // 2, q:q + 32, LANES:] = p
        groups.append(jnp.zeros((64, LANES), F32))
        for h in range(self.twos + 1):
            self.left[t, h] = stack(groups[2 * h], groups[2 * h + 1], 0).T.astype(BF16)

    def build(self, slot, k, g, j):
        for s in range(self.copies + 1):
            y = self.v[j, s] - self.centre[g, s]
            norm = jnp.sum(y * y, axis=0, keepdims=True)
            a, b, c = split3((self.unit(3) + self.unit(5)) - 2.0 * y + norm * self.unit(4))
            q, m = 64 * (s % 2), LANES * (s % 2)
            self.right[slot][k, s // 2, q:q + 64, m:m + LANES] = jnp.concatenate([a, b, a, c, b, a, c, b], axis=0).astype(BF16)

    def squares(self, slot, k, g, h):
        return dot(self.left[g, h], self.right[slot][k, h])

    def weigh(self, slot, cut_j, live, share):
        total = jnp.zeros((8, LANES), F32)
        for b in range(16):
            k = slice(8 * b, 8 * b + 8)
            d2 = jnp.maximum(self.d[slot][self.twos, k, :LANES], EPS)
            dist = d2 * lax.rsqrt(d2)
            w = jnp.where(dist < cut_j(k), 0.0625, 0.0) + jnp.where(dist < self.d[slot][self.twos, k, LANES:], 0.0625, 0.0)
            if live is not None:
                w = w * live(k)
            self.true[slot][k, :] = dist
            self.weight[slot][k, :] = w
            total = total + w
        self.count[...] += total * share

    def factor(self, slot, share):
        for s in range(self.copies):
            h, m = s // 2, LANES * (s % 2)
            score = jnp.zeros((8, LANES), F32)
            for q in range(8):
                k = slice(16 * q, 16 * q + 16)
                d2 = jnp.maximum(self.d[slot][h, k, m:m + LANES], EPS)
                r = lax.rsqrt(d2)
                diff = d2 * r - self.true[slot][k, :]
                spread = jnp.abs(diff)
                u = [jnp.tanh(t - spread) for t in HALF_THRESHOLDS]
                w = self.weight[slot][k, :]
                z = w * ((u[0] + u[1]) + (u[2] + u[3]))
                score = score + z[:8] + z[8:]
                slope = ((u[0] * u[0] + u[1] * u[1]) + (u[2] * u[2] + u[3] * u[3])) - 4.0
                f = slope * r * jnp.maximum(jnp.minimum(diff * 1e30, w), -w)
                high = f.astype(BF16)
                self.f[slot][h, k, m:m + LANES] = high
                self.f[slot][h, LANES + 16 * q:LANES + 16 * q + 16, m:m + LANES] = (f - high.astype(F32)).astype(BF16)
            self.score[s] += score * share

    @staticmethod
    def fold(z):
        return [z[k:k + 8, m:m + LANES] + z[k + 8:k + 16, m:m + LANES] + z[k + 16:k + 24, m:m + LANES] for k, m in ((0, 0), (32, LANES))]

    def along_j(self, p, f):
        return self.fold(dot(p, f))

    def along_i(self, p, f):
        one = stack(f[:LANES, :LANES], f[LANES:, :LANES], 1)
        two = stack(f[:LANES, LANES:], f[LANES:, LANES:], 1)
        return self.fold(dot_nt(p, stack(one, two, 0)))

    def cross_build(self, item, slot):
        self.build(slot, 0, item[0], item[1])

    def cross_measure(self, item, slot):
        for h in [self.twos, *range(self.twos)]:
            self.d[slot][h] = self.squares(slot, 0, item[0], h)

    def cross_factor(self, item, slot):
        share = item[2].astype(F32) * 0.5
        cut = self.cut[item[1]]
        self.weigh(slot, lambda k: cut, None, share)
        self.factor(slot, share)

    def cross_collect(self, item, slot):
        g, j = item[0], item[1]
        for h in range(self.twos):
            f = self.f[slot][h]
            x = self.along_j(self.point[g, h], f)
            y = self.along_i(self.point[j, h], f)
            for k in range(2):
                self.acc[j, 2 * h + k] += x[k]
                self.acc[g, 2 * h + k] += y[k]

    def self_build(self, item, slot):
        for k in range(2):
            self.build(slot, k, item[k], item[k])

    def self_measure(self, item, slot):
        row = lax.broadcasted_iota(jnp.int32, (LANES, 2 * LANES), 0)
        lane = lax.broadcasted_iota(jnp.int32, (LANES, 2 * LANES), 1) % LANES
        for h in [self.twos, *range(self.twos)]:
            self.d[slot][h] = jnp.where(lane > row, self.squares(slot, 0, item[0], h), self.squares(slot, 1, item[1], h))

    def self_factor(self, item, slot):
        row = lax.broadcasted_iota(jnp.int32, (8, LANES), 0)
        lane = lax.broadcasted_iota(jnp.int32, (8, LANES), 1)
        cut = [self.cut[item[0]], self.cut[item[1]]]
        self.weigh(slot, lambda k: jnp.where(lane > row + k.start, cut[0], cut[1]), lambda k: jnp.where(lane == row + k.start, 0.0, 1.0), 1.0)
        self.factor(slot, 1.0)

    def self_collect(self, item, slot):
        for h in range(self.twos):
            f = self.f[slot][h]
            for k in range(2):
                mask = stack(self.tri[k], self.tri[k], 0)
                part = f * stack(mask, mask, 1)
                x = self.along_j(self.point[item[k], h], part)
                y = self.along_i(self.point[item[k], h], part)
                for q in range(2):
                    self.acc[item[k], 2 * h + q] += x[q] + y[q]

    def half(self, kind, items, slot):
        last, now, soon, later = items
        getattr(self, kind + "_collect")(last, 1 - slot)
        getattr(self, kind + "_measure")(soon, 1 - slot)
        getattr(self, kind + "_build")(later, slot)
        getattr(self, kind + "_factor")(now, slot)

    def begin_list(self, kind, item, n):
        getattr(self, kind + "_build")(item(0), 0)
        getattr(self, kind + "_measure")(item(0), 0)
        getattr(self, kind + "_build")(item(jnp.minimum(1, n - 1)), 1)

    def pairs_of_items(self, kind, item, n, dummy):
        def at(p):
            return tuple(jnp.where(p < 0, dummy, z) for z in item(jnp.clip(p, 0, n - 1)))

        @pl.loop(0, n // 2)
        def _(i):
            p = 2 * i
            for slot in range(2):
                self.half(kind, [at(p + slot - 1), at(p + slot), at(p + slot + 1), at(p + slot + 2)], slot)

    def pull(self, t, s):
        a = self.acc[t, s]
        return (self.v[t, s] * a[3:4] - a)[0:3]

    def scores(self, weight_total):
        rows = [jnp.sum(self.score[s], axis=0, keepdims=True) for s in range(self.copies)]
        rows += [jnp.sum(self.count[...], axis=0, keepdims=True), weight_total]
        total = jnp.zeros((8, LANES), F32)
        for k, x in enumerate(rows):
            total = total + x * self.unit(k)
        return jnp.broadcast_to(jnp.sum(total, axis=1, keepdims=True), (8, LANES))


def finish_list(e, item, n, dummy):
    @pl.when(n % 2 == 1)
    def _():
        before = tuple(jnp.where(n > 1, z, dummy) for z in item(jnp.maximum(n - 2, 0)))
        e.cross_collect(before, 1)
        e.cross_factor(item(n - 1), 0)
        e.cross_collect(item(n - 1), 0)

    @pl.when(n % 2 == 0)
    def _():
        e.cross_collect(item(n - 1), 1)


def interior_kernel(base_ref, part_ref, pred_ref, true_ref, kind_ref, pull_ref, stat_ref, x_ref, mom_ref, *scratch, copies, tiles):
    e = Engine(copies, scratch)
    base = base_ref[0]
    rows = 3 * copies
    e.begin(tiles)
    x_ref[...] = jnp.zeros_like(x_ref)
    mom_ref[...] = jnp.zeros_like(mom_ref)

    def scan(t, n):
        for o in range(1, BAND + 1):
            hit = listed(part_ref, t, base + t - o) & (t >= o)

            @pl.when(hit)
            def _(n=n, o=o):
                e.items[0, n] = t - o
                e.items[1, n] = t
                e.items[2, n] = 2

            n = n + jnp.where(hit, 1, 0)
        return n

    n = lax.fori_loop(0, tiles, scan, jnp.int32(0))
    unroll = next(u for u in (6, 4, 3, 2, 1) if tiles % u == 0)

    @pl.loop(0, tiles // unroll)
    def _(m):
        for q in range(unroll):
            t = m * unroll + q
            sl = pl.ds(pl.multiple_of(t * LANES, LANES), LANES)
            kind = kind_ref[:, sl]
            weight = jnp.where(kind == 1, 5.0, jnp.where(kind == 2, 10.0, 1.0))
            for s in range(copies):
                v = pred_ref[s, :, sl] * 0.5
                e.v[t, s, 0:3, :] = v
                x_ref[q, 3 * s:3 * s + 3, :] = v
            v = true_ref[:, sl] * 0.5
            e.v[t, copies, 0:3, :] = v
            x_ref[q, rows:rows + 3, :] = v
            e.cut[t] = jnp.where(kind == 1, 15.0, 7.5)
            x = x_ref[q]
            wx = x * weight
            terms = [wx * x[rows + c:rows + c + 1] for c in range(3)] + [wx, wx * x]
            for i, term in enumerate(terms):
                total, error = two_sum(mom_ref[0, i], term)
                mom_ref[0, i] = total
                mom_ref[1, i] += error
            mom_ref[0, 5, 0:1, :] += weight
            e.prep(t)

    e.prep(tiles)

    blank = jnp.zeros((LANES - 80, LANES), F32)
    high, low = (jnp.concatenate([mom_ref[part, i] for i in range(5)] + [blank], axis=0).T for part in range(2))
    sums = [(high[8 * k:8 * k + 8], low[8 * k:8 * k + 8]) for k in range(16)]
    while len(sums) > 1:
        sums = [pair_add(a, b) for a, b in zip(sums[::2], sums[1::2])]
    sums = sums[0]
    for k in (4, 2, 1):
        sums = pair_add(sums, (roll(sums[0], k, 0), roll(sums[1], k, 0)))
    stat_ref[0] = sums[0] * e.unit(0) + sums[1] * e.unit(1)

    def twin(i):
        return 2 * i, 2 * i + 1

    half = tiles // 2
    e.begin_list("self", twin, half)
    e.pairs_of_items("self", twin, half, tiles)

    def item(i):
        return e.items[0, i], e.items[1, i], e.items[2, i]

    @pl.when(n == 0)
    def _():
        for k, z in enumerate((tiles, tiles, 0)):
            e.items[k, 0] = z

    n = jnp.maximum(n, 1)
    e.begin_list("cross", item, n)
    e.self_collect(twin(half - 1), 1)
    e.pairs_of_items("cross", item, n, tiles)
    finish_list(e, item, n, tiles)

    @pl.loop(0, tiles)
    def _(t):
        sl = pl.ds(pl.multiple_of(t * LANES, LANES), LANES)
        for s in range(copies):
            pull_ref[s, :, sl] = e.pull(t, s)

    stat_ref[1] = e.scores(mom_ref[0, 5, 0:1, :])


def edge_kernel(base_ref, part_ref, pred_ref, true_ref, kind_ref, low_ref, high_ref, stat_ref, pull_ref, out_ref, *scratch, copies, tiles):
    e = Engine(copies, scratch)
    base = base_ref[0]
    span = BAND * LANES
    local = tiles * LANES
    window = 4 * BAND
    e.begin(window)
    for q in range(BAND):
        sl = slice(q * LANES, q * LANES + LANES)
        for ref, t in ((low_ref, q), (high_ref, 3 * BAND + q)):
            for s in range(copies + 1):
                e.v[t, s, 0:3, :] = ref[3 * s:3 * s + 3, sl]
            e.cut[t] = ref[3 * copies + 3:3 * copies + 4, sl]
        for start, t in ((0, BAND + q), (local - span, 2 * BAND + q)):
            sl = slice(start + q * LANES, start + q * LANES + LANES)
            for s in range(copies):
                e.v[t, s, 0:3, :] = pred_ref[s, :, sl] * 0.5
            e.v[t, copies, 0:3, :] = true_ref[:, sl] * 0.5
            e.cut[t] = jnp.where(kind_ref[:, sl] == 1, 15.0, 7.5)
    n = jnp.int32(0)
    for o in range(1, BAND + 1):
        for k in range(o):
            for owner, other, g, j in ((k, k - o, BAND + k - o, BAND + k), (tiles - 1 - k, tiles - 1 - k + o, 3 * BAND - 1 - k, 3 * BAND - 1 - k + o)):
                hit = listed(part_ref, owner, base + other)

                @pl.when(hit)
                def _(n=n, g=g, j=j):
                    e.items[0, n] = g
                    e.items[1, n] = j
                    e.items[2, n] = 1

                n = n + jnp.where(hit, 1, 0)

    def item(i):
        return e.items[0, i], e.items[1, i], e.items[2, i]

    @pl.when(n > 0)
    def _():
        for t in range(window + 1):
            e.prep(t)
        e.begin_list("cross", item, n)
        e.pairs_of_items("cross", item, n, window)
        finish_list(e, item, n, window)

    for t in range(2 * BAND):
        for s in range(copies):
            pull_ref[s, :, t * LANES:(t + 1) * LANES] = e.pull(BAND + t, s)
    out_ref[0] = stat_ref[0]
    out_ref[1] = stat_ref[1] + e.scores(jnp.zeros((1, LANES), F32))


def finish_kernel(stat_ref, noise_ref, pred_ref, true_ref, kind_ref, pull_ref, edge_ref, loss_ref, grad_ref, m_ref, k_ref, s_ref, *, copies, tiles, atoms):
    rows = 3 * copies
    column = stack(stat_ref[0], jnp.zeros((LANES - 8, LANES), F32), 0).T
    for part in range(2):
        s_ref[part] = jnp.broadcast_to(column[:, part:part + 1], (LANES, LANES))

    def per_copy(c, q, scale):
        return tuple(s_ref[part, pl.ds(16 * q + c, copies, stride=3), :] * scale for part in range(2))

    def shared(r, q, scale):
        return tuple(s_ref[part, 16 * q + r:16 * q + r + 1, :] * scale for part in range(2))

    def wide(x):
        return tuple(jnp.broadcast_to(v, (copies, LANES)) for v in x)

    weight_sum = jnp.broadcast_to(stat_ref[1, copies + 1:copies + 2, :], (copies, LANES))
    count = jnp.broadcast_to(stat_ref[1, copies:copies + 1, :], (copies, LANES)) * 16.0
    score = stat_ref[1, 0:copies, :] * 2.0 + 0.5 * count
    pred_sum = [wide(per_copy(c, 3, 2.0)) for c in range(3)]
    true_sum = [wide(shared(rows + c, 3, 2.0)) for c in range(3)]
    pred_mean = [pair_div(x, weight_sum) for x in pred_sum]
    true_mean = [pair_div(x, weight_sum) for x in true_sum]
    cov = [[pair_add(wide(per_copy(c, d, 4.0)), pair_neg(pair_mul(pred_sum[c], true_mean[d]))) for d in range(3)] for c in range(3)]
    ct = {}
    for d in range(3):
        for e in range(d + 1):
            ct[d, e] = pair_add(wide(shared(rows + d, e, 4.0)), pair_neg(pair_mul(true_sum[d], true_mean[e])))
    var = None
    for c in range(3):
        term = pair_add(wide(per_copy(c, 4, 4.0)), pair_neg(pair_mul(pred_sum[c], pred_mean[c])))
        var = term if var is None else pair_add(var, term)

    x = [[cov[c][d][0] for d in range(3)] for c in range(3)]
    frobenius = jnp.sqrt(sum(x[c][d] * x[c][d] for c in range(3) for d in range(3)))
    x = [[x[c][d] / frobenius for d in range(3)] for c in range(3)]

    def sweep(_, flat):
        x = [flat[0:3], flat[3:6], flat[6:9]]
        gram = {}
        for a in range(3):
            for b in range(a + 1):
                gram[a, b] = gram[b, a] = x[a][0] * x[b][0] + x[a][1] * x[b][1] + x[a][2] * x[b][2]
        return tuple(1.5 * x[a][d] - 0.5 * (gram[a, 0] * x[0][d] + gram[a, 1] * x[1][d] + gram[a, 2] * x[2][d])
                     for a in range(3) for d in range(3))

    flat = lax.fori_loop(0, SWEEPS, sweep, tuple(v for line in x for v in line))
    x = [flat[0:3], flat[3:6], flat[6:9]]

    square = var
    nothing = jnp.zeros((copies, LANES), F32)
    for c in range(3):
        for d in range(3):
            square = pair_add(square, pair_mul((-2.0 * x[c][d], nothing), cov[c][d]))
    for d in range(3):
        for e in range(d + 1):
            gram = None
            for c in range(3):
                term = two_prod(x[c][d], x[c][e])
                gram = term if gram is None else pair_add(gram, term)
            if d != e:
                gram = (2.0 * gram[0], 2.0 * gram[1])
            square = pair_add(square, pair_mul(gram, ct[d, e]))

    row = lax.broadcasted_iota(jnp.int32, (copies, LANES), 0)
    noise = nothing
    for s in range(copies):
        noise = jnp.where(row == s, noise_ref[s], noise)
    loss_weight = (noise * noise + SIGMA * SIGMA) / (noise * SIGMA * (noise * SIGMA))
    mean_square = (square[0] + square[1]) / (3.0 * weight_sum)
    loss_ref[...] = loss_weight * mean_square + 1.0 - score / count

    grad_scale = 16.0 * atoms
    for c in range(3):
        for d in range(3):
            m_ref[d, pl.ds(c, copies, stride=3), :] = x[c][d]
        m_ref[3, pl.ds(c, copies, stride=3), :] = pred_mean[c][0]
        m_ref[4, pl.ds(c, copies, stride=3), :] = grad_scale * 2.0 * loss_weight / (3.0 * weight_sum)
        m_ref[5, pl.ds(c, copies, stride=3), :] = grad_scale / count
        k_ref[c:c + 1, :] = true_mean[c][0][0:1]

    @pl.loop(0, tiles)
    def _(t):
        sl = pl.ds(pl.multiple_of(t * LANES, LANES), LANES)
        kind = kind_ref[:, sl]
        weight = jnp.where(kind == 1, 5.0, jnp.where(kind == 2, 10.0, 1.0))
        centred = true_ref[:, sl] - k_ref[0:3, :]
        for s in range(copies):
            r = slice(3 * s, 3 * s + 3)
            target = m_ref[0, r, :] * centred[0:1] + m_ref[1, r, :] * centred[1:2] + m_ref[2, r, :] * centred[2:3] + m_ref[3, r, :]
            deviation = pred_ref[s, :, sl] - target
            grad_ref[s, :, sl] = m_ref[4, r, :] * weight * deviation - m_ref[5, r, :] * pull_ref[s, :, sl]

    for t in range(2 * BAND):
        start = t * LANES if t < BAND else (tiles - 2 * BAND + t) * LANES
        for s in range(copies):
            grad_ref[s, :, start:start + LANES] -= m_ref[5, 3 * s:3 * s + 3, :] * edge_ref[s, :, t * LANES:(t + 1) * LANES]


VMEM = pl.BlockSpec(memory_space=pltpu.VMEM)
SMEM = pl.BlockSpec(memory_space=pltpu.SMEM)
PARAMS = pltpu.CompilerParams(vmem_limit_bytes=40 * 2**20)


def swap(x, axis, step):
    return lax.ppermute(x, axis, [(i, i ^ step) for i in range(lax.axis_size(axis))])


def shards(coords_pred, coords_true, atom_kind, partners, noise_level):
    copies, _, local = coords_pred.shape
    tiles = partners.shape[0]
    rows = 3 * copies
    size = lax.axis_size("res")
    kind = atom_kind[None]
    base = (lax.axis_index("res") * tiles)[None].astype(jnp.int32)
    stats_shape = jax.ShapeDtypeStruct((2, 8, LANES), F32)

    def edge(start):
        take = lambda a: lax.slice_in_dim(a, start, start + BAND * LANES, axis=a.ndim - 1)
        cut = jnp.where(take(atom_kind) == 1, 15.0, 7.5).astype(F32)
        return jnp.concatenate([take(coords_pred).reshape(rows, -1) * 0.5, take(coords_true) * 0.5, cut[None]], axis=0)

    forward = [(i, i + 1) for i in range(size - 1)]
    low = lax.ppermute(edge(local - BAND * LANES), "res", forward)
    high = lax.ppermute(edge(0), "res", [(b, a) for a, b in forward])

    pull, stats = pl.pallas_call(
        functools.partial(interior_kernel, copies=copies, tiles=tiles),
        in_specs=[SMEM, SMEM] + [VMEM] * 3,
        out_specs=[VMEM, VMEM],
        out_shape=[jax.ShapeDtypeStruct((copies, 3, local), F32), stats_shape],
        scratch_shapes=[pltpu.VMEM((6, 16, LANES), F32), pltpu.VMEM((2, 6, 16, LANES), F32)] + Engine.scratch(tiles, copies, BAND * tiles),
        compiler_params=PARAMS,
        cost_estimate=pl.CostEstimate(flops=10**8, bytes_accessed=10**6, transcendentals=10**7),
        name="interior",
    )(base, partners, coords_pred, coords_true, kind)
    edge_pull, stats = pl.pallas_call(
        functools.partial(edge_kernel, copies=copies, tiles=tiles),
        in_specs=[SMEM, SMEM] + [VMEM] * 6,
        out_specs=[VMEM, VMEM],
        out_shape=[jax.ShapeDtypeStruct((copies, 3, 2 * BAND * LANES), F32), stats_shape],
        scratch_shapes=Engine.scratch(4 * BAND, copies, BAND * (BAND + 1)),
        compiler_params=PARAMS,
        name="edges",
    )(base, partners, coords_pred, coords_true, kind, low, high, stats)

    step = 1
    while step < size:
        other = swap(stats, "res", step)
        total, error = two_sum(stats[0, 0], other[0, 0])
        moments = jnp.stack([total, (stats[0, 1] + other[0, 1]) + error] + [jnp.zeros((LANES,), F32)] * 6)
        stats = jnp.stack([moments, stats[1] + other[1]])
        step *= 2

    loss, grad = pl.pallas_call(
        functools.partial(finish_kernel, copies=copies, tiles=tiles, atoms=local * size),
        in_specs=[VMEM, SMEM] + [VMEM] * 5,
        out_specs=[VMEM, VMEM],
        out_shape=[jax.ShapeDtypeStruct((copies, LANES), F32), jax.ShapeDtypeStruct((copies, 3, local), F32)],
        scratch_shapes=[pltpu.VMEM((6, rows, LANES), F32), pltpu.VMEM((8, LANES), F32), pltpu.VMEM((2, LANES, LANES), F32)],
        compiler_params=PARAMS,
        name="finish",
    )(stats, noise_level, coords_pred, coords_true, kind, pull, edge_pull)
    copy_loss = loss[:, 0]
    total = jnp.sum(copy_loss)[None]
    step = 1
    while step < lax.axis_size("samp"):
        total = total + swap(total, "samp", step)
        step *= 2
    mean_loss = total[0] / (copies * lax.axis_size("samp"))
    return copy_loss, mean_loss, grad


def solution(mesh):
    in_specs = (P("samp", None, "res"), P(None, "res"), P("res"), P("res", None), P("samp"))
    out_specs = (P("samp"), P(), P("samp", None, "res"))
    return jax.shard_map(shards, mesh=mesh, in_specs=in_specs, out_specs=out_specs, check_vma=False)
```

```python
import functools

import jax
import jax.numpy as jnp
from jax import lax
from jax.experimental import pallas as pl
from jax.experimental.pallas import tpu as pltpu
from jax.sharding import PartitionSpec as P

LANES = 128
BAND = 2
SWEEPS = 20
SIGMA = 16.0
HALF_THRESHOLDS = (0.25, 0.5, 1.0, 2.0)
EPS = 0.25e-6
F32 = jnp.float32
BF16 = jnp.bfloat16


def roll(x, shift, axis=1):
    return pltpu.roll(x, shift, axis)


def two_sum(a, b):
    s = a + b
    t = s - a
    return s, (a - (s - t)) + (b - t)


def two_prod(a, b):
    def halves(x):
        t = x * 4097.0
        h = t - (t - x)
        return h, x - h

    p = a * b
    ah, al = halves(a)
    bh, bl = halves(b)
    return p, ((ah * bh - p) + ah * bl + al * bh) + al * bl


def pair_add(x, y):
    s, e = two_sum(x[0], y[0])
    return two_sum(s, e + (x[1] + y[1]))


def pair_neg(x):
    return -x[0], -x[1]


def pair_mul(x, y):
    p, e = two_prod(x[0], y[0])
    return two_sum(p, e + (x[0] * y[1] + x[1] * y[0]))


def pair_div(x, w):
    q = x[0] / w
    p, e = two_prod(q, w)
    return two_sum(q, (((x[0] - p) - e) + x[1]) / w)


def dot(a, b):
    return jnp.dot(a, b, preferred_element_type=F32)


def dot_nt(a, b):
    return lax.dot_general(a, b, (((1,), (1,)), ((), ())), preferred_element_type=F32)


def split3(x):
    a = x.astype(BF16).astype(F32)
    rest = x - a
    b = rest.astype(BF16).astype(F32)
    return a, b, (rest - b).astype(BF16).astype(F32)


def stack(a, b, axis):
    return jnp.concatenate([a, b], axis=axis)


def listed(part_ref, owner, other):
    hit = jnp.bool_(False)
    for k in range(1, part_ref.shape[1]):
        hit = hit | (part_ref[owner, k] == other)
    return hit


class Engine:
    names = ("v", "cut", "centre", "left", "point", "right", "true", "weight", "minus", "d", "f", "acc", "score", "count", "tri", "items")

    def __init__(self, copies, refs):
        self.copies = copies
        self.twos = copies // 2
        for name, ref in zip(self.names, refs):
            setattr(self, name, ref)

    @staticmethod
    def scratch(tiles, copies, items):
        n, twos = tiles + 1, copies // 2
        return [
            pltpu.VMEM((n, copies + 1, 8, LANES), F32),
            pltpu.VMEM((n, 1, LANES), F32),
            pltpu.VMEM((n, copies + 1, 8, LANES), F32),
            pltpu.VMEM((n, twos + 1, LANES, LANES), BF16),
            pltpu.VMEM((n, twos, 64, 2 * LANES), BF16),
            [pltpu.VMEM((1, twos + 1, LANES, 2 * LANES), BF16)] * 2,
            [pltpu.VMEM((LANES, LANES), F32)] * 2,
            [pltpu.VMEM((LANES, LANES), F32)] * 2,
            [pltpu.VMEM((LANES, LANES), F32)] * 2,
            [pltpu.VMEM((1, twos + 1, LANES, 2 * LANES), F32)] * 2,
            [pltpu.VMEM((1, twos, 2 * LANES, 2 * LANES), BF16)] * 2,
            pltpu.VMEM((n, copies, 8, LANES), F32),
            pltpu.VMEM((copies, 8, LANES), F32),
            pltpu.VMEM((8, LANES), F32),
            pltpu.VMEM((2, LANES, LANES), BF16),
            pltpu.SMEM((4, items + 2), jnp.int32),
        ]

    @staticmethod
    def self_scratch(copies):
        twos = copies // 2
        return [
            [pltpu.VMEM((2, twos + 1, LANES, 2 * LANES), BF16)] * 2,
            [pltpu.VMEM((2, twos + 1, LANES, 2 * LANES), F32)] * 2,
            [pltpu.VMEM((2, twos, 2 * LANES, 2 * LANES), BF16)] * 2,
        ]

    def for_self(self, refs):
        other = Engine(self.copies, [])
        other.__dict__.update(self.__dict__)
        other.right, other.d, other.f = refs
        return other

    def begin(self, tiles):
        for ref in [self.acc, self.score, self.count, *self.f, self.v.at[tiles], self.cut.at[tiles], self.centre.at[tiles], self.left.at[tiles], self.point.at[tiles]]:
            ref[...] = jnp.zeros_like(ref)
        row = lax.broadcasted_iota(jnp.int32, (LANES, LANES), 0)
        lane = lax.broadcasted_iota(jnp.int32, (LANES, LANES), 1)
        self.tri[0] = jnp.where(lane > row, 1.0, 0.0).astype(BF16)
        self.tri[1] = jnp.where(lane < row, 1.0, 0.0).astype(BF16)
        self.begin_right()

    def begin_right(self):
        pick = jnp.where(lax.broadcasted_iota(jnp.int32, (LANES, LANES), 0) == 7, 1.0, 0.0).astype(BF16)
        for ref in self.right:
            ref[...] = jnp.zeros_like(ref)
            for k in range(ref.shape[0]):
                ref[k, self.twos, :, LANES:] = pick

    def place(self, t, ref):
        blank = jnp.zeros((5, LANES), F32)
        for s in range(self.copies):
            self.v[t, s] = stack(ref[pl.ds(s, 3, stride=self.copies), :], blank, 0)
        self.v[t, self.copies] = stack(ref[3 * self.copies:3 * self.copies + 3, :], blank, 0)

    @staticmethod
    def unit(k):
        return jnp.where(lax.broadcasted_iota(jnp.int32, (8, LANES), 0) == k, 1.0, 0.0)

    def prep(self, t):
        groups = []
        for s in range(self.copies + 1):
            v = self.v[t, s]
            centre = jnp.broadcast_to(jnp.sum(v, axis=1, keepdims=True) * (1.0 / LANES), (8, LANES))
            self.centre[t, s] = centre
            y = v - centre
            norm = jnp.sum(y * y, axis=0, keepdims=True)
            x = y + (self.unit(4) + EPS * self.unit(5)) + norm * self.unit(3)
            if s == self.copies:
                x = x + self.unit(7) * self.cut[t]
            a, b, c = split3(x)
            groups.append(jnp.concatenate([a, a, b, a, b, c, b, c], axis=0))
            if s < self.copies:
                a, b, c = split3(v + self.unit(3))
                p = jnp.concatenate([a, b, c, jnp.zeros_like(a)], axis=0).astype(BF16)
                q = 32 * (s % 2)
                self.point[t, s // 2, q:q + 32, :LANES] = p
                self.point[t, s // 2, q:q + 32, LANES:] = p
        groups.append(jnp.zeros((64, LANES), F32))
        for h in range(self.twos + 1):
            self.left[t, h] = stack(groups[2 * h], groups[2 * h + 1], 0).T.astype(BF16)

    def build(self, slot, k, g, j):
        for s in range(self.copies + 1):
            y = self.v[j, s] - self.centre[g, s]
            norm = jnp.sum(y * y, axis=0, keepdims=True)
            a, b, c = split3((self.unit(3) + self.unit(5)) - 2.0 * y + norm * self.unit(4))
            q, m = 64 * (s % 2), LANES * (s % 2)
            self.right[slot][k, s // 2, q:q + 64, m:m + LANES] = jnp.concatenate([a, b, a, c, b, a, c, b], axis=0).astype(BF16)

    def squares(self, slot, k, g, h):
        return dot(self.left[g, h], self.right[slot][k, h])

    def get(self, slot, h, k, lanes, shared):
        one = self.d[slot][0, h, k, lanes]
        if not shared:
            return one
        return jnp.where(self.upper(k), one, self.d[slot][1, h, k, lanes])

    @staticmethod
    def upper(k):
        shape = (k.stop - k.start, LANES)
        return lax.broadcasted_iota(jnp.int32, shape, 1) > lax.broadcasted_iota(jnp.int32, shape, 0) + k.start

    def weigh(self, slot, cuts, share, shared):
        total = jnp.zeros((8, LANES), F32)
        for b in range(16):
            k = slice(8 * b, 8 * b + 8)
            d2 = jnp.maximum(self.get(slot, self.twos, k, slice(0, LANES), shared), EPS)
            dist = d2 * lax.rsqrt(d2)
            cut_j = jnp.where(self.upper(k), cuts[0], cuts[1]) if shared else cuts[0]
            cut_i = self.get(slot, self.twos, k, slice(LANES, 2 * LANES), shared)
            w = jnp.where(dist < cut_j, 0.0625, 0.0) + jnp.where(dist < cut_i, 0.0625, 0.0)
            if shared:
                row = lax.broadcasted_iota(jnp.int32, (8, LANES), 0) + 8 * b
                w = jnp.where(lax.broadcasted_iota(jnp.int32, (8, LANES), 1) == row, 0.0, w)
            self.true[slot][k, :] = dist
            self.weight[slot][k, :] = w
            self.minus[slot][k, :] = -w
            total = total + w
        self.count[...] += total * share

    def factor(self, slot, share, shared):
        for s in range(self.copies):
            h, m = s // 2, LANES * (s % 2)
            score = jnp.zeros((8, LANES), F32)
            for q in range(8):
                k = slice(16 * q, 16 * q + 16)
                d2 = jnp.maximum(self.get(slot, h, k, slice(m, m + LANES), shared), EPS)
                r = lax.rsqrt(d2)
                diff = d2 * r - self.true[slot][k, :]
                spread = jnp.abs(diff)
                u = [jnp.tanh(t - spread) for t in HALF_THRESHOLDS]
                w = self.weight[slot][k, :]
                z = w * ((u[0] + u[1]) + (u[2] + u[3]))
                score = score + z[:8] + z[8:]
                slope = ((u[0] * u[0] + u[1] * u[1]) + (u[2] * u[2] + u[3] * u[3])) - 4.0
                f = slope * r * jnp.maximum(jnp.minimum(diff * 1e30, w), self.minus[slot][k, :])
                high = f.astype(BF16)
                low = (f - high.astype(F32)).astype(BF16)
                for i in range(1 + shared):
                    part = (high * self.tri[i, k, :], low * self.tri[i, k, :]) if shared else (high, low)
                    for x, start in zip(part, (16 * q, LANES + 16 * q)):
                        self.f[slot][i, h, start:start + 16, m:m + LANES] = x
            self.score[s] += score * share

    @staticmethod
    def fold(z):
        return [z[k:k + 8, m:m + LANES] + z[k + 8:k + 16, m:m + LANES] + z[k + 16:k + 24, m:m + LANES] for k, m in ((0, 0), (32, LANES))]

    def along_j(self, p, f):
        return self.fold(dot(p, f))

    def along_i(self, p, f):
        one = stack(f[:LANES, :LANES], f[LANES:, :LANES], 1)
        two = stack(f[:LANES, LANES:], f[LANES:, LANES:], 1)
        return self.fold(dot_nt(p, stack(one, two, 0)))

    def cross_build(self, item, slot):
        self.build(slot, 0, item[0], item[1])

    def cross_measure(self, item, slot):
        for h in [self.twos, *range(self.twos)]:
            self.d[slot][0, h] = self.squares(slot, 0, item[0], h)

    def cross_factor(self, item, slot):
        share = item[2].astype(F32) * 0.5
        self.weigh(slot, [self.cut[item[1]]], share, False)
        self.factor(slot, share, False)

    def cross_collect(self, item, slot):
        g, j = item[0], item[1]
        for h in range(self.twos):
            f = self.f[slot][0, h]
            x = self.along_j(self.point[g, h], f)
            y = self.along_i(self.point[j, h], f)
            for k in range(2):
                self.acc[j, 2 * h + k] += x[k]
                self.acc[g, 2 * h + k] += y[k]

    def self_build(self, item, slot):
        for k in range(2):
            self.build(slot, k, item[k], item[k])

    def self_measure(self, item, slot):
        for h in [self.twos, *range(self.twos)]:
            for k in range(2):
                self.d[slot][k, h] = self.squares(slot, k, item[k], h)

    def self_factor(self, item, slot):
        self.weigh(slot, [self.cut[item[0]], self.cut[item[1]]], 1.0, True)
        self.factor(slot, 1.0, True)

    def self_collect(self, item, slot):
        for h in range(self.twos):
            for k in range(2):
                f = self.f[slot][k, h]
                x = self.along_j(self.point[item[k], h], f)
                y = self.along_i(self.point[item[k], h], f)
                for q in range(2):
                    self.acc[item[k], 2 * h + q] += x[q] + y[q]

    def half(self, kind, items, slot):
        last, now, soon, later = items
        getattr(self, kind + "_collect")(last, 1 - slot)
        getattr(self, kind + "_measure")(soon, 1 - slot)
        getattr(self, kind + "_build")(later, 1 - slot)
        getattr(self, kind + "_factor")(now, slot)

    def begin_list(self, kind, item, n):
        getattr(self, kind + "_build")(item(0), 0)
        getattr(self, kind + "_measure")(item(0), 0)
        for i in (1, 2):
            getattr(self, kind + "_build")(item(jnp.minimum(i, n - 1)), i % 2)

    def run_list(self, kind, item, n, dummy):
        def at(p):
            return tuple(jnp.where(p < 0, dummy, z) for z in item(jnp.clip(p, 0, n - 1)))

        @pl.loop(0, n // 2)
        def _(i):
            p = 2 * i
            for slot in range(2):
                self.half(kind, [at(p + slot - 1), at(p + slot), at(p + slot + 1), at(p + slot + 3)], slot)

    def pull(self, t, s):
        a = self.acc[t, s]
        return (self.v[t, s] * a[3:4] - a)[0:3]

    def scores(self, weight_total):
        rows = [jnp.sum(self.score[s], axis=0, keepdims=True) for s in range(self.copies)]
        rows += [jnp.sum(self.count[...], axis=0, keepdims=True), weight_total]
        total = jnp.zeros((8, LANES), F32)
        for k, x in enumerate(rows):
            total = total + x * self.unit(2 + k)
        return jnp.broadcast_to(jnp.sum(total, axis=1, keepdims=True), (8, LANES))


def finish_list(e, item, n, dummy, also=lambda: None):
    @pl.when(n % 2 == 1)
    def _():
        before = tuple(jnp.where(n > 1, z, dummy) for z in item(jnp.maximum(n - 2, 0)))
        also()
        e.cross_collect(before, 1)
        e.cross_factor(item(n - 1), 0)
        e.cross_collect(item(n - 1), 0)

    @pl.when(n % 2 == 0)
    def _():
        also()
        e.cross_collect(item(n - 1), 1)


def interior_kernel(base_ref, part_ref, pred_ref, true_ref, kind_ref, pull_ref, stat_ref, x_ref, mom_ref, self_refs, *scratch, copies, tiles):
    e = Engine(copies, scratch)
    own = e.for_self(self_refs)
    base = base_ref[0]
    rows = 3 * copies
    e.begin(tiles)
    own.begin_right()
    x_ref[...] = jnp.zeros_like(x_ref)
    mom_ref[...] = jnp.zeros_like(mom_ref)

    unroll = next(u for u in (6, 4, 3, 2, 1) if tiles % u == 0)

    def prepare(m, n):
        for q in range(unroll):
            t = m * unroll + q
            for o in range(1, BAND + 1):
                e.items[0, n] = t - o
                e.items[1, n] = t
                e.items[2, n] = 2
                n = n + jnp.where(listed(part_ref, t, base + t - o) & (t >= o), 1, 0)
            sl = pl.ds(pl.multiple_of(t * LANES, LANES), LANES)
            kind = kind_ref[:, sl]
            weight = jnp.where(kind == 1, 5.0, jnp.where(kind == 2, 10.0, 1.0))
            for c in range(3):
                x_ref[q, c * copies:(c + 1) * copies, :] = pred_ref[c, :, sl] * 0.5
            x_ref[q, rows:rows + 3, :] = true_ref[:, sl] * 0.5
            e.place(t, x_ref.at[q])
            e.cut[t] = jnp.where(kind == 1, 15.0, 7.5)
            x = x_ref[q]
            wx = x * weight
            terms = [wx * x[rows + c:rows + c + 1] for c in range(3)] + [wx, wx * x]
            for i, term in enumerate(terms):
                total, error = two_sum(mom_ref[0, i], term)
                mom_ref[0, i] = total
                mom_ref[1, i] += error
            mom_ref[0, 5, 0:1, :] += weight
            e.prep(t)
        return n

    n = lax.fori_loop(0, tiles // unroll, prepare, jnp.int32(0))

    blank = jnp.zeros((LANES - 80, LANES), F32)
    high, low = (jnp.concatenate([mom_ref[part, i] for i in range(5)] + [blank], axis=0).T for part in range(2))
    sums = [(high[8 * k:8 * k + 8], low[8 * k:8 * k + 8]) for k in range(16)]
    while len(sums) > 1:
        sums = [pair_add(a, b) for a, b in zip(sums[::2], sums[1::2])]
    sums = sums[0]
    for k in (4, 2, 1):
        sums = pair_add(sums, (roll(sums[0], k, 0), roll(sums[1], k, 0)))
    moments = [x * e.unit(0) for x in sums]

    def twin(i):
        return 2 * i, 2 * i + 1

    def item(i):
        return e.items[0, i], e.items[1, i], e.items[2, i]

    for k, z in enumerate((tiles, tiles, 0)):
        e.items[k, 0] = jnp.where(n == 0, z, e.items[k, 0])
    n = jnp.maximum(n, 1)
    half = tiles // 2
    own.begin_list("self", twin, half)
    e.begin_list("cross", item, n)
    own.run_list("self", twin, half, tiles)
    e.run_list("cross", item, n, tiles)
    finish_list(e, item, n, tiles, lambda: own.self_collect(twin(half - 1), 1))

    @pl.loop(0, tiles // unroll)
    def _(m):
        for q in range(unroll):
            t = m * unroll + q
            sl = pl.ds(pl.multiple_of(t * LANES, LANES), LANES)
            for s in range(copies):
                pull = e.pull(t, s)
                for c in range(3):
                    pull_ref[c, s:s + 1, sl] = pull[c:c + 1]

    stat_ref[0] = moments[0] + e.scores(mom_ref[0, 5, 0:1, :])
    stat_ref[1] = moments[1]


def edge_kernel(base_ref, part_ref, pred_ref, true_ref, kind_ref, low_ref, high_ref, stat_ref, pull_ref, out_ref, x_ref, *scratch, copies, tiles):
    e = Engine(copies, scratch)
    base = base_ref[0]
    span = BAND * LANES
    local = tiles * LANES
    window = 4 * BAND
    e.begin(window)
    rows = 3 * copies
    for q in range(BAND):
        sl = slice(q * LANES, q * LANES + LANES)
        for ref, t in ((low_ref, q), (high_ref, 3 * BAND + q)):
            x_ref[t] = ref[:, sl]
        for start, t in ((0, BAND + q), (local - span, 2 * BAND + q)):
            sl = slice(start + q * LANES, start + q * LANES + LANES)
            for c in range(3):
                x_ref[t, c * copies:(c + 1) * copies, :] = pred_ref[c, :, sl] * 0.5
            x_ref[t, rows:rows + 3, :] = true_ref[:, sl] * 0.5
            x_ref[t, rows + 3:rows + 4, :] = jnp.where(kind_ref[:, sl] == 1, 15.0, 7.5)
    for t in range(window):
        e.place(t, x_ref.at[t])
        e.cut[t] = x_ref[t, rows + 3:rows + 4, :]
    n = jnp.int32(0)
    for o in range(1, BAND + 1):
        for k in range(o):
            for owner, other, g, j in ((k, k - o, BAND + k - o, BAND + k), (tiles - 1 - k, tiles - 1 - k + o, 3 * BAND - 1 - k, 3 * BAND - 1 - k + o)):
                e.items[0, n] = g
                e.items[1, n] = j
                e.items[2, n] = 1
                n = n + jnp.where(listed(part_ref, owner, base + other), 1, 0)

    def item(i):
        return e.items[0, i], e.items[1, i], e.items[2, i]

    @pl.when(n > 0)
    def _():
        for t in range(window):
            e.prep(t)
        e.begin_list("cross", item, n)
        e.run_list("cross", item, n, window)
        finish_list(e, item, n, window)

    for t in range(2 * BAND):
        for s in range(copies):
            pull = e.pull(BAND + t, s)
            for c in range(3):
                pull_ref[c, s:s + 1, t * LANES:(t + 1) * LANES] = pull[c:c + 1]
    out_ref[0] = stat_ref[0] + e.scores(jnp.zeros((1, LANES), F32))
    out_ref[1] = stat_ref[1]


def solve_kernel(stat_ref, noise_ref, loss_ref, sum_ref, m_ref, k_ref, s_ref, *, copies, atoms):
    rows = 3 * copies
    for part in range(2):
        column = jnp.broadcast_to(stat_ref[part, 0:1, :], (LANES, LANES)).T
        s_ref[part] = column

    def per_copy(c, q, scale):
        return tuple(s_ref[part, 16 * q + c * copies:16 * q + (c + 1) * copies, :] * scale for part in range(2))

    def shared(r, q, scale):
        return tuple(s_ref[part, 16 * q + r:16 * q + r + 1, :] * scale for part in range(2))

    def wide(x):
        return tuple(jnp.broadcast_to(v, (copies, LANES)) for v in x)

    weight_sum = jnp.broadcast_to(stat_ref[0, copies + 3:copies + 4, :], (copies, LANES))
    count = jnp.broadcast_to(stat_ref[0, copies + 2:copies + 3, :], (copies, LANES)) * 16.0
    score = stat_ref[0, 2:copies + 2, :] * 2.0 + 0.5 * count
    pred_sum = [wide(per_copy(c, 3, 2.0)) for c in range(3)]
    true_sum = [wide(shared(rows + c, 3, 2.0)) for c in range(3)]
    pred_mean = [pair_div(x, weight_sum) for x in pred_sum]
    true_mean = [pair_div(x, weight_sum) for x in true_sum]
    cov = [[pair_add(wide(per_copy(c, d, 4.0)), pair_neg(pair_mul(pred_sum[c], true_mean[d]))) for d in range(3)] for c in range(3)]
    ct = {}
    for d in range(3):
        for e in range(d + 1):
            ct[d, e] = pair_add(wide(shared(rows + d, e, 4.0)), pair_neg(pair_mul(true_sum[d], true_mean[e])))
    var = None
    for c in range(3):
        term = pair_add(wide(per_copy(c, 4, 4.0)), pair_neg(pair_mul(pred_sum[c], pred_mean[c])))
        var = term if var is None else pair_add(var, term)

    x = [[cov[c][d][0] for d in range(3)] for c in range(3)]
    frobenius = jnp.sqrt(sum(x[c][d] * x[c][d] for c in range(3) for d in range(3)))
    x = [[x[c][d] / frobenius for d in range(3)] for c in range(3)]

    def sweep(_, flat):
        x = [flat[0:3], flat[3:6], flat[6:9]]
        gram = {}
        for a in range(3):
            for b in range(a + 1):
                gram[a, b] = gram[b, a] = x[a][0] * x[b][0] + x[a][1] * x[b][1] + x[a][2] * x[b][2]
        return tuple(1.5 * x[a][d] - 0.5 * (gram[a, 0] * x[0][d] + gram[a, 1] * x[1][d] + gram[a, 2] * x[2][d])
                     for a in range(3) for d in range(3))

    flat = lax.fori_loop(0, SWEEPS, sweep, tuple(v for line in x for v in line))
    x = [flat[0:3], flat[3:6], flat[6:9]]

    square = var
    nothing = jnp.zeros((copies, LANES), F32)
    for c in range(3):
        for d in range(3):
            square = pair_add(square, pair_mul((-2.0 * x[c][d], nothing), cov[c][d]))
    for d in range(3):
        for e in range(d + 1):
            gram = None
            for c in range(3):
                term = two_prod(x[c][d], x[c][e])
                gram = term if gram is None else pair_add(gram, term)
            if d != e:
                gram = (2.0 * gram[0], 2.0 * gram[1])
            square = pair_add(square, pair_mul(gram, ct[d, e]))

    row = lax.broadcasted_iota(jnp.int32, (copies, LANES), 0)
    noise = nothing
    for s in range(copies):
        noise = jnp.where(row == s, noise_ref[s], noise)
    loss_weight = (noise * noise + SIGMA * SIGMA) / (noise * SIGMA * (noise * SIGMA))
    mean_square = (square[0] + square[1]) / (3.0 * weight_sum)
    loss = loss_weight * mean_square + 1.0 - score / count
    for s in range(copies):
        loss_ref[s] = loss[s, 0]
    sum_ref[...] = jnp.broadcast_to(jnp.sum(loss, axis=0, keepdims=True), (8, LANES))

    grad_scale = 16.0 * atoms
    for c in range(3):
        for d in range(3):
            m_ref[3 * c + d] = x[c][d]
        m_ref[9 + c] = pred_mean[c][0]
        k_ref[c:c + 1, :] = true_mean[c][0][0:1]
    m_ref[12] = grad_scale * 2.0 * loss_weight / (3.0 * weight_sum)
    m_ref[13] = grad_scale / count


def gradient_kernel(m_ref, k_ref, pred_ref, true_ref, kind_ref, pull_ref, edge_ref, grad_ref, *, copies, tiles):
    for t in range(tiles):
        sl = slice(t * LANES, (t + 1) * LANES)
        kind = kind_ref[:, sl]
        weight = jnp.where(kind == 1, 5.0, jnp.where(kind == 2, 10.0, 1.0))
        centred = true_ref[:, sl] - k_ref[0:3, :]
        for c in range(3):
            target = m_ref[3 * c] * centred[0:1] + m_ref[3 * c + 1] * centred[1:2] + m_ref[3 * c + 2] * centred[2:3] + m_ref[9 + c]
            deviation = pred_ref[c, :, sl] - target
            grad_ref[c, :, sl] = m_ref[12] * weight * deviation - m_ref[13] * pull_ref[c, :, sl]

    for t in range(2 * BAND):
        start = t * LANES if t < BAND else (tiles - 2 * BAND + t) * LANES
        for c in range(3):
            grad_ref[c, :, start:start + LANES] -= m_ref[13] * edge_ref[c, :, t * LANES:(t + 1) * LANES]


def pack_kernel(part_ref, noise_ref, pred_ref, true_ref, kind_ref, first_ref, last_ref, *, copies, tiles):
    span = BAND * LANES
    for ref, start in ((first_ref, 0), (last_ref, tiles * LANES - span)):
        sl = slice(start, start + span)
        for c in range(3):
            ref[c * copies:(c + 1) * copies, :] = pred_ref[c, :, sl] * 0.5
        ref[3 * copies:3 * copies + 3, :] = true_ref[:, sl] * 0.5
        ref[3 * copies + 3:3 * copies + 4, :] = jnp.where(kind_ref[:, sl] == 1, 15.0, 7.5)


VMEM = pl.BlockSpec(memory_space=pltpu.VMEM)
SMEM = pl.BlockSpec(memory_space=pltpu.SMEM)
PARAMS = pltpu.CompilerParams(vmem_limit_bytes=40 * 2**20)


def swap(x, axis, step):
    return lax.ppermute(x, axis, [(i, i ^ step) for i in range(lax.axis_size(axis))])


def shards(coords_pred, coords_true, atom_kind, partners, noise_level):
    copies, _, local = coords_pred.shape
    tiles = partners.shape[0]
    rows = 3 * copies
    size = lax.axis_size("res")
    kind = atom_kind[None]
    coords_pred = jnp.transpose(coords_pred, (1, 0, 2))
    base = (lax.axis_index("res") * tiles)[None].astype(jnp.int32)
    stats_shape = jax.ShapeDtypeStruct((2, 8, LANES), F32)

    block = jax.ShapeDtypeStruct((rows + 4, BAND * LANES), F32)
    first, last = pl.pallas_call(
        functools.partial(pack_kernel, copies=copies, tiles=tiles),
        in_specs=[SMEM, SMEM] + [VMEM] * 3,
        out_specs=[VMEM, VMEM],
        out_shape=[block, block],
        name="pack",
    )(partners, noise_level, coords_pred, coords_true, kind)
    forward = [(i, i + 1) for i in range(size - 1)]
    low = lax.ppermute(last, "res", forward)
    high = lax.ppermute(first, "res", [(b, a) for a, b in forward])

    pull, stats = pl.pallas_call(
        functools.partial(interior_kernel, copies=copies, tiles=tiles),
        in_specs=[SMEM, SMEM] + [VMEM] * 3,
        out_specs=[VMEM, VMEM],
        out_shape=[jax.ShapeDtypeStruct((3, copies, local), F32), stats_shape],
        scratch_shapes=[pltpu.VMEM((6, 16, LANES), F32), pltpu.VMEM((2, 6, 16, LANES), F32), Engine.self_scratch(copies)] + Engine.scratch(tiles, copies, BAND * tiles),
        compiler_params=PARAMS,
        cost_estimate=pl.CostEstimate(flops=10**8, bytes_accessed=10**6, transcendentals=10**7),
        name="interior",
    )(base, partners, coords_pred, coords_true, kind)
    edge_pull, stats = pl.pallas_call(
        functools.partial(edge_kernel, copies=copies, tiles=tiles),
        in_specs=[SMEM, SMEM] + [VMEM] * 6,
        out_specs=[VMEM, VMEM],
        out_shape=[jax.ShapeDtypeStruct((3, copies, 2 * BAND * LANES), F32), stats_shape],
        scratch_shapes=[pltpu.VMEM((4 * BAND, 16, LANES), F32)] + Engine.scratch(4 * BAND, copies, BAND * (BAND + 1)),
        compiler_params=PARAMS,
        name="edges",
    )(base, partners, coords_pred, coords_true, kind, low, high, stats)

    step = 1
    while step < size:
        other = swap(stats, "res", step)
        total, error = two_sum(stats[0], other[0])
        stats = jnp.stack([total, (stats[1] + other[1]) + error])
        step *= 2

    copy_loss, total, maps, centre = pl.pallas_call(
        functools.partial(solve_kernel, copies=copies, atoms=local * size),
        in_specs=[VMEM, SMEM],
        out_specs=[SMEM] + [VMEM] * 3,
        out_shape=[
            jax.ShapeDtypeStruct((copies,), F32),
            jax.ShapeDtypeStruct((8, LANES), F32),
            jax.ShapeDtypeStruct((14, copies, LANES), F32),
            jax.ShapeDtypeStruct((8, LANES), F32),
        ],
        scratch_shapes=[pltpu.VMEM((2, LANES, LANES), F32)],
        name="solve",
    )(stats, noise_level)
    step = 1
    while step < lax.axis_size("samp"):
        total = total + swap(total, "samp", step)
        step *= 2
    mean_loss = total[0, 0] / (copies * lax.axis_size("samp"))
    grad = pl.pallas_call(
        functools.partial(gradient_kernel, copies=copies, tiles=tiles),
        in_specs=[VMEM] * 7,
        out_specs=VMEM,
        out_shape=jax.ShapeDtypeStruct((3, copies, local), F32),
        cost_estimate=pl.CostEstimate(flops=10**6, bytes_accessed=10**6, transcendentals=0),
        name="gradient",
    )(maps, centre, coords_pred, coords_true, kind, pull, edge_pull)
    return copy_loss, mean_loss, jnp.transpose(grad, (1, 0, 2))


def solution(mesh):
    in_specs = (P("samp", None, "res"), P(None, "res"), P("res"), P("res", None), P("samp"))
    out_specs = (P("samp"), P(), P("samp", None, "res"))
    return jax.shard_map(shards, mesh=mesh, in_specs=in_specs, out_specs=out_specs, check_vma=False)
```

```python
import functools

import jax
import jax.numpy as jnp
from jax import lax
from jax.experimental import pallas as pl
from jax.experimental.pallas import tpu as pltpu
from jax.sharding import PartitionSpec as P

LANES = 128
BAND = 2
SWEEPS = 20
SIGMA = 16.0
HALF_THRESHOLDS = (0.25, 0.5, 1.0, 2.0)
EPS = 0.25e-6
F32 = jnp.float32
BF16 = jnp.bfloat16


def roll(x, shift, axis=1):
    return pltpu.roll(x, shift, axis)


def two_sum(a, b):
    s = a + b
    t = s - a
    return s, (a - (s - t)) + (b - t)


def two_prod(a, b):
    def halves(x):
        t = x * 4097.0
        h = t - (t - x)
        return h, x - h

    p = a * b
    ah, al = halves(a)
    bh, bl = halves(b)
    return p, ((ah * bh - p) + ah * bl + al * bh) + al * bl


def pair_add(x, y):
    s, e = two_sum(x[0], y[0])
    return two_sum(s, e + (x[1] + y[1]))


def pair_neg(x):
    return -x[0], -x[1]


def pair_mul(x, y):
    p, e = two_prod(x[0], y[0])
    return two_sum(p, e + (x[0] * y[1] + x[1] * y[0]))


def pair_div(x, w):
    q = x[0] / w
    p, e = two_prod(q, w)
    return two_sum(q, (((x[0] - p) - e) + x[1]) / w)


def dot(a, b):
    return jnp.dot(a, b, preferred_element_type=F32)


def dot_nt(a, b):
    return lax.dot_general(a, b, (((1,), (1,)), ((), ())), preferred_element_type=F32)


def split3(x):
    a = x.astype(BF16).astype(F32)
    rest = x - a
    b = rest.astype(BF16).astype(F32)
    return a, b, (rest - b).astype(BF16).astype(F32)


def stack(a, b, axis):
    return jnp.concatenate([a, b], axis=axis)


def listed(part_ref, owner, other):
    hit = jnp.bool_(False)
    for k in range(1, part_ref.shape[0]):
        hit = hit | (part_ref[k, owner] == other)
    return hit


def spread(steps, work, ticks):
    state = [0, 0]

    def tick():
        state[0] += 1
        while state[1] < len(steps) and state[1] * ticks * 3 < state[0] * len(steps) * 4:
            steps[state[1]]()
            state[1] += 1

    work(tick)
    for step in steps[state[1]:]:
        step()


class Engine:
    names = ("v", "cut", "centre", "left", "point", "right", "true", "weight", "minus", "d", "f", "acc", "score", "count", "tri", "items")

    def __init__(self, copies, refs):
        self.copies = copies
        self.twos = copies // 2
        for name, ref in zip(self.names, refs):
            setattr(self, name, ref)

    @staticmethod
    def scratch(tiles, copies, items):
        n, twos = tiles + 1, copies // 2
        return [
            pltpu.VMEM((n, copies + 1, 8, LANES), F32),
            pltpu.VMEM((n, 1, LANES), F32),
            pltpu.VMEM((n, copies + 1, 8, LANES), F32),
            pltpu.VMEM((n, twos + 1, LANES, LANES), BF16),
            pltpu.VMEM((n, twos, 64, 2 * LANES), BF16),
            [pltpu.VMEM((1, twos + 1, LANES, 2 * LANES), BF16)] * 2,
            [pltpu.VMEM((LANES, LANES), F32)] * 2,
            [pltpu.VMEM((LANES, LANES), F32)] * 2,
            [pltpu.VMEM((LANES, LANES), F32)] * 2,
            [pltpu.VMEM((1, twos + 1, LANES, 2 * LANES), F32)] * 2,
            [pltpu.VMEM((1, twos, 2 * LANES, 2 * LANES), BF16)] * 2,
            pltpu.VMEM((n, copies, 8, LANES), F32),
            pltpu.VMEM((copies, 8, LANES), F32),
            pltpu.VMEM((8, LANES), F32),
            pltpu.VMEM((2, LANES, LANES), BF16),
            pltpu.SMEM((4, items + 2), jnp.int32),
        ]

    @staticmethod
    def self_scratch(copies):
        twos = copies // 2
        return [
            [pltpu.VMEM((2, twos + 1, LANES, 2 * LANES), BF16)] * 2,
            [pltpu.VMEM((2, twos + 1, LANES, 2 * LANES), F32)] * 2,
            [pltpu.VMEM((2, twos, 2 * LANES, 2 * LANES), BF16)] * 2,
        ]

    def for_self(self, refs):
        other = Engine(self.copies, [])
        other.__dict__.update(self.__dict__)
        other.right, other.d, other.f = refs
        return other

    def begin(self, tiles):
        for ref in [self.acc, self.score, self.count, *self.f, self.v.at[tiles], self.cut.at[tiles], self.centre.at[tiles], self.left.at[tiles], self.point.at[tiles]]:
            ref[...] = jnp.zeros_like(ref)
        row = lax.broadcasted_iota(jnp.int32, (LANES, LANES), 0)
        lane = lax.broadcasted_iota(jnp.int32, (LANES, LANES), 1)
        self.tri[0] = jnp.where(lane > row, 1.0, 0.0).astype(BF16)
        self.tri[1] = jnp.where(lane < row, 1.0, 0.0).astype(BF16)
        self.begin_right()

    def begin_right(self):
        pick = jnp.where(lax.broadcasted_iota(jnp.int32, (LANES, LANES), 0) == 7, 1.0, 0.0).astype(BF16)
        for ref in self.right:
            ref[...] = jnp.zeros_like(ref)
            for k in range(ref.shape[0]):
                ref[k, self.twos, :, LANES:] = pick

    def place(self, t, ref):
        blank = jnp.zeros((5, LANES), F32)
        for s in range(self.copies):
            self.v[t, s] = stack(ref[pl.ds(s, 3, stride=self.copies), :], blank, 0)
        self.v[t, self.copies] = stack(ref[3 * self.copies:3 * self.copies + 3, :], blank, 0)

    @staticmethod
    def unit(k):
        return jnp.where(lax.broadcasted_iota(jnp.int32, (8, LANES), 0) == k, 1.0, 0.0)

    def prep(self, t):
        groups = []
        for s in range(self.copies + 1):
            v = self.v[t, s]
            centre = jnp.broadcast_to(jnp.sum(v, axis=1, keepdims=True) * (1.0 / LANES), (8, LANES))
            self.centre[t, s] = centre
            y = v - centre
            norm = jnp.sum(y * y, axis=0, keepdims=True)
            x = y + (self.unit(4) + EPS * self.unit(5)) + norm * self.unit(3)
            if s == self.copies:
                x = x + self.unit(7) * self.cut[t]
            a, b, c = split3(x)
            groups.append(jnp.concatenate([a, a, b, a, b, c, b, c], axis=0))
            if s < self.copies:
                a, b, c = split3(v + self.unit(3))
                p = jnp.concatenate([a, b, c, jnp.zeros_like(a)], axis=0).astype(BF16)
                q = 32 * (s % 2)
                self.point[t, s // 2, q:q + 32, :LANES] = p
                self.point[t, s // 2, q:q + 32, LANES:] = p
        groups.append(jnp.zeros((64, LANES), F32))
        for h in range(self.twos + 1):
            self.left[t, h] = stack(groups[2 * h], groups[2 * h + 1], 0).T.astype(BF16)

    def build(self, slot, k, g, j, s):
        y = self.v[j, s] - self.centre[g, s]
        norm = jnp.sum(y * y, axis=0, keepdims=True)
        a, b, c = split3((self.unit(3) + self.unit(5)) - 2.0 * y + norm * self.unit(4))
        q, m = 64 * (s % 2), LANES * (s % 2)
        self.right[slot][k, s // 2, q:q + 64, m:m + LANES] = jnp.concatenate([a, b, a, c, b, a, c, b], axis=0).astype(BF16)

    def squares(self, slot, k, g, h):
        return dot(self.left[g, h], self.right[slot][k, h])

    def get(self, slot, h, k, lanes, shared):
        one = self.d[slot][0, h, k, lanes]
        if not shared:
            return one
        return jnp.where(self.upper(k), one, self.d[slot][1, h, k, lanes])

    @staticmethod
    def upper(k):
        shape = (k.stop - k.start, LANES)
        return lax.broadcasted_iota(jnp.int32, shape, 1) > lax.broadcasted_iota(jnp.int32, shape, 0) + k.start

    def weigh(self, slot, cuts, share, shared, tick):
        total = jnp.zeros((8, LANES), F32)
        for b in range(16):
            k = slice(8 * b, 8 * b + 8)
            d2 = jnp.maximum(self.get(slot, self.twos, k, slice(0, LANES), shared), EPS)
            dist = d2 * lax.rsqrt(d2)
            cut_j = jnp.where(self.upper(k), cuts[0], cuts[1]) if shared else cuts[0]
            cut_i = self.get(slot, self.twos, k, slice(LANES, 2 * LANES), shared)
            w = jnp.where(dist < cut_j, 0.0625, 0.0) + jnp.where(dist < cut_i, 0.0625, 0.0)
            if shared:
                row = lax.broadcasted_iota(jnp.int32, (8, LANES), 0) + 8 * b
                w = jnp.where(lax.broadcasted_iota(jnp.int32, (8, LANES), 1) == row, 0.0, w)
            self.true[slot][k, :] = dist
            self.weight[slot][k, :] = w
            self.minus[slot][k, :] = -w
            total = total + w
            tick()
        self.count[...] += total * share

    def factor(self, slot, share, shared, tick):
        for s in range(self.copies):
            h, m = s // 2, LANES * (s % 2)
            score = jnp.zeros((8, LANES), F32)
            for q in range(8):
                k = slice(16 * q, 16 * q + 16)
                d2 = jnp.maximum(self.get(slot, h, k, slice(m, m + LANES), shared), EPS)
                r = lax.rsqrt(d2)
                diff = d2 * r - self.true[slot][k, :]
                spread = jnp.abs(diff)
                u = [jnp.tanh(t - spread) for t in HALF_THRESHOLDS]
                w = self.weight[slot][k, :]
                z = w * ((u[0] + u[1]) + (u[2] + u[3]))
                score = score + z[:8] + z[8:]
                slope = ((u[0] * u[0] + u[1] * u[1]) + (u[2] * u[2] + u[3] * u[3])) - 4.0
                f = slope * r * jnp.maximum(jnp.minimum(diff * 1e30, w), self.minus[slot][k, :])
                high = f.astype(BF16)
                low = (f - high.astype(F32)).astype(BF16)
                for i in range(1 + shared):
                    part = (high * self.tri[i, k, :], low * self.tri[i, k, :]) if shared else (high, low)
                    for x, start in zip(part, (16 * q, LANES + 16 * q)):
                        self.f[slot][i, h, start:start + 16, m:m + LANES] = x
                tick()
            self.score[s] += score * share

    @staticmethod
    def fold(z):
        return [z[k:k + 8, m:m + LANES] + z[k + 8:k + 16, m:m + LANES] + z[k + 16:k + 24, m:m + LANES] for k, m in ((0, 0), (32, LANES))]

    def along_j(self, p, f):
        return self.fold(dot(p, f))

    def along_i(self, p, f):
        one = stack(f[:LANES, :LANES], f[LANES:, :LANES], 1)
        two = stack(f[:LANES, LANES:], f[LANES:, LANES:], 1)
        return self.fold(dot_nt(p, stack(one, two, 0)))

    def cross_build(self, item, slot):
        return [functools.partial(self.build, slot, 0, item[0], item[1], s) for s in range(self.copies + 1)]

    def cross_measure(self, item, slot):
        def step(h):
            self.d[slot][0, h] = self.squares(slot, 0, item[0], h)

        return [functools.partial(step, h) for h in [self.twos, *range(self.twos)]]

    def cross_factor(self, item, slot, tick):
        share = item[2].astype(F32) * 0.5
        self.weigh(slot, [self.cut[item[1]]], share, False, tick)
        self.factor(slot, share, False, tick)

    def add(self, t, h, parts):
        for q in range(2):
            self.acc[t, 2 * h + q] += parts[q]

    def cross_collect(self, item, slot):
        steps = []
        for h in range(self.twos):
            steps.append(lambda h=h: self.add(item[1], h, self.along_j(self.point[item[0], h], self.f[slot][0, h])))
            steps.append(lambda h=h: self.add(item[0], h, self.along_i(self.point[item[1], h], self.f[slot][0, h])))
        return steps

    def self_build(self, item, slot):
        return [functools.partial(self.build, slot, k, item[k], item[k], s) for s in range(self.copies + 1) for k in range(2)]

    def self_measure(self, item, slot):
        def step(h, k):
            self.d[slot][k, h] = self.squares(slot, k, item[k], h)

        return [functools.partial(step, h, k) for h in [self.twos, *range(self.twos)] for k in range(2)]

    def self_factor(self, item, slot, tick):
        self.weigh(slot, [self.cut[item[0]], self.cut[item[1]]], 1.0, True, tick)
        self.factor(slot, 1.0, True, tick)

    def self_collect(self, item, slot):
        steps = []
        for h in range(self.twos):
            for k in range(2):
                for side in (self.along_j, self.along_i):
                    steps.append(lambda h=h, k=k, side=side: self.add(item[k], h, side(self.point[item[k], h], self.f[slot][k, h])))
        return steps

    def half(self, kind, items, slot):
        last, now, soon, later = items
        steps = getattr(self, kind + "_collect")(last, 1 - slot)
        steps += getattr(self, kind + "_measure")(soon, 1 - slot)
        steps += getattr(self, kind + "_build")(later, 1 - slot)
        spread(steps, lambda tick: getattr(self, kind + "_factor")(now, slot, tick), 16 + 8 * self.copies)

    def begin_list(self, kind, item, n):
        steps = getattr(self, kind + "_build")(item(0), 0)
        steps += getattr(self, kind + "_measure")(item(0), 0)
        for i in (1, 2):
            steps += getattr(self, kind + "_build")(item(jnp.minimum(i, n - 1)), i % 2)
        for step in steps:
            step()

    def run_list(self, kind, item, n, dummy):
        def at(p):
            return tuple(jnp.where(p < 0, dummy, z) for z in item(jnp.clip(p, 0, n - 1)))

        @pl.loop(0, n // 2)
        def _(i):
            p = 2 * i
            for slot in range(2):
                self.half(kind, [at(p + slot - 1), at(p + slot), at(p + slot + 1), at(p + slot + 3)], slot)

    def pull(self, t, s):
        a = self.acc[t, s]
        return (self.v[t, s] * a[3:4] - a)[0:3]

    def scores(self, weight_total):
        rows = [jnp.sum(self.score[s], axis=0, keepdims=True) for s in range(self.copies)]
        rows += [jnp.sum(self.count[...], axis=0, keepdims=True), weight_total]
        total = jnp.zeros((8, LANES), F32)
        for k, x in enumerate(rows):
            total = total + x * self.unit(2 + k)
        return jnp.broadcast_to(jnp.sum(total, axis=1, keepdims=True), (8, LANES))


def finish_list(e, item, n, dummy, also=()):
    also = list(also)

    @pl.when(n % 2 == 1)
    def _():
        before = tuple(jnp.where(n > 1, z, dummy) for z in item(jnp.maximum(n - 2, 0)))
        spread(also + e.cross_collect(before, 1), lambda tick: e.cross_factor(item(n - 1), 0, tick), 16 + 8 * e.copies)
        for step in e.cross_collect(item(n - 1), 0):
            step()

    @pl.when(n % 2 == 0)
    def _():
        for step in also + e.cross_collect(item(n - 1), 1):
            step()


def interior_kernel(base_ref, part_ref, noise_ref, pred_ref, true_ref, kind_ref, pull_ref, stat_ref, noise_rows_ref, x_ref, mom_ref, self_refs, *scratch, copies, tiles):
    e = Engine(copies, scratch)
    own = e.for_self(self_refs)
    base = base_ref[0]
    rows = 3 * copies
    e.begin(tiles)
    own.begin_right()
    x_ref[...] = jnp.zeros_like(x_ref)
    mom_ref[...] = jnp.zeros_like(mom_ref)

    unroll = next(u for u in (6, 4, 3, 2, 1) if tiles % u == 0)

    def prepare(m, n):
        for q in range(unroll):
            t = m * unroll + q
            for o in range(1, BAND + 1):
                e.items[0, n] = t - o
                e.items[1, n] = t
                e.items[2, n] = 2
                n = n + jnp.where(listed(part_ref, t, base + t - o) & (t >= o), 1, 0)
            sl = pl.ds(pl.multiple_of(t * LANES, LANES), LANES)
            kind = kind_ref[:, sl]
            weight = jnp.where(kind == 1, 5.0, jnp.where(kind == 2, 10.0, 1.0))
            for c in range(3):
                x_ref[q, c * copies:(c + 1) * copies, :] = pred_ref[c, :, sl] * 0.5
            x_ref[q, rows:rows + 3, :] = true_ref[:, sl] * 0.5
            e.place(t, x_ref.at[q])
            e.cut[t] = jnp.where(kind == 1, 15.0, 7.5)
            x = x_ref[q]
            wx = x * weight
            terms = [wx * x[rows + c:rows + c + 1] for c in range(3)] + [wx, wx * x]
            for i, term in enumerate(terms):
                total, error = two_sum(mom_ref[0, i], term)
                mom_ref[0, i] = total
                mom_ref[1, i] += error
            mom_ref[0, 5, 0:1, :] += weight
            e.prep(t)
        return n

    n = lax.fori_loop(0, tiles // unroll, prepare, jnp.int32(0))

    blank = jnp.zeros((LANES - 80, LANES), F32)
    high, low = (jnp.concatenate([mom_ref[part, i] for i in range(5)] + [blank], axis=0).T for part in range(2))
    sums = [(high[8 * k:8 * k + 8], low[8 * k:8 * k + 8]) for k in range(16)]
    while len(sums) > 1:
        sums = [pair_add(a, b) for a, b in zip(sums[::2], sums[1::2])]
    sums = sums[0]
    for k in (4, 2, 1):
        sums = pair_add(sums, (roll(sums[0], k, 0), roll(sums[1], k, 0)))
    moments = [x * e.unit(0) for x in sums]

    def twin(i):
        return 2 * i, 2 * i + 1

    def item(i):
        return e.items[0, i], e.items[1, i], e.items[2, i]

    for k, z in enumerate((tiles, tiles, 0)):
        e.items[k, 0] = jnp.where(n == 0, z, e.items[k, 0])
    n = jnp.maximum(n, 1)
    half = tiles // 2
    own.begin_list("self", twin, half)
    e.begin_list("cross", item, n)
    own.run_list("self", twin, half, tiles)
    e.run_list("cross", item, n, tiles)
    finish_list(e, item, n, tiles, own.self_collect(twin(half - 1), 1))

    @pl.loop(0, tiles // unroll)
    def _(m):
        for q in range(unroll):
            t = m * unroll + q
            sl = pl.ds(pl.multiple_of(t * LANES, LANES), LANES)
            for s in range(copies):
                pull = e.pull(t, s)
                for c in range(3):
                    pull_ref[c, s:s + 1, sl] = pull[c:c + 1]

    stat_ref[0] = moments[0] + e.scores(mom_ref[0, 5, 0:1, :])
    stat_ref[1] = moments[1]
    row = lax.broadcasted_iota(jnp.int32, (copies, LANES), 0)
    noise = jnp.zeros((copies, LANES), F32)
    for s in range(copies):
        noise = jnp.where(row == s, noise_ref[s], noise)
    noise_rows_ref[...] = noise


def edge_kernel(base_ref, part_ref, pred_ref, true_ref, kind_ref, low_ref, high_ref, stat_ref, pull_ref, out_ref, x_ref, *scratch, copies, tiles):
    e = Engine(copies, scratch)
    base = base_ref[0]
    span = BAND * LANES
    local = tiles * LANES
    window = 4 * BAND
    e.begin(window)
    rows = 3 * copies
    for q in range(BAND):
        sl = slice(q * LANES, q * LANES + LANES)
        for ref, t in ((low_ref, q), (high_ref, 3 * BAND + q)):
            x_ref[t] = ref[:, sl]
        for start, t in ((0, BAND + q), (local - span, 2 * BAND + q)):
            sl = slice(start + q * LANES, start + q * LANES + LANES)
            for c in range(3):
                x_ref[t, c * copies:(c + 1) * copies, :] = pred_ref[c, :, sl] * 0.5
            x_ref[t, rows:rows + 3, :] = true_ref[:, sl] * 0.5
            x_ref[t, rows + 3:rows + 4, :] = jnp.where(kind_ref[:, sl] == 1, 15.0, 7.5)
    for t in range(window):
        e.place(t, x_ref.at[t])
        e.cut[t] = x_ref[t, rows + 3:rows + 4, :]
    n = jnp.int32(0)
    for o in range(1, BAND + 1):
        for k in range(o):
            for owner, other, g, j in ((k, k - o, BAND + k - o, BAND + k), (tiles - 1 - k, tiles - 1 - k + o, 3 * BAND - 1 - k, 3 * BAND - 1 - k + o)):
                e.items[0, n] = g
                e.items[1, n] = j
                e.items[2, n] = 1
                n = n + jnp.where(listed(part_ref, owner, base + other), 1, 0)

    def item(i):
        return e.items[0, i], e.items[1, i], e.items[2, i]

    @pl.when(n > 0)
    def _():
        for t in range(window):
            e.prep(t)
        e.begin_list("cross", item, n)
        e.run_list("cross", item, n, window)
        finish_list(e, item, n, window)

    for t in range(2 * BAND):
        for s in range(copies):
            pull = e.pull(BAND + t, s)
            for c in range(3):
                pull_ref[c, s:s + 1, t * LANES:(t + 1) * LANES] = pull[c:c + 1]
    out_ref[0] = stat_ref[0] + e.scores(jnp.zeros((1, LANES), F32))
    out_ref[1] = stat_ref[1]


def solve_kernel(stat_ref, other_ref, noise_ref, loss_ref, sum_ref, m_ref, k_ref, s_ref, *, copies, atoms):
    rows = 3 * copies
    stats, error = two_sum(stat_ref[0], other_ref[0])
    low = (stat_ref[1] + other_ref[1]) + error
    for part, x in enumerate((stats, low)):
        s_ref[part] = jnp.broadcast_to(x[0:1], (LANES, LANES)).T

    def per_copy(c, q, scale):
        return tuple(s_ref[part, 16 * q + c * copies:16 * q + (c + 1) * copies, :] * scale for part in range(2))

    def shared(r, q, scale):
        return tuple(s_ref[part, 16 * q + r:16 * q + r + 1, :] * scale for part in range(2))

    def wide(x):
        return tuple(jnp.broadcast_to(v, (copies, LANES)) for v in x)

    weight_sum = jnp.broadcast_to(stats[copies + 3:copies + 4], (copies, LANES))
    count = jnp.broadcast_to(stats[copies + 2:copies + 3], (copies, LANES)) * 16.0
    score = stats[2:copies + 2] * 2.0 + 0.5 * count
    pred_sum = [wide(per_copy(c, 3, 2.0)) for c in range(3)]
    true_sum = [wide(shared(rows + c, 3, 2.0)) for c in range(3)]
    pred_mean = [pair_div(x, weight_sum) for x in pred_sum]
    true_mean = [pair_div(x, weight_sum) for x in true_sum]
    cov = [[pair_add(wide(per_copy(c, d, 4.0)), pair_neg(pair_mul(pred_sum[c], true_mean[d]))) for d in range(3)] for c in range(3)]
    ct = {}
    for d in range(3):
        for e in range(d + 1):
            ct[d, e] = pair_add(wide(shared(rows + d, e, 4.0)), pair_neg(pair_mul(true_sum[d], true_mean[e])))
    var = None
    for c in range(3):
        term = pair_add(wide(per_copy(c, 4, 4.0)), pair_neg(pair_mul(pred_sum[c], pred_mean[c])))
        var = term if var is None else pair_add(var, term)

    x = [[cov[c][d][0] for d in range(3)] for c in range(3)]
    frobenius = jnp.sqrt(sum(x[c][d] * x[c][d] for c in range(3) for d in range(3)))
    x = [[x[c][d] / frobenius for d in range(3)] for c in range(3)]

    def sweep(_, flat):
        x = [flat[0:3], flat[3:6], flat[6:9]]
        gram = {}
        for a in range(3):
            for b in range(a + 1):
                gram[a, b] = gram[b, a] = x[a][0] * x[b][0] + x[a][1] * x[b][1] + x[a][2] * x[b][2]
        return tuple(1.5 * x[a][d] - 0.5 * (gram[a, 0] * x[0][d] + gram[a, 1] * x[1][d] + gram[a, 2] * x[2][d])
                     for a in range(3) for d in range(3))

    flat = lax.fori_loop(0, SWEEPS, sweep, tuple(v for line in x for v in line))
    x = [flat[0:3], flat[3:6], flat[6:9]]

    square = var
    nothing = jnp.zeros((copies, LANES), F32)
    for c in range(3):
        for d in range(3):
            square = pair_add(square, pair_mul((-2.0 * x[c][d], nothing), cov[c][d]))
    for d in range(3):
        for e in range(d + 1):
            gram = None
            for c in range(3):
                term = two_prod(x[c][d], x[c][e])
                gram = term if gram is None else pair_add(gram, term)
            if d != e:
                gram = (2.0 * gram[0], 2.0 * gram[1])
            square = pair_add(square, pair_mul(gram, ct[d, e]))

    noise = noise_ref[...]
    loss_weight = (noise * noise + SIGMA * SIGMA) / (noise * SIGMA * (noise * SIGMA))
    mean_square = (square[0] + square[1]) / (3.0 * weight_sum)
    loss = loss_weight * mean_square + 1.0 - score / count
    for s in range(copies):
        loss_ref[s] = loss[s, 0]
    sum_ref[...] = jnp.broadcast_to(jnp.sum(loss, axis=0, keepdims=True), (8, LANES))

    grad_scale = 16.0 * atoms
    for c in range(3):
        for d in range(3):
            m_ref[3 * c + d] = x[c][d]
        m_ref[9 + c] = pred_mean[c][0]
        k_ref[c:c + 1, :] = true_mean[c][0][0:1]
    m_ref[12] = grad_scale * 2.0 * loss_weight / (3.0 * weight_sum)
    m_ref[13] = grad_scale / count


def gradient_kernel(m_ref, k_ref, pred_ref, true_ref, kind_ref, pull_ref, edge_ref, grad_ref, *, copies, tiles):
    for t in range(tiles):
        sl = slice(t * LANES, (t + 1) * LANES)
        kind = kind_ref[:, sl]
        weight = jnp.where(kind == 1, 5.0, jnp.where(kind == 2, 10.0, 1.0))
        centred = true_ref[:, sl] - k_ref[0:3, :]
        for c in range(3):
            target = m_ref[3 * c] * centred[0:1] + m_ref[3 * c + 1] * centred[1:2] + m_ref[3 * c + 2] * centred[2:3] + m_ref[9 + c]
            deviation = pred_ref[c, :, sl] - target
            grad_ref[c, :, sl] = m_ref[12] * weight * deviation - m_ref[13] * pull_ref[c, :, sl]

    for t in range(2 * BAND):
        start = t * LANES if t < BAND else (tiles - 2 * BAND + t) * LANES
        for c in range(3):
            grad_ref[c, :, start:start + LANES] -= m_ref[13] * edge_ref[c, :, t * LANES:(t + 1) * LANES]


def pack_kernel(pred_ref, true_ref, kind_ref, first_ref, last_ref, *, copies, tiles):
    span = BAND * LANES
    for ref, start in ((first_ref, 0), (last_ref, tiles * LANES - span)):
        sl = slice(start, start + span)
        for c in range(3):
            ref[c * copies:(c + 1) * copies, :] = pred_ref[c, :, sl] * 0.5
        ref[3 * copies:3 * copies + 3, :] = true_ref[:, sl] * 0.5
        ref[3 * copies + 3:3 * copies + 4, :] = jnp.where(kind_ref[:, sl] == 1, 15.0, 7.5)


VMEM = pl.BlockSpec(memory_space=pltpu.VMEM)
SMEM = pl.BlockSpec(memory_space=pltpu.SMEM)
PARAMS = pltpu.CompilerParams(vmem_limit_bytes=40 * 2**20)
SMALL = pltpu.CompilerParams(vmem_limit_bytes=4 * 2**20)


def swap(x, axis, step):
    return lax.ppermute(x, axis, [(i, i ^ step) for i in range(lax.axis_size(axis))])


def shards(coords_pred, coords_true, atom_kind, partners, noise_level):
    copies, _, local = coords_pred.shape
    tiles = partners.shape[0]
    rows = 3 * copies
    size = lax.axis_size("res")
    kind = atom_kind[None]
    coords_pred = jnp.transpose(coords_pred, (1, 0, 2))
    partners = partners.T
    base = (lax.axis_index("res") * tiles)[None].astype(jnp.int32)
    stats_shape = jax.ShapeDtypeStruct((2, 8, LANES), F32)

    block = jax.ShapeDtypeStruct((rows + 4, BAND * LANES), F32)
    first, last = pl.pallas_call(
        functools.partial(pack_kernel, copies=copies, tiles=tiles),
        in_specs=[VMEM] * 3,
        out_specs=[VMEM, VMEM],
        out_shape=[block, block],
        compiler_params=SMALL,
        name="pack",
    )(coords_pred, coords_true, kind)
    forward = [(i, i + 1) for i in range(size - 1)]
    low = lax.ppermute(last, "res", forward)
    high = lax.ppermute(first, "res", [(b, a) for a, b in forward])

    pull, stats, noise = pl.pallas_call(
        functools.partial(interior_kernel, copies=copies, tiles=tiles),
        in_specs=[SMEM, SMEM, SMEM] + [VMEM] * 3,
        out_specs=[VMEM, VMEM, VMEM],
        out_shape=[jax.ShapeDtypeStruct((3, copies, local), F32), stats_shape, jax.ShapeDtypeStruct((copies, LANES), F32)],
        scratch_shapes=[pltpu.VMEM((6, 16, LANES), F32), pltpu.VMEM((2, 6, 16, LANES), F32), Engine.self_scratch(copies)] + Engine.scratch(tiles, copies, BAND * tiles),
        compiler_params=PARAMS,
        cost_estimate=pl.CostEstimate(flops=10**8, bytes_accessed=10**6, transcendentals=10**7),
        name="interior",
    )(base, partners, noise_level, coords_pred, coords_true, kind)
    edge_pull, stats = pl.pallas_call(
        functools.partial(edge_kernel, copies=copies, tiles=tiles),
        in_specs=[SMEM, SMEM] + [VMEM] * 6,
        out_specs=[VMEM, VMEM],
        out_shape=[jax.ShapeDtypeStruct((3, copies, 2 * BAND * LANES), F32), stats_shape],
        scratch_shapes=[pltpu.VMEM((4 * BAND, 16, LANES), F32)] + Engine.scratch(4 * BAND, copies, BAND * (BAND + 1)),
        compiler_params=PARAMS,
        name="edges",
    )(base, partners, coords_pred, coords_true, kind, low, high, stats)

    step = 1
    while True:
        other = swap(stats, "res", step)
        step *= 2
        if step == size:
            break
        total, error = two_sum(stats[0], other[0])
        stats = jnp.stack([total, (stats[1] + other[1]) + error])

    copy_loss, total, maps, centre = pl.pallas_call(
        functools.partial(solve_kernel, copies=copies, atoms=local * size),
        in_specs=[VMEM] * 3,
        out_specs=[SMEM] + [VMEM] * 3,
        out_shape=[
            jax.ShapeDtypeStruct((copies,), F32),
            jax.ShapeDtypeStruct((8, LANES), F32),
            jax.ShapeDtypeStruct((14, copies, LANES), F32),
            jax.ShapeDtypeStruct((8, LANES), F32),
        ],
        scratch_shapes=[pltpu.VMEM((2, LANES, LANES), F32)],
        compiler_params=SMALL,
        name="solve",
    )(stats, other, noise)
    step = 1
    while step < lax.axis_size("samp"):
        total = total + swap(total, "samp", step)
        step *= 2
    mean_loss = total[0, 0] / (copies * lax.axis_size("samp"))
    grad = pl.pallas_call(
        functools.partial(gradient_kernel, copies=copies, tiles=tiles),
        in_specs=[VMEM] * 7,
        out_specs=VMEM,
        out_shape=jax.ShapeDtypeStruct((3, copies, local), F32),
        cost_estimate=pl.CostEstimate(flops=10**6, bytes_accessed=10**6, transcendentals=0),
        compiler_params=SMALL,
        name="gradient",
    )(maps, centre, coords_pred, coords_true, kind, pull, edge_pull)
    return copy_loss, mean_loss, jnp.transpose(grad, (1, 0, 2))


def solution(mesh):
    in_specs = (P("samp", None, "res"), P(None, "res"), P("res"), P("res", None), P("samp"))
    out_specs = (P("samp"), P(), P("samp", None, "res"))
    return jax.shard_map(shards, mesh=mesh, in_specs=in_specs, out_specs=out_specs, check_vma=False)
```

```python
import functools

import jax
import jax.numpy as jnp
from jax import lax
from jax.experimental import pallas as pl
from jax.experimental.pallas import tpu as pltpu
from jax.sharding import PartitionSpec as P

LANES = 128
BAND = 2
SWEEPS = 20
SIGMA = 16.0
HALF_THRESHOLDS = (0.25, 0.5, 1.0, 2.0)
EPS = 0.25e-6
F32 = jnp.float32
BF16 = jnp.bfloat16


def roll(x, shift, axis=1):
    return pltpu.roll(x, shift, axis)


def two_sum(a, b):
    s = a + b
    t = s - a
    return s, (a - (s - t)) + (b - t)


def two_prod(a, b):
    def halves(x):
        t = x * 4097.0
        h = t - (t - x)
        return h, x - h

    p = a * b
    ah, al = halves(a)
    bh, bl = halves(b)
    return p, ((ah * bh - p) + ah * bl + al * bh) + al * bl


def pair_add(x, y):
    s, e = two_sum(x[0], y[0])
    return two_sum(s, e + (x[1] + y[1]))


def pair_neg(x):
    return -x[0], -x[1]


def pair_mul(x, y):
    p, e = two_prod(x[0], y[0])
    return two_sum(p, e + (x[0] * y[1] + x[1] * y[0]))


def pair_div(x, w):
    q = x[0] / w
    p, e = two_prod(q, w)
    return two_sum(q, (((x[0] - p) - e) + x[1]) / w)


def dot(a, b):
    return jnp.dot(a, b, preferred_element_type=F32)


def dot_nt(a, b):
    return lax.dot_general(a, b, (((1,), (1,)), ((), ())), preferred_element_type=F32)


def split3(x):
    a = x.astype(BF16).astype(F32)
    rest = x - a
    b = rest.astype(BF16).astype(F32)
    return a, b, (rest - b).astype(BF16).astype(F32)


def stack(a, b, axis):
    return jnp.concatenate([a, b], axis=axis)


def listed(part_ref, owner, other):
    hit = jnp.bool_(False)
    for k in range(1, part_ref.shape[0]):
        hit = hit | (part_ref[k, owner] == other)
    return hit


def spread(steps, work, ticks):
    state = [0, 0]

    def tick():
        state[0] += 1
        while state[1] < len(steps) and state[1] * ticks * 3 < state[0] * len(steps) * 4:
            steps[state[1]]()
            state[1] += 1

    work(tick)
    for step in steps[state[1]:]:
        step()


class Engine:
    names = ("v", "cut", "centre", "left", "point", "right", "true", "weight", "minus", "d", "f", "acc", "score", "count", "tri", "items")

    def __init__(self, copies, refs):
        self.copies = copies
        self.twos = copies // 2
        for name, ref in zip(self.names, refs):
            setattr(self, name, ref)

    @staticmethod
    def scratch(tiles, copies, items):
        n, twos = tiles + 1, copies // 2
        return [
            pltpu.VMEM((n, copies + 1, 8, LANES), F32),
            pltpu.VMEM((n, 1, LANES), F32),
            pltpu.VMEM((n, copies + 1, 8, LANES), F32),
            pltpu.VMEM((n, twos + 1, LANES, LANES), BF16),
            pltpu.VMEM((n, twos, 64, 2 * LANES), BF16),
            [pltpu.VMEM((1, twos + 1, LANES, 2 * LANES), BF16)] * 2,
            [pltpu.VMEM((LANES, LANES), F32)] * 2,
            [pltpu.VMEM((LANES, LANES), F32)] * 2,
            [pltpu.VMEM((LANES, LANES), F32)] * 2,
            [pltpu.VMEM((1, twos + 1, LANES, 2 * LANES), F32)] * 2,
            [pltpu.VMEM((1, twos, 2 * LANES, 2 * LANES), BF16)] * 2,
            pltpu.VMEM((n, copies, 8, LANES), F32),
            pltpu.VMEM((copies, 8, LANES), F32),
            pltpu.VMEM((8, LANES), F32),
            pltpu.VMEM((2, LANES, LANES), BF16),
            pltpu.SMEM((4, items + 2), jnp.int32),
        ]

    @staticmethod
    def self_scratch(copies):
        twos = copies // 2
        return [
            [pltpu.VMEM((2, twos + 1, LANES, 2 * LANES), BF16)] * 2,
            [pltpu.VMEM((2, twos + 1, LANES, 2 * LANES), F32)] * 2,
            [pltpu.VMEM((2, twos, 2 * LANES, 2 * LANES), BF16)] * 2,
        ]

    def for_self(self, refs):
        other = Engine(self.copies, [])
        other.__dict__.update(self.__dict__)
        other.right, other.d, other.f = refs
        return other

    def begin(self, tiles):
        for ref in [self.acc, self.score, self.count, *self.f, self.v.at[tiles], self.cut.at[tiles], self.centre.at[tiles], self.left.at[tiles], self.point.at[tiles]]:
            ref[...] = jnp.zeros_like(ref)
        row = lax.broadcasted_iota(jnp.int32, (LANES, LANES), 0)
        lane = lax.broadcasted_iota(jnp.int32, (LANES, LANES), 1)
        self.tri[0] = jnp.where(lane > row, 1.0, 0.0).astype(BF16)
        self.tri[1] = jnp.where(lane < row, 1.0, 0.0).astype(BF16)
        self.begin_right()

    def begin_right(self):
        pick = jnp.where(lax.broadcasted_iota(jnp.int32, (LANES, LANES), 0) == 7, 1.0, 0.0).astype(BF16)
        for ref in self.right:
            ref[...] = jnp.zeros_like(ref)
            for k in range(ref.shape[0]):
                ref[k, self.twos, :, LANES:] = pick

    def place(self, t, ref):
        blank = jnp.zeros((5, LANES), F32)
        for s in range(self.copies):
            self.v[t, s] = stack(ref[pl.ds(s, 3, stride=self.copies), :], blank, 0)
        self.v[t, self.copies] = stack(ref[3 * self.copies:3 * self.copies + 3, :], blank, 0)

    @staticmethod
    def unit(k):
        return jnp.where(lax.broadcasted_iota(jnp.int32, (8, LANES), 0) == k, 1.0, 0.0)

    def prep(self, t):
        groups = []
        for s in range(self.copies + 1):
            v = self.v[t, s]
            centre = jnp.broadcast_to(jnp.sum(v, axis=1, keepdims=True) * (1.0 / LANES), (8, LANES))
            self.centre[t, s] = centre
            y = v - centre
            norm = jnp.sum(y * y, axis=0, keepdims=True)
            x = y + (self.unit(4) + EPS * self.unit(5)) + norm * self.unit(3)
            if s == self.copies:
                x = x + self.unit(7) * self.cut[t]
            a, b, c = split3(x)
            groups.append(jnp.concatenate([a, a, b, a, b, c, b, c], axis=0))
            if s < self.copies:
                a, b, c = split3(v + self.unit(3))
                p = jnp.concatenate([a, b, c, jnp.zeros_like(a)], axis=0).astype(BF16)
                q = 32 * (s % 2)
                self.point[t, s // 2, q:q + 32, :LANES] = p
                self.point[t, s // 2, q:q + 32, LANES:] = p
        groups.append(jnp.zeros((64, LANES), F32))
        for h in range(self.twos + 1):
            self.left[t, h] = stack(groups[2 * h], groups[2 * h + 1], 0).T.astype(BF16)

    def build(self, slot, k, g, j, s):
        y = self.v[j, s] - self.centre[g, s]
        norm = jnp.sum(y * y, axis=0, keepdims=True)
        a, b, c = split3((self.unit(3) + self.unit(5)) - 2.0 * y + norm * self.unit(4))
        q, m = 64 * (s % 2), LANES * (s % 2)
        self.right[slot][k, s // 2, q:q + 64, m:m + LANES] = jnp.concatenate([a, b, a, c, b, a, c, b], axis=0).astype(BF16)

    def squares(self, slot, k, g, h):
        return dot(self.left[g, h], self.right[slot][k, h])

    def get(self, slot, h, k, lanes, shared):
        one = self.d[slot][0, h, k, lanes]
        if not shared:
            return one
        return jnp.where(self.upper(k), one, self.d[slot][1, h, k, lanes])

    @staticmethod
    def upper(k):
        shape = (k.stop - k.start, LANES)
        return lax.broadcasted_iota(jnp.int32, shape, 1) > lax.broadcasted_iota(jnp.int32, shape, 0) + k.start

    def weigh(self, slot, cuts, share, shared, tick):
        total = jnp.zeros((8, LANES), F32)
        for b in range(16):
            k = slice(8 * b, 8 * b + 8)
            d2 = jnp.maximum(self.get(slot, self.twos, k, slice(0, LANES), shared), EPS)
            dist = d2 * lax.rsqrt(d2)
            cut_j = jnp.where(self.upper(k), cuts[0], cuts[1]) if shared else cuts[0]
            cut_i = self.get(slot, self.twos, k, slice(LANES, 2 * LANES), shared)
            w = jnp.where(dist < cut_j, 0.0625, 0.0) + jnp.where(dist < cut_i, 0.0625, 0.0)
            if shared:
                row = lax.broadcasted_iota(jnp.int32, (8, LANES), 0) + 8 * b
                w = jnp.where(lax.broadcasted_iota(jnp.int32, (8, LANES), 1) == row, 0.0, w)
            self.true[slot][k, :] = dist
            self.weight[slot][k, :] = w
            self.minus[slot][k, :] = -w
            total = total + w
            tick()
        self.count[...] += total * share

    def factor(self, slot, share, shared, tick):
        for s in range(self.copies):
            h, m = s // 2, LANES * (s % 2)
            score = jnp.zeros((8, LANES), F32)
            for q in range(8):
                k = slice(16 * q, 16 * q + 16)
                d2 = jnp.maximum(self.get(slot, h, k, slice(m, m + LANES), shared), EPS)
                r = lax.rsqrt(d2)
                diff = d2 * r - self.true[slot][k, :]
                spread = jnp.abs(diff)
                u = [jnp.tanh(t - spread) for t in HALF_THRESHOLDS]
                w = self.weight[slot][k, :]
                z = w * ((u[0] + u[1]) + (u[2] + u[3]))
                score = score + z[:8] + z[8:]
                slope = ((u[0] * u[0] + u[1] * u[1]) + (u[2] * u[2] + u[3] * u[3])) - 4.0
                f = slope * r * jnp.maximum(jnp.minimum(diff * 1e30, w), self.minus[slot][k, :])
                high = f.astype(BF16)
                low = (f - high.astype(F32)).astype(BF16)
                for i in range(1 + shared):
                    part = (high * self.tri[i, k, :], low * self.tri[i, k, :]) if shared else (high, low)
                    for x, start in zip(part, (16 * q, LANES + 16 * q)):
                        self.f[slot][i, h, start:start + 16, m:m + LANES] = x
                tick()
            self.score[s] += score * share

    @staticmethod
    def fold(z):
        return [z[k:k + 8, m:m + LANES] + z[k + 8:k + 16, m:m + LANES] + z[k + 16:k + 24, m:m + LANES] for k, m in ((0, 0), (32, LANES))]

    def along_j(self, p, f):
        return self.fold(dot(p, f))

    def along_i(self, p, f):
        one = stack(f[:LANES, :LANES], f[LANES:, :LANES], 1)
        two = stack(f[:LANES, LANES:], f[LANES:, LANES:], 1)
        return self.fold(dot_nt(p, stack(one, two, 0)))

    def cross_build(self, item, slot):
        return [functools.partial(self.build, slot, 0, item[0], item[1], s) for s in range(self.copies + 1)]

    def cross_measure(self, item, slot):
        def step(h):
            self.d[slot][0, h] = self.squares(slot, 0, item[0], h)

        return [functools.partial(step, h) for h in [self.twos, *range(self.twos)]]

    def cross_factor(self, item, slot, tick):
        share = item[2].astype(F32) * 0.5
        self.weigh(slot, [self.cut[item[1]]], share, False, tick)
        self.factor(slot, share, False, tick)

    def add(self, t, h, parts):
        for q in range(2):
            self.acc[t, 2 * h + q] += parts[q]

    def cross_collect(self, item, slot):
        steps = []
        for h in range(self.twos):
            steps.append(lambda h=h: self.add(item[1], h, self.along_j(self.point[item[0], h], self.f[slot][0, h])))
            steps.append(lambda h=h: self.add(item[0], h, self.along_i(self.point[item[1], h], self.f[slot][0, h])))
        return steps

    def self_build(self, item, slot):
        return [functools.partial(self.build, slot, k, item[k], item[k], s) for s in range(self.copies + 1) for k in range(2)]

    def self_measure(self, item, slot):
        def step(h, k):
            self.d[slot][k, h] = self.squares(slot, k, item[k], h)

        return [functools.partial(step, h, k) for h in [self.twos, *range(self.twos)] for k in range(2)]

    def self_factor(self, item, slot, tick):
        self.weigh(slot, [self.cut[item[0]], self.cut[item[1]]], 1.0, True, tick)
        self.factor(slot, 1.0, True, tick)

    def self_collect(self, item, slot):
        steps = []
        for h in range(self.twos):
            for k in range(2):
                for side in (self.along_j, self.along_i):
                    steps.append(lambda h=h, k=k, side=side: self.add(item[k], h, side(self.point[item[k], h], self.f[slot][k, h])))
        return steps

    def half(self, kind, items, slot):
        last, now, soon, later = items
        steps = getattr(self, kind + "_collect")(last, 1 - slot)
        steps += getattr(self, kind + "_measure")(soon, 1 - slot)
        steps += getattr(self, kind + "_build")(later, 1 - slot)
        spread(steps, lambda tick: getattr(self, kind + "_factor")(now, slot, tick), 16 + 8 * self.copies)

    def begin_list(self, kind, item, n):
        steps = getattr(self, kind + "_build")(item(0), 0)
        steps += getattr(self, kind + "_measure")(item(0), 0)
        for i in (1, 2):
            steps += getattr(self, kind + "_build")(item(jnp.minimum(i, n - 1)), i % 2)
        for step in steps:
            step()

    def run_list(self, kind, item, n, dummy):
        def at(p):
            return tuple(jnp.where(p < 0, dummy, z) for z in item(jnp.clip(p, 0, n - 1)))

        @pl.loop(0, n // 2)
        def _(i):
            p = 2 * i
            for slot in range(2):
                self.half(kind, [at(p + slot - 1), at(p + slot), at(p + slot + 1), at(p + slot + 3)], slot)

    def pull(self, t, s):
        a = self.acc[t, s]
        return (self.v[t, s] * a[3:4] - a)[0:3]

    def scores(self, weight_total):
        rows = [jnp.sum(self.score[s], axis=0, keepdims=True) for s in range(self.copies)]
        rows += [jnp.sum(self.count[...], axis=0, keepdims=True), weight_total]
        total = jnp.zeros((8, LANES), F32)
        for k, x in enumerate(rows):
            total = total + x * self.unit(2 + k)
        return jnp.broadcast_to(jnp.sum(total, axis=1, keepdims=True), (8, LANES))


def finish_list(e, item, n, dummy, also=()):
    also = list(also)

    @pl.when(n % 2 == 1)
    def _():
        before = tuple(jnp.where(n > 1, z, dummy) for z in item(jnp.maximum(n - 2, 0)))
        spread(also + e.cross_collect(before, 1), lambda tick: e.cross_factor(item(n - 1), 0, tick), 16 + 8 * e.copies)
        for step in e.cross_collect(item(n - 1), 0):
            step()

    @pl.when(n % 2 == 0)
    def _():
        for step in also + e.cross_collect(item(n - 1), 1):
            step()


def interior_kernel(base_ref, part_ref, pred_ref, true_ref, kind_ref, pull_ref, stat_ref, x_ref, mom_ref, self_refs, *scratch, copies, tiles):
    e = Engine(copies, scratch)
    own = e.for_self(self_refs)
    base = base_ref[0]
    rows = 3 * copies
    e.begin(tiles)
    own.begin_right()
    x_ref[...] = jnp.zeros_like(x_ref)
    mom_ref[...] = jnp.zeros_like(mom_ref)

    unroll = next(u for u in (6, 4, 3, 2, 1) if tiles % u == 0)

    def prepare(m, n):
        for q in range(unroll):
            t = m * unroll + q
            for o in range(1, BAND + 1):
                e.items[0, n] = t - o
                e.items[1, n] = t
                e.items[2, n] = 2
                n = n + jnp.where(listed(part_ref, t, base + t - o) & (t >= o), 1, 0)
            sl = pl.ds(pl.multiple_of(t * LANES, LANES), LANES)
            kind = kind_ref[:, sl]
            weight = jnp.where(kind == 1, 5.0, jnp.where(kind == 2, 10.0, 1.0))
            for c in range(3):
                x_ref[q, c * copies:(c + 1) * copies, :] = pred_ref[c, :, sl] * 0.5
            x_ref[q, rows:rows + 3, :] = true_ref[:, sl] * 0.5
            e.place(t, x_ref.at[q])
            e.cut[t] = jnp.where(kind == 1, 15.0, 7.5)
            x = x_ref[q]
            wx = x * weight
            terms = [wx * x[rows + c:rows + c + 1] for c in range(3)] + [wx, wx * x]
            for i, term in enumerate(terms):
                total, error = two_sum(mom_ref[0, i], term)
                mom_ref[0, i] = total
                mom_ref[1, i] += error
            mom_ref[0, 5, 0:1, :] += weight
            e.prep(t)
        return n

    n = lax.fori_loop(0, tiles // unroll, prepare, jnp.int32(0))

    blank = jnp.zeros((LANES - 80, LANES), F32)
    high, low = (jnp.concatenate([mom_ref[part, i] for i in range(5)] + [blank], axis=0).T for part in range(2))
    sums = [(high[8 * k:8 * k + 8], low[8 * k:8 * k + 8]) for k in range(16)]
    while len(sums) > 1:
        sums = [pair_add(a, b) for a, b in zip(sums[::2], sums[1::2])]
    sums = sums[0]
    for k in (4, 2, 1):
        sums = pair_add(sums, (roll(sums[0], k, 0), roll(sums[1], k, 0)))
    moments = [x * e.unit(0) for x in sums]

    def twin(i):
        return 2 * i, 2 * i + 1

    def item(i):
        return e.items[0, i], e.items[1, i], e.items[2, i]

    for k, z in enumerate((tiles, tiles, 0)):
        e.items[k, 0] = jnp.where(n == 0, z, e.items[k, 0])
    n = jnp.maximum(n, 1)
    half = tiles // 2
    own.begin_list("self", twin, half)
    e.begin_list("cross", item, n)
    own.run_list("self", twin, half, tiles)
    e.run_list("cross", item, n, tiles)
    finish_list(e, item, n, tiles, own.self_collect(twin(half - 1), 1))

    @pl.loop(0, tiles // unroll)
    def _(m):
        for q in range(unroll):
            t = m * unroll + q
            sl = pl.ds(pl.multiple_of(t * LANES, LANES), LANES)
            for s in range(copies):
                pull = e.pull(t, s)
                for c in range(3):
                    pull_ref[c, s:s + 1, sl] = pull[c:c + 1]

    stat_ref[0] = moments[0] + e.scores(mom_ref[0, 5, 0:1, :])
    stat_ref[1] = moments[1]


def edge_kernel(base_ref, part_ref, pred_ref, true_ref, kind_ref, low_ref, high_ref, stat_ref, pull_ref, out_ref, x_ref, *scratch, copies, tiles):
    e = Engine(copies, scratch)
    base = base_ref[0]
    span = BAND * LANES
    local = tiles * LANES
    window = 4 * BAND
    e.begin(window)
    rows = 3 * copies
    for q in range(BAND):
        sl = slice(q * LANES, q * LANES + LANES)
        for ref, t in ((low_ref, q), (high_ref, 3 * BAND + q)):
            x_ref[t] = ref[:, sl]
        for start, t in ((0, BAND + q), (local - span, 2 * BAND + q)):
            sl = slice(start + q * LANES, start + q * LANES + LANES)
            for c in range(3):
                x_ref[t, c * copies:(c + 1) * copies, :] = pred_ref[c, :, sl] * 0.5
            x_ref[t, rows:rows + 3, :] = true_ref[:, sl] * 0.5
            x_ref[t, rows + 3:rows + 4, :] = jnp.where(kind_ref[:, sl] == 1, 15.0, 7.5)
    for t in range(window):
        e.place(t, x_ref.at[t])
        e.cut[t] = x_ref[t, rows + 3:rows + 4, :]
    n = jnp.int32(0)
    for o in range(1, BAND + 1):
        for k in range(o):
            for owner, other, g, j in ((k, k - o, BAND + k - o, BAND + k), (tiles - 1 - k, tiles - 1 - k + o, 3 * BAND - 1 - k, 3 * BAND - 1 - k + o)):
                e.items[0, n] = g
                e.items[1, n] = j
                e.items[2, n] = 1
                n = n + jnp.where(listed(part_ref, owner, base + other), 1, 0)

    def item(i):
        return e.items[0, i], e.items[1, i], e.items[2, i]

    @pl.when(n > 0)
    def _():
        for t in range(window):
            e.prep(t)
        e.begin_list("cross", item, n)
        e.run_list("cross", item, n, window)
        finish_list(e, item, n, window)

    for t in range(2 * BAND):
        for s in range(copies):
            pull = e.pull(BAND + t, s)
            for c in range(3):
                pull_ref[c, s:s + 1, t * LANES:(t + 1) * LANES] = pull[c:c + 1]
    out_ref[0] = stat_ref[0] + e.scores(jnp.zeros((1, LANES), F32))
    out_ref[1] = stat_ref[1]


def solve_kernel(stat_ref, other_ref, noise_ref, loss_ref, sum_ref, m_ref, k_ref, s_ref, *, copies, atoms):
    rows = 3 * copies
    stats, error = two_sum(stat_ref[0], other_ref[0])
    low = (stat_ref[1] + other_ref[1]) + error
    for part, x in enumerate((stats, low)):
        s_ref[part] = jnp.broadcast_to(x[0:1], (LANES, LANES)).T

    def per_copy(c, q, scale):
        return tuple(s_ref[part, 16 * q + c * copies:16 * q + (c + 1) * copies, :] * scale for part in range(2))

    def shared(r, q, scale):
        return tuple(s_ref[part, 16 * q + r:16 * q + r + 1, :] * scale for part in range(2))

    def wide(x):
        return tuple(jnp.broadcast_to(v, (copies, LANES)) for v in x)

    weight_sum = jnp.broadcast_to(stats[copies + 3:copies + 4], (copies, LANES))
    count = jnp.broadcast_to(stats[copies + 2:copies + 3], (copies, LANES)) * 16.0
    score = stats[2:copies + 2] * 2.0 + 0.5 * count
    pred_sum = [wide(per_copy(c, 3, 2.0)) for c in range(3)]
    true_sum = [wide(shared(rows + c, 3, 2.0)) for c in range(3)]
    pred_mean = [pair_div(x, weight_sum) for x in pred_sum]
    true_mean = [pair_div(x, weight_sum) for x in true_sum]
    cov = [[pair_add(wide(per_copy(c, d, 4.0)), pair_neg(pair_mul(pred_sum[c], true_mean[d]))) for d in range(3)] for c in range(3)]
    ct = {}
    for d in range(3):
        for e in range(d + 1):
            ct[d, e] = pair_add(wide(shared(rows + d, e, 4.0)), pair_neg(pair_mul(true_sum[d], true_mean[e])))
    var = None
    for c in range(3):
        term = pair_add(wide(per_copy(c, 4, 4.0)), pair_neg(pair_mul(pred_sum[c], pred_mean[c])))
        var = term if var is None else pair_add(var, term)

    x = [[cov[c][d][0] for d in range(3)] for c in range(3)]
    frobenius = jnp.sqrt(sum(x[c][d] * x[c][d] for c in range(3) for d in range(3)))
    x = [[x[c][d] / frobenius for d in range(3)] for c in range(3)]

    def sweep(_, flat):
        x = [flat[0:3], flat[3:6], flat[6:9]]
        gram = {}
        for a in range(3):
            for b in range(a + 1):
                gram[a, b] = gram[b, a] = x[a][0] * x[b][0] + x[a][1] * x[b][1] + x[a][2] * x[b][2]
        return tuple(1.5 * x[a][d] - 0.5 * (gram[a, 0] * x[0][d] + gram[a, 1] * x[1][d] + gram[a, 2] * x[2][d])
                     for a in range(3) for d in range(3))

    flat = lax.fori_loop(0, SWEEPS, sweep, tuple(v for line in x for v in line))
    x = [flat[0:3], flat[3:6], flat[6:9]]

    square = var
    nothing = jnp.zeros((copies, LANES), F32)
    for c in range(3):
        for d in range(3):
            square = pair_add(square, pair_mul((-2.0 * x[c][d], nothing), cov[c][d]))
    for d in range(3):
        for e in range(d + 1):
            gram = None
            for c in range(3):
                term = two_prod(x[c][d], x[c][e])
                gram = term if gram is None else pair_add(gram, term)
            if d != e:
                gram = (2.0 * gram[0], 2.0 * gram[1])
            square = pair_add(square, pair_mul(gram, ct[d, e]))

    noise = noise_ref[...]
    loss_weight = (noise * noise + SIGMA * SIGMA) / (noise * SIGMA * (noise * SIGMA))
    mean_square = (square[0] + square[1]) / (3.0 * weight_sum)
    loss = loss_weight * mean_square + 1.0 - score / count
    for s in range(copies):
        loss_ref[s] = loss[s, 0]
    sum_ref[...] = jnp.broadcast_to(jnp.sum(loss, axis=0, keepdims=True), (8, LANES))

    grad_scale = 16.0 * atoms
    for c in range(3):
        for d in range(3):
            m_ref[3 * c + d] = x[c][d]
        m_ref[9 + c] = pred_mean[c][0]
        k_ref[c:c + 1, :] = true_mean[c][0][0:1]
    m_ref[12] = grad_scale * 2.0 * loss_weight / (3.0 * weight_sum)
    m_ref[13] = grad_scale / count


def gradient_kernel(m_ref, k_ref, pred_ref, true_ref, kind_ref, pull_ref, edge_ref, grad_ref, *, copies, tiles):
    for t in range(tiles):
        sl = slice(t * LANES, (t + 1) * LANES)
        kind = kind_ref[:, sl]
        weight = jnp.where(kind == 1, 5.0, jnp.where(kind == 2, 10.0, 1.0))
        centred = true_ref[:, sl] - k_ref[0:3, :]
        for c in range(3):
            target = m_ref[3 * c] * centred[0:1] + m_ref[3 * c + 1] * centred[1:2] + m_ref[3 * c + 2] * centred[2:3] + m_ref[9 + c]
            deviation = pred_ref[c, :, sl] - target
            grad_ref[c, :, sl] = m_ref[12] * weight * deviation - m_ref[13] * pull_ref[c, :, sl]

    for t in range(2 * BAND):
        start = t * LANES if t < BAND else (tiles - 2 * BAND + t) * LANES
        for c in range(3):
            grad_ref[c, :, start:start + LANES] -= m_ref[13] * edge_ref[c, :, t * LANES:(t + 1) * LANES]


def pack_kernel(pred_hbm, true_hbm, kind_hbm, part_hbm, noise_hbm, first_ref, last_ref, pred_ref, true_ref, kind_ref, part_ref, noise_ref, noise_smem, sems, *, copies, tiles):
    span = BAND * LANES
    moves = [
        pltpu.make_async_copy(source, target, sems.at[i])
        for i, (source, target) in enumerate(
            ((pred_hbm, pred_ref), (true_hbm, true_ref), (kind_hbm, kind_ref), (part_hbm, part_ref), (noise_hbm, noise_smem))
        )
    ]
    for move in moves:
        move.start()
    for move in moves:
        move.wait()
    for ref, start in ((first_ref, 0), (last_ref, tiles * LANES - span)):
        sl = slice(start, start + span)
        for c in range(3):
            ref[c * copies:(c + 1) * copies, :] = pred_ref[c, :, sl] * 0.5
        ref[3 * copies:3 * copies + 3, :] = true_ref[:, sl] * 0.5
        ref[3 * copies + 3:3 * copies + 4, :] = jnp.where(kind_ref[:, sl] == 1, 15.0, 7.5)
    row = lax.broadcasted_iota(jnp.int32, (copies, LANES), 0)
    noise = jnp.zeros((copies, LANES), F32)
    for s in range(copies):
        noise = jnp.where(row == s, noise_smem[s], noise)
    noise_ref[...] = noise


VMEM = pl.BlockSpec(memory_space=pltpu.VMEM)
SMEM = pl.BlockSpec(memory_space=pltpu.SMEM)
PARAMS = pltpu.CompilerParams(vmem_limit_bytes=40 * 2**20)
SMALL = pltpu.CompilerParams(vmem_limit_bytes=4 * 2**20)


def swap(x, axis, step):
    return lax.ppermute(x, axis, [(i, i ^ step) for i in range(lax.axis_size(axis))])


def shards(coords_pred, coords_true, atom_kind, partners, noise_level):
    copies, _, local = coords_pred.shape
    tiles = partners.shape[0]
    rows = 3 * copies
    size = lax.axis_size("res")
    kind = atom_kind[None]
    coords_pred = jnp.transpose(coords_pred, (1, 0, 2))
    partners = partners.T
    base = (lax.axis_index("res") * tiles)[None].astype(jnp.int32)
    stats_shape = jax.ShapeDtypeStruct((2, 8, LANES), F32)

    block = jax.ShapeDtypeStruct((rows + 4, BAND * LANES), F32)
    same = [jax.ShapeDtypeStruct(x.shape, x.dtype) for x in (coords_pred, coords_true, kind, partners)]
    first, last, coords_pred, coords_true, kind, partners, noise = pl.pallas_call(
        functools.partial(pack_kernel, copies=copies, tiles=tiles),
        in_specs=[pl.BlockSpec(memory_space=pltpu.HBM)] * 5,
        out_specs=[VMEM] * 7,
        out_shape=[block, block, *same, jax.ShapeDtypeStruct((copies, LANES), F32)],
        scratch_shapes=[pltpu.SMEM((copies,), F32), pltpu.SemaphoreType.DMA((5,))],
        compiler_params=SMALL,
        name="pack",
    )(*(pltpu.with_memory_space_constraint(x, pltpu.HBM) for x in (coords_pred, coords_true, kind, partners, noise_level)))
    forward = [(i, i + 1) for i in range(size - 1)]
    low = lax.ppermute(last, "res", forward)
    high = lax.ppermute(first, "res", [(b, a) for a, b in forward])

    pull, stats = pl.pallas_call(
        functools.partial(interior_kernel, copies=copies, tiles=tiles),
        in_specs=[SMEM, SMEM] + [VMEM] * 3,
        out_specs=[VMEM, VMEM],
        out_shape=[jax.ShapeDtypeStruct((3, copies, local), F32), stats_shape],
        scratch_shapes=[pltpu.VMEM((6, 16, LANES), F32), pltpu.VMEM((2, 6, 16, LANES), F32), Engine.self_scratch(copies)] + Engine.scratch(tiles, copies, BAND * tiles),
        compiler_params=PARAMS,
        cost_estimate=pl.CostEstimate(flops=10**8, bytes_accessed=10**6, transcendentals=10**7),
        name="interior",
    )(base, partners, coords_pred, coords_true, kind)
    edge_pull, stats = pl.pallas_call(
        functools.partial(edge_kernel, copies=copies, tiles=tiles),
        in_specs=[SMEM, SMEM] + [VMEM] * 6,
        out_specs=[VMEM, VMEM],
        out_shape=[jax.ShapeDtypeStruct((3, copies, 2 * BAND * LANES), F32), stats_shape],
        scratch_shapes=[pltpu.VMEM((4 * BAND, 16, LANES), F32)] + Engine.scratch(4 * BAND, copies, BAND * (BAND + 1)),
        compiler_params=PARAMS,
        name="edges",
    )(base, partners, coords_pred, coords_true, kind, low, high, stats)

    step = 1
    while True:
        other = swap(stats, "res", step)
        step *= 2
        if step == size:
            break
        total, error = two_sum(stats[0], other[0])
        stats = jnp.stack([total, (stats[1] + other[1]) + error])

    copy_loss, total, maps, centre = pl.pallas_call(
        functools.partial(solve_kernel, copies=copies, atoms=local * size),
        in_specs=[VMEM] * 3,
        out_specs=[SMEM] + [VMEM] * 3,
        out_shape=[
            jax.ShapeDtypeStruct((copies,), F32),
            jax.ShapeDtypeStruct((8, LANES), F32),
            jax.ShapeDtypeStruct((14, copies, LANES), F32),
            jax.ShapeDtypeStruct((8, LANES), F32),
        ],
        scratch_shapes=[pltpu.VMEM((2, LANES, LANES), F32)],
        compiler_params=SMALL,
        name="solve",
    )(stats, other, noise)
    step = 1
    while step < lax.axis_size("samp"):
        total = total + swap(total, "samp", step)
        step *= 2
    mean_loss = total[0, 0] / (copies * lax.axis_size("samp"))
    grad = pl.pallas_call(
        functools.partial(gradient_kernel, copies=copies, tiles=tiles),
        in_specs=[VMEM] * 7,
        out_specs=VMEM,
        out_shape=jax.ShapeDtypeStruct((3, copies, local), F32),
        cost_estimate=pl.CostEstimate(flops=10**6, bytes_accessed=10**6, transcendentals=0),
        compiler_params=SMALL,
        name="gradient",
    )(maps, centre, coords_pred, coords_true, kind, pull, edge_pull)
    return copy_loss, mean_loss, jnp.transpose(grad, (1, 0, 2))


def solution(mesh):
    in_specs = (P("samp", None, "res"), P(None, "res"), P("res"), P("res", None), P("samp"))
    out_specs = (P("samp"), P(), P("samp", None, "res"))
    return jax.shard_map(shards, mesh=mesh, in_specs=in_specs, out_specs=out_specs, check_vma=False)
```

```python
import functools

import jax
import jax.numpy as jnp
from jax import lax
from jax.experimental import pallas as pl
from jax.experimental.pallas import tpu as pltpu
from jax.sharding import PartitionSpec as P

LANES = 128
BAND = 2
SWEEPS = 20
SIGMA = 16.0
HALF_THRESHOLDS = (0.25, 0.5, 1.0, 2.0)
EPS = 0.25e-6
F32 = jnp.float32
BF16 = jnp.bfloat16


def roll(x, shift, axis=1):
    return pltpu.roll(x, shift, axis)


def two_sum(a, b):
    s = a + b
    t = s - a
    return s, (a - (s - t)) + (b - t)


def two_prod(a, b):
    def halves(x):
        t = x * 4097.0
        h = t - (t - x)
        return h, x - h

    p = a * b
    ah, al = halves(a)
    bh, bl = halves(b)
    return p, ((ah * bh - p) + ah * bl + al * bh) + al * bl


def pair_add(x, y):
    s, e = two_sum(x[0], y[0])
    return two_sum(s, e + (x[1] + y[1]))


def pair_neg(x):
    return -x[0], -x[1]


def pair_mul(x, y):
    p, e = two_prod(x[0], y[0])
    return two_sum(p, e + (x[0] * y[1] + x[1] * y[0]))


def pair_div(x, w):
    q = x[0] / w
    p, e = two_prod(q, w)
    return two_sum(q, (((x[0] - p) - e) + x[1]) / w)


def dot(a, b):
    return jnp.dot(a, b, preferred_element_type=F32)


def dot_nt(a, b):
    return lax.dot_general(a, b, (((1,), (1,)), ((), ())), preferred_element_type=F32)


def split3(x):
    a = x.astype(BF16).astype(F32)
    rest = x - a
    b = rest.astype(BF16).astype(F32)
    return a, b, (rest - b).astype(BF16).astype(F32)


def stack(a, b, axis):
    return jnp.concatenate([a, b], axis=axis)


def listed(part_ref, owner, other):
    hit = jnp.bool_(False)
    for k in range(1, part_ref.shape[0]):
        hit = hit | (part_ref[k, owner] == other)
    return hit


def spread(steps, work, ticks):
    state = [0, 0]

    def tick():
        state[0] += 1
        while state[1] < len(steps) and state[1] * ticks * 3 < state[0] * len(steps) * 4:
            steps[state[1]]()
            state[1] += 1

    work(tick)
    for step in steps[state[1]:]:
        step()


class Engine:
    shared = ("v", "cut", "centre", "left", "point", "acc", "score", "count")
    work = ("true", "weight", "minus", "right", "d", "f")

    def __init__(self, copies, tiles, shared, work):
        self.copies = copies
        self.twos = copies // 2
        self.low, self.high, self.dummy = tiles, tiles + BAND, tiles + 2 * BAND
        for name, ref in zip(self.shared + self.work, (*shared, *work)):
            setattr(self, name, ref)

    @staticmethod
    def shared_shapes(tiles, copies):
        n, twos = tiles + 2 * BAND + 1, copies // 2
        return [
            jax.ShapeDtypeStruct(shape, dtype)
            for shape, dtype in (
                ((n, copies + 1, 8, LANES), F32),
                ((n, 1, LANES), F32),
                ((n, copies + 1, 8, LANES), F32),
                ((n, twos + 1, LANES, LANES), BF16),
                ((n, twos, 64, 2 * LANES), BF16),
                ((n, copies * 8, LANES), F32),
                ((copies, 8, LANES), F32),
                ((8, LANES), F32),
            )
        ]

    @staticmethod
    def work_shapes(copies, parts):
        twos = copies // 2
        return [[pltpu.VMEM((LANES, LANES), F32)] * 2] * 3 + [
            [pltpu.VMEM((parts, twos + 1, LANES, 2 * LANES), BF16)] * 2,
            [pltpu.VMEM((parts, twos + 1, LANES, 2 * LANES), F32)] * 2,
            [pltpu.VMEM((parts, twos, 2 * LANES, 2 * LANES), BF16)] * 2,
        ]

    def begin_right(self):
        pick = jnp.where(lax.broadcasted_iota(jnp.int32, (LANES, LANES), 0) == 7, 1.0, 0.0).astype(BF16)
        for ref in self.right:
            ref[...] = jnp.zeros_like(ref)
            for k in range(ref.shape[0]):
                ref[k, self.twos, :, LANES:] = pick
        for ref in self.f:
            ref[0] = jnp.zeros(ref.shape[1:], BF16)

    def place(self, t, ref):
        blank = jnp.zeros((5, LANES), F32)
        for s in range(self.copies):
            self.v[t, s] = stack(ref[pl.ds(s, 3, stride=self.copies), :], blank, 0)
        self.v[t, self.copies] = stack(ref[3 * self.copies:3 * self.copies + 3, :], blank, 0)

    @staticmethod
    def unit(k):
        return jnp.where(lax.broadcasted_iota(jnp.int32, (8, LANES), 0) == k, 1.0, 0.0)

    def prep(self, t):
        groups = []
        for s in range(self.copies + 1):
            v = self.v[t, s]
            centre = jnp.broadcast_to(jnp.sum(v, axis=1, keepdims=True) * (1.0 / LANES), (8, LANES))
            self.centre[t, s] = centre
            y = v - centre
            norm = jnp.sum(y * y, axis=0, keepdims=True)
            x = y + (self.unit(4) + EPS * self.unit(5)) + norm * self.unit(3)
            if s == self.copies:
                x = x + self.unit(7) * self.cut[t]
            a, b, c = split3(x)
            groups.append(jnp.concatenate([a, a, b, a, b, c, b, c], axis=0))
            if s < self.copies:
                a, b, c = split3(v + self.unit(3))
                p = jnp.concatenate([a, b, c, jnp.zeros_like(a)], axis=0).astype(BF16)
                q = 32 * (s % 2)
                self.point[t, s // 2, q:q + 32, :LANES] = p
                self.point[t, s // 2, q:q + 32, LANES:] = p
        groups.append(jnp.zeros((64, LANES), F32))
        for h in range(self.twos + 1):
            self.left[t, h] = stack(groups[2 * h], groups[2 * h + 1], 0).T.astype(BF16)

    def build(self, slot, k, g, j, s):
        y = self.v[j, s] - self.centre[g, s]
        norm = jnp.sum(y * y, axis=0, keepdims=True)
        a, b, c = split3((self.unit(3) + self.unit(5)) - 2.0 * y + norm * self.unit(4))
        q, m = 64 * (s % 2), LANES * (s % 2)
        self.right[slot][k, s // 2, q:q + 64, m:m + LANES] = jnp.concatenate([a, b, a, c, b, a, c, b], axis=0).astype(BF16)

    def squares(self, slot, k, g, h):
        return dot(self.left[g, h], self.right[slot][k, h])

    def get(self, slot, h, k, lanes, shared):
        one = self.d[slot][0, h, k, lanes]
        if not shared:
            return one
        return jnp.where(self.upper(k), one, self.d[slot][1, h, k, lanes])

    @staticmethod
    def upper(k):
        shape = (k.stop - k.start, LANES)
        return lax.broadcasted_iota(jnp.int32, shape, 1) > lax.broadcasted_iota(jnp.int32, shape, 0) + k.start

    def weigh(self, slot, cuts, share, shared, tick):
        total = jnp.zeros((8, LANES), F32)
        for b in range(16):
            k = slice(8 * b, 8 * b + 8)
            d2 = jnp.maximum(self.get(slot, self.twos, k, slice(0, LANES), shared), EPS)
            dist = d2 * lax.rsqrt(d2)
            cut_j = jnp.where(self.upper(k), cuts[0], cuts[1]) if shared else cuts[0]
            cut_i = self.get(slot, self.twos, k, slice(LANES, 2 * LANES), shared)
            w = jnp.where(dist < cut_j, 0.0625, 0.0) + jnp.where(dist < cut_i, 0.0625, 0.0)
            if shared:
                row = lax.broadcasted_iota(jnp.int32, (8, LANES), 0) + 8 * b
                w = jnp.where(lax.broadcasted_iota(jnp.int32, (8, LANES), 1) == row, 0.0, w)
            self.true[slot][k, :] = dist
            self.weight[slot][k, :] = w
            self.minus[slot][k, :] = -w
            total = total + w
            tick()
        self.count[...] += total * share

    def factor(self, slot, share, shared, tick):
        for s in range(self.copies):
            h, m = s // 2, LANES * (s % 2)
            score = jnp.zeros((8, LANES), F32)
            for q in range(8):
                k = slice(16 * q, 16 * q + 16)
                d2 = jnp.maximum(self.get(slot, h, k, slice(m, m + LANES), shared), EPS)
                r = lax.rsqrt(d2)
                diff = d2 * r - self.true[slot][k, :]
                spread = jnp.abs(diff)
                u = [jnp.tanh(t - spread) for t in HALF_THRESHOLDS]
                w = self.weight[slot][k, :]
                z = w * ((u[0] + u[1]) + (u[2] + u[3]))
                score = score + z[:8] + z[8:]
                slope = ((u[0] * u[0] + u[1] * u[1]) + (u[2] * u[2] + u[3] * u[3])) - 4.0
                f = slope * r * jnp.maximum(jnp.minimum(diff * 1e30, w), self.minus[slot][k, :])
                high = f.astype(BF16)
                low = (f - high.astype(F32)).astype(BF16)
                for i in range(1 + shared):
                    part = (high * self.tri[i, k, :], low * self.tri[i, k, :]) if shared else (high, low)
                    for x, start in zip(part, (16 * q, LANES + 16 * q)):
                        self.f[slot][i, h, start:start + 16, m:m + LANES] = x
                tick()
            self.score[s] += score * share

    @staticmethod
    def fold(z):
        return [z[k:k + 8, m:m + LANES] + z[k + 8:k + 16, m:m + LANES] + z[k + 16:k + 24, m:m + LANES] for k, m in ((0, 0), (32, LANES))]

    def along_j(self, p, f):
        return self.fold(dot(p, f))

    def along_i(self, p, f):
        one = stack(f[:LANES, :LANES], f[LANES:, :LANES], 1)
        two = stack(f[:LANES, LANES:], f[LANES:, LANES:], 1)
        return self.fold(dot_nt(p, stack(one, two, 0)))

    def cross_build(self, item, slot):
        return [functools.partial(self.build, slot, 0, item[0], item[1], s) for s in range(self.copies + 1)]

    def cross_measure(self, item, slot):
        def step(h):
            self.d[slot][0, h] = self.squares(slot, 0, item[0], h)

        return [functools.partial(step, h) for h in [self.twos, *range(self.twos)]]

    def cross_factor(self, item, slot, tick):
        share = item[2].astype(F32) * 0.5
        self.weigh(slot, [self.cut[item[1]]], share, False, tick)
        self.factor(slot, share, False, tick)

    def add(self, t, h, parts):
        for q in range(2):
            self.acc[t, 8 * (2 * h + q):8 * (2 * h + q) + 8, :] += parts[q]

    def cross_collect(self, item, slot):
        steps = []
        for h in range(self.twos):
            steps.append(lambda h=h: self.add(item[1], h, self.along_j(self.point[item[0], h], self.f[slot][0, h])))
            steps.append(lambda h=h: self.add(item[0], h, self.along_i(self.point[item[1], h], self.f[slot][0, h])))
        return steps

    def self_build(self, item, slot):
        return [functools.partial(self.build, slot, k, item[k], item[k], s) for s in range(self.copies + 1) for k in range(2)]

    def self_measure(self, item, slot):
        def step(h, k):
            self.d[slot][k, h] = self.squares(slot, k, item[k], h)

        return [functools.partial(step, h, k) for h in [self.twos, *range(self.twos)] for k in range(2)]

    def self_factor(self, item, slot, tick):
        self.weigh(slot, [self.cut[item[0]], self.cut[item[1]]], 1.0, True, tick)
        self.factor(slot, 1.0, True, tick)

    def self_collect(self, item, slot):
        steps = []
        for h in range(self.twos):
            for k in range(2):
                for side in (self.along_j, self.along_i):
                    steps.append(lambda h=h, k=k, side=side: self.add(item[k], h, side(self.point[item[k], h], self.f[slot][k, h])))
        return steps

    def half(self, kind, items, slot):
        last, now, soon, later = items
        steps = getattr(self, kind + "_collect")(last, 1 - slot)
        steps += getattr(self, kind + "_measure")(soon, 1 - slot)
        steps += getattr(self, kind + "_build")(later, 1 - slot)
        spread(steps, lambda tick: getattr(self, kind + "_factor")(now, slot, tick), 16 + 8 * self.copies)

    def begin_list(self, kind, item, n):
        steps = getattr(self, kind + "_build")(item(0), 0)
        steps += getattr(self, kind + "_measure")(item(0), 0)
        for i in (1, 2):
            steps += getattr(self, kind + "_build")(item(jnp.minimum(i, n - 1)), i % 2)
        for step in steps:
            step()

    def run_list(self, kind, item, n, dummy):
        def at(p):
            return tuple(jnp.where(p < 0, dummy, z) for z in item(jnp.clip(p, 0, n - 1)))

        @pl.loop(0, n // 2)
        def _(i):
            p = 2 * i
            for slot in range(2):
                self.half(kind, [at(p + slot - 1), at(p + slot), at(p + slot + 1), at(p + slot + 3)], slot)

    def end_list(self, kind, item, n, dummy):
        def last(i, slot):
            return getattr(self, kind + "_collect")(item(i), slot)

        def odd():
            before = tuple(jnp.where(n > 1, z, dummy) for z in item(jnp.maximum(n - 2, 0)))
            steps = getattr(self, kind + "_collect")(before, 1)
            spread(steps, lambda tick: getattr(self, kind + "_factor")(item(n - 1), 0, tick), 16 + 8 * self.copies)
            for step in last(n - 1, 0):
                step()

        def even():
            for step in last(n - 1, 1):
                step()

        if isinstance(n, int):
            (odd if n % 2 else even)()
        else:
            pl.when(n % 2 == 1)(odd)
            pl.when(n % 2 == 0)(even)

    def scores(self, weight_total):
        rows = [jnp.sum(self.score[s], axis=0, keepdims=True) for s in range(self.copies)]
        rows += [jnp.sum(self.count[...], axis=0, keepdims=True), weight_total]
        total = jnp.zeros((8, LANES), F32)
        for k, x in enumerate(rows):
            total = total + x * self.unit(2 + k)
        return jnp.broadcast_to(jnp.sum(total, axis=1, keepdims=True), (8, LANES))


def self_kernel(base_ref, part_ref, pred_ref, true_ref, kind_ref, *refs, copies, tiles):
    count = len(Engine.shared)
    shared, (items, moment_ref), (x_ref, sum_ref, tri), work = refs[:count], refs[count:count + 2], refs[count + 2:count + 5], refs[count + 5:]
    e = Engine(copies, tiles, shared, work)
    e.tri = tri
    base = base_ref[0]
    rows = 3 * copies
    e.begin_right()
    for ref in [e.acc, e.score, e.count, x_ref, sum_ref, *(r.at[e.dummy] for r in shared[:5])]:
        ref[...] = jnp.zeros_like(ref)
    row = lax.broadcasted_iota(jnp.int32, (LANES, LANES), 0)
    lane = lax.broadcasted_iota(jnp.int32, (LANES, LANES), 1)
    tri[0] = jnp.where(lane > row, 1.0, 0.0).astype(BF16)
    tri[1] = jnp.where(lane < row, 1.0, 0.0).astype(BF16)

    def append(n, owner, other, g, j, share):
        for k, z in enumerate((g, j, share)):
            items[k, n] = jnp.int32(z)
        return n + jnp.where(listed(part_ref, owner, base + other), 1, 0)

    unroll = next(u for u in (6, 4, 3, 2, 1) if tiles % u == 0)

    def prepare(m, n):
        for q in range(unroll):
            t = m * unroll + q
            for o in range(1, BAND + 1):
                more = append(n, t, t - o, t - o, t, 2)
                n = jnp.where(t >= o, more, n)
            sl = pl.ds(pl.multiple_of(t * LANES, LANES), LANES)
            kind = kind_ref[:, sl]
            weight = jnp.where(kind == 1, 5.0, jnp.where(kind == 2, 10.0, 1.0))
            for c in range(3):
                x_ref[q, c * copies:(c + 1) * copies, :] = pred_ref[c, :, sl] * 0.5
            x_ref[q, rows:rows + 3, :] = true_ref[:, sl] * 0.5
            e.place(t, x_ref.at[q])
            e.cut[t] = jnp.where(kind == 1, 15.0, 7.5)
            x = x_ref[q]
            wx = x * weight
            terms = [wx * x[rows + c:rows + c + 1] for c in range(3)] + [wx, wx * x]
            for i, term in enumerate(terms):
                total, error = two_sum(sum_ref[0, i], term)
                sum_ref[0, i] = total
                sum_ref[1, i] += error
            sum_ref[0, 5, 0:1, :] += weight
            e.prep(t)
        return n

    n = lax.fori_loop(0, tiles // unroll, prepare, jnp.int32(0))
    for o in range(1, BAND + 1):
        for k in range(o):
            n = append(n, k, k - o, e.low + BAND + k - o, k, 1)
            n = append(n, tiles - 1 - k, tiles - 1 - k + o, tiles - 1 - k, e.high + o - 1 - k, 1)
    for k, z in enumerate((e.dummy, e.dummy, 0)):
        items[k, 0] = jnp.where(n == 0, z, items[k, 0])
    items[3, 0] = jnp.maximum(n, 1)

    blank = jnp.zeros((LANES - 80, LANES), F32)
    high, low = (jnp.concatenate([sum_ref[part, i] for i in range(5)] + [blank], axis=0).T for part in range(2))
    sums = [(high[8 * k:8 * k + 8], low[8 * k:8 * k + 8]) for k in range(16)]
    while len(sums) > 1:
        sums = [pair_add(a, b) for a, b in zip(sums[::2], sums[1::2])]
    sums = sums[0]
    for k in (4, 2, 1):
        sums = pair_add(sums, (roll(sums[0], k, 0), roll(sums[1], k, 0)))
    for part in range(2):
        moment_ref[part] = sums[part] * e.unit(0)
    moment_ref[2] = jnp.broadcast_to(sum_ref[0, 5, 0:1, :], (8, LANES))

    def twin(i):
        return 2 * i, 2 * i + 1

    half = tiles // 2
    e.begin_list("self", twin, half)
    e.run_list("self", twin, half, e.dummy)
    e.end_list("self", twin, half, e.dummy)


def cross_kernel(items, moment_ref, low_ref, high_ref, *refs, copies, tiles):
    count = len(Engine.shared)
    stat_ref, shared, x_ref, work = refs[count], refs[count + 1:2 * count + 1], refs[2 * count + 1], refs[2 * count + 2:]
    e = Engine(copies, tiles, shared, work)
    rows = 3 * copies
    e.begin_right()

    def item(i):
        return items[0, i], items[1, i], items[2, i]

    n = items[3, 0]
    for i, (ref, start) in enumerate(((low_ref, e.low), (high_ref, e.high))):
        for q in range(BAND):
            t = start + q
            x_ref[BAND * i + q] = ref[:, q * LANES:(q + 1) * LANES]
            e.place(t, x_ref.at[BAND * i + q])
            e.cut[t] = x_ref[BAND * i + q, rows + 3:rows + 4, :]
            e.prep(t)
    e.begin_list("cross", item, n)
    e.run_list("cross", item, n, e.dummy)
    e.end_list("cross", item, n, e.dummy)
    stat_ref[0] = moment_ref[0] + e.scores(moment_ref[2, 0:1, :])
    stat_ref[1] = moment_ref[1]


def solve_kernel(stat_ref, other_ref, noise_ref, loss_ref, sum_ref, m_ref, k_ref, s_ref, *, copies, atoms):
    rows = 3 * copies
    stats, error = two_sum(stat_ref[0], other_ref[0])
    low = (stat_ref[1] + other_ref[1]) + error
    for part, x in enumerate((stats, low)):
        s_ref[part] = jnp.broadcast_to(x[0:1], (LANES, LANES)).T

    def per_copy(c, q, scale):
        return tuple(s_ref[part, 16 * q + c * copies:16 * q + (c + 1) * copies, :] * scale for part in range(2))

    def shared(r, q, scale):
        return tuple(s_ref[part, 16 * q + r:16 * q + r + 1, :] * scale for part in range(2))

    def wide(x):
        return tuple(jnp.broadcast_to(v, (copies, LANES)) for v in x)

    weight_sum = jnp.broadcast_to(stats[copies + 3:copies + 4], (copies, LANES))
    count = jnp.broadcast_to(stats[copies + 2:copies + 3], (copies, LANES)) * 16.0
    score = stats[2:copies + 2] * 2.0 + 0.5 * count
    pred_sum = [wide(per_copy(c, 3, 2.0)) for c in range(3)]
    true_sum = [wide(shared(rows + c, 3, 2.0)) for c in range(3)]
    pred_mean = [pair_div(x, weight_sum) for x in pred_sum]
    true_mean = [pair_div(x, weight_sum) for x in true_sum]
    cov = [[pair_add(wide(per_copy(c, d, 4.0)), pair_neg(pair_mul(pred_sum[c], true_mean[d]))) for d in range(3)] for c in range(3)]
    ct = {}
    for d in range(3):
        for e in range(d + 1):
            ct[d, e] = pair_add(wide(shared(rows + d, e, 4.0)), pair_neg(pair_mul(true_sum[d], true_mean[e])))
    var = None
    for c in range(3):
        term = pair_add(wide(per_copy(c, 4, 4.0)), pair_neg(pair_mul(pred_sum[c], pred_mean[c])))
        var = term if var is None else pair_add(var, term)

    x = [[cov[c][d][0] for d in range(3)] for c in range(3)]
    frobenius = jnp.sqrt(sum(x[c][d] * x[c][d] for c in range(3) for d in range(3)))
    x = [[x[c][d] / frobenius for d in range(3)] for c in range(3)]

    def sweep(_, flat):
        x = [flat[0:3], flat[3:6], flat[6:9]]
        gram = {}
        for a in range(3):
            for b in range(a + 1):
                gram[a, b] = gram[b, a] = x[a][0] * x[b][0] + x[a][1] * x[b][1] + x[a][2] * x[b][2]
        return tuple(1.5 * x[a][d] - 0.5 * (gram[a, 0] * x[0][d] + gram[a, 1] * x[1][d] + gram[a, 2] * x[2][d])
                     for a in range(3) for d in range(3))

    flat = lax.fori_loop(0, SWEEPS, sweep, tuple(v for line in x for v in line))
    x = [flat[0:3], flat[3:6], flat[6:9]]

    square = var
    nothing = jnp.zeros((copies, LANES), F32)
    for c in range(3):
        for d in range(3):
            square = pair_add(square, pair_mul((-2.0 * x[c][d], nothing), cov[c][d]))
    for d in range(3):
        for e in range(d + 1):
            gram = None
            for c in range(3):
                term = two_prod(x[c][d], x[c][e])
                gram = term if gram is None else pair_add(gram, term)
            if d != e:
                gram = (2.0 * gram[0], 2.0 * gram[1])
            square = pair_add(square, pair_mul(gram, ct[d, e]))

    noise = noise_ref[...]
    loss_weight = (noise * noise + SIGMA * SIGMA) / (noise * SIGMA * (noise * SIGMA))
    mean_square = (square[0] + square[1]) / (3.0 * weight_sum)
    loss = loss_weight * mean_square + 1.0 - score / count
    for s in range(copies):
        loss_ref[s] = loss[s, 0]
    sum_ref[...] = jnp.broadcast_to(jnp.sum(loss, axis=0, keepdims=True), (8, LANES))

    grad_scale = 16.0 * atoms
    for c in range(3):
        for d in range(3):
            m_ref[3 * c + d] = x[c][d]
        m_ref[9 + c] = pred_mean[c][0]
        k_ref[c:c + 1, :] = true_mean[c][0][0:1]
    m_ref[12] = grad_scale * 2.0 * loss_weight / (3.0 * weight_sum)
    m_ref[13] = grad_scale / count


def gradient_kernel(m_ref, k_ref, pred_ref, true_ref, kind_ref, acc_ref, grad_ref, *, copies, tiles):
    for t in range(tiles):
        sl = slice(t * LANES, (t + 1) * LANES)
        kind = kind_ref[:, sl]
        weight = jnp.where(kind == 1, 5.0, jnp.where(kind == 2, 10.0, 1.0))
        centred = true_ref[:, sl] - k_ref[0:3, :]
        factor_sum = 0.5 * acc_ref[t, pl.ds(3, copies, stride=8), :]
        for c in range(3):
            target = m_ref[3 * c] * centred[0:1] + m_ref[3 * c + 1] * centred[1:2] + m_ref[3 * c + 2] * centred[2:3] + m_ref[9 + c]
            pred = pred_ref[c, :, sl]
            pull = pred * factor_sum - acc_ref[t, pl.ds(c, copies, stride=8), :]
            grad_ref[c, :, sl] = m_ref[12] * weight * (pred - target) - m_ref[13] * pull


def pack_kernel(pred_hbm, true_hbm, kind_hbm, part_hbm, noise_hbm, first_ref, last_ref, pred_ref, true_ref, kind_ref, part_ref, noise_ref, noise_smem, sems, *, copies, tiles):
    span = BAND * LANES
    moves = [
        pltpu.make_async_copy(source, target, sems.at[i])
        for i, (source, target) in enumerate(
            ((pred_hbm, pred_ref), (true_hbm, true_ref), (kind_hbm, kind_ref), (part_hbm, part_ref), (noise_hbm, noise_smem))
        )
    ]
    for move in moves:
        move.start()
    for move in moves:
        move.wait()
    for ref, start in ((first_ref, 0), (last_ref, tiles * LANES - span)):
        sl = slice(start, start + span)
        for c in range(3):
            ref[c * copies:(c + 1) * copies, :] = pred_ref[c, :, sl] * 0.5
        ref[3 * copies:3 * copies + 3, :] = true_ref[:, sl] * 0.5
        ref[3 * copies + 3:3 * copies + 4, :] = jnp.where(kind_ref[:, sl] == 1, 15.0, 7.5)
    row = lax.broadcasted_iota(jnp.int32, (copies, LANES), 0)
    noise = jnp.zeros((copies, LANES), F32)
    for s in range(copies):
        noise = jnp.where(row == s, noise_smem[s], noise)
    noise_ref[...] = noise


VMEM = pl.BlockSpec(memory_space=pltpu.VMEM)
SMEM = pl.BlockSpec(memory_space=pltpu.SMEM)
PARAMS = pltpu.CompilerParams(vmem_limit_bytes=40 * 2**20)
SMALL = pltpu.CompilerParams(vmem_limit_bytes=4 * 2**20)


def swap(x, axis, step):
    return lax.ppermute(x, axis, [(i, i ^ step) for i in range(lax.axis_size(axis))])


def shards(coords_pred, coords_true, atom_kind, partners, noise_level):
    copies, _, local = coords_pred.shape
    tiles = partners.shape[0]
    rows = 3 * copies
    size = lax.axis_size("res")
    kind = atom_kind[None]
    coords_pred = jnp.transpose(coords_pred, (1, 0, 2))
    partners = partners.T
    base = (lax.axis_index("res") * tiles)[None].astype(jnp.int32)
    stats_shape = jax.ShapeDtypeStruct((2, 8, LANES), F32)

    block = jax.ShapeDtypeStruct((rows + 4, BAND * LANES), F32)
    same = [jax.ShapeDtypeStruct(x.shape, x.dtype) for x in (coords_pred, coords_true, kind, partners)]
    first, last, coords_pred, coords_true, kind, partners, noise = pl.pallas_call(
        functools.partial(pack_kernel, copies=copies, tiles=tiles),
        in_specs=[pl.BlockSpec(memory_space=pltpu.HBM)] * 5,
        out_specs=[VMEM] * 7,
        out_shape=[block, block, *same, jax.ShapeDtypeStruct((copies, LANES), F32)],
        scratch_shapes=[pltpu.SMEM((copies,), F32), pltpu.SemaphoreType.DMA((5,))],
        compiler_params=SMALL,
        name="pack",
    )(*(pltpu.with_memory_space_constraint(x, pltpu.HBM) for x in (coords_pred, coords_true, kind, partners, noise_level)))
    forward = [(i, i + 1) for i in range(size - 1)]
    low = lax.ppermute(last, "res", forward)
    high = lax.ppermute(first, "res", [(b, a) for a, b in forward])

    shared_shapes = Engine.shared_shapes(tiles, copies)
    count = len(shared_shapes)
    x_shape = pltpu.VMEM((6, 16, LANES), F32)
    *shared, items, moments = pl.pallas_call(
        functools.partial(self_kernel, copies=copies, tiles=tiles),
        in_specs=[SMEM, SMEM] + [VMEM] * 3,
        out_specs=[VMEM] * count + [SMEM, VMEM],
        out_shape=[*shared_shapes, jax.ShapeDtypeStruct((4, LANES), jnp.int32), jax.ShapeDtypeStruct((3, 8, LANES), F32)],
        scratch_shapes=[x_shape, pltpu.VMEM((2, 6, 16, LANES), F32), pltpu.VMEM((2, LANES, LANES), BF16), *Engine.work_shapes(copies, 2)],
        compiler_params=PARAMS,
        cost_estimate=pl.CostEstimate(flops=10**8, bytes_accessed=10**6, transcendentals=10**7),
        name="self_tiles",
    )(base, partners, coords_pred, coords_true, kind)
    stats, *shared = pl.pallas_call(
        functools.partial(cross_kernel, copies=copies, tiles=tiles),
        in_specs=[SMEM] + [VMEM] * (3 + count),
        out_specs=[VMEM] * (1 + count),
        out_shape=[stats_shape, *shared_shapes],
        input_output_aliases={4 + i: 1 + i for i in range(count)},
        scratch_shapes=[x_shape, *Engine.work_shapes(copies, 1)],
        compiler_params=PARAMS,
        name="cross_tiles",
    )(items, moments, low, high, *shared)

    step = 1
    while True:
        other = swap(stats, "res", step)
        step *= 2
        if step == size:
            break
        total, error = two_sum(stats[0], other[0])
        stats = jnp.stack([total, (stats[1] + other[1]) + error])

    copy_loss, total, maps, centre = pl.pallas_call(
        functools.partial(solve_kernel, copies=copies, atoms=local * size),
        in_specs=[VMEM] * 3,
        out_specs=[SMEM] + [VMEM] * 3,
        out_shape=[
            jax.ShapeDtypeStruct((copies,), F32),
            jax.ShapeDtypeStruct((8, LANES), F32),
            jax.ShapeDtypeStruct((14, copies, LANES), F32),
            jax.ShapeDtypeStruct((8, LANES), F32),
        ],
        scratch_shapes=[pltpu.VMEM((2, LANES, LANES), F32)],
        compiler_params=SMALL,
        name="solve",
    )(stats, other, noise)
    step = 1
    while step < lax.axis_size("samp"):
        total = total + swap(total, "samp", step)
        step *= 2
    mean_loss = total[0, 0] / (copies * lax.axis_size("samp"))
    grad = pl.pallas_call(
        functools.partial(gradient_kernel, copies=copies, tiles=tiles),
        in_specs=[VMEM] * 6,
        out_specs=VMEM,
        out_shape=jax.ShapeDtypeStruct((3, copies, local), F32),
        cost_estimate=pl.CostEstimate(flops=10**6, bytes_accessed=10**6, transcendentals=0),
        compiler_params=SMALL,
        name="gradient",
    )(maps, centre, coords_pred, coords_true, kind, shared[Engine.shared.index("acc")])
    return copy_loss, mean_loss, jnp.transpose(grad, (1, 0, 2))


def solution(mesh):
    in_specs = (P("samp", None, "res"), P(None, "res"), P("res"), P("res", None), P("samp"))
    out_specs = (P("samp"), P(), P("samp", None, "res"))
    return jax.shard_map(shards, mesh=mesh, in_specs=in_specs, out_specs=out_specs, check_vma=False)
```

```python
import functools

import jax
import jax.numpy as jnp
from jax import lax
from jax.experimental import pallas as pl
from jax.experimental.pallas import tpu as pltpu
from jax.sharding import PartitionSpec as P

LANES = 128
BAND = 2
SWEEPS = 20
SIGMA = 16.0
HALF_THRESHOLDS = (0.25, 0.5, 1.0, 2.0)
EPS = 0.25e-6
F32 = jnp.float32
BF16 = jnp.bfloat16


def roll(x, shift, axis=1):
    return pltpu.roll(x, shift, axis)


def two_sum(a, b):
    s = a + b
    t = s - a
    return s, (a - (s - t)) + (b - t)


def two_prod(a, b):
    def halves(x):
        t = x * 4097.0
        h = t - (t - x)
        return h, x - h

    p = a * b
    ah, al = halves(a)
    bh, bl = halves(b)
    return p, ((ah * bh - p) + ah * bl + al * bh) + al * bl


def pair_add(x, y):
    s, e = two_sum(x[0], y[0])
    return two_sum(s, e + (x[1] + y[1]))


def pair_neg(x):
    return -x[0], -x[1]


def pair_mul(x, y):
    p, e = two_prod(x[0], y[0])
    return two_sum(p, e + (x[0] * y[1] + x[1] * y[0]))


def pair_div(x, w):
    q = x[0] / w
    p, e = two_prod(q, w)
    return two_sum(q, (((x[0] - p) - e) + x[1]) / w)


def dot(a, b):
    return jnp.dot(a, b, preferred_element_type=F32)


def dot_nt(a, b):
    return lax.dot_general(a, b, (((1,), (1,)), ((), ())), preferred_element_type=F32)


def split3(x):
    a = x.astype(BF16).astype(F32)
    rest = x - a
    b = rest.astype(BF16).astype(F32)
    return a, b, (rest - b).astype(BF16).astype(F32)


def stack(a, b, axis):
    return jnp.concatenate([a, b], axis=axis)


def spread(steps, work, ticks):
    state = [0, 0]

    def tick():
        state[0] += 1
        while state[1] < len(steps) and state[1] * ticks * 3 < state[0] * len(steps) * 4:
            steps[state[1]]()
            state[1] += 1

    work(tick)
    for step in steps[state[1]:]:
        step()


class Engine:
    shared = ("v", "cut", "centre", "left", "point", "acc", "score", "count")
    work = ("true", "weight", "minus", "right", "d", "f")

    def __init__(self, copies, tiles, shared, work):
        self.copies = copies
        self.twos = copies // 2
        self.low, self.high, self.dummy = tiles, tiles + BAND, tiles + 2 * BAND
        for name, ref in zip(self.shared + self.work, (*shared, *work)):
            setattr(self, name, ref)

    @staticmethod
    def shared_shapes(tiles, copies):
        n, twos = tiles + 2 * BAND + 1, copies // 2
        return [
            jax.ShapeDtypeStruct(shape, dtype)
            for shape, dtype in (
                ((n, copies + 1, 8, LANES), F32),
                ((n, 1, LANES), F32),
                ((n, copies + 1, 8, LANES), F32),
                ((n, twos + 1, LANES, LANES), BF16),
                ((n, twos, 64, 2 * LANES), BF16),
                ((n, copies * 8, LANES), F32),
                ((copies, 8, LANES), F32),
                ((8, LANES), F32),
            )
        ]

    @staticmethod
    def work_shapes(copies, parts):
        twos = copies // 2
        return [[pltpu.VMEM((LANES, LANES), F32)] * 2] * 3 + [
            [pltpu.VMEM((parts, twos + 1, LANES, 2 * LANES), BF16)] * 2,
            [pltpu.VMEM((parts, twos + 1, LANES, 2 * LANES), F32)] * 2,
            [pltpu.VMEM((parts, twos, 2 * LANES, 2 * LANES), BF16)] * 2,
        ]

    def begin_right(self):
        pick = jnp.where(lax.broadcasted_iota(jnp.int32, (LANES, LANES), 0) == 7, 1.0, 0.0).astype(BF16)
        blank = jnp.zeros((64, LANES), BF16)
        for ref in self.right:
            for k in range(ref.shape[0]):
                for h in range(self.twos + 1):
                    ref[k, h, 64:, :LANES] = blank
                    ref[k, h, :64, LANES:] = blank
                ref[k, self.twos, :, LANES:] = pick

    def place(self, t, ref):
        blank = jnp.zeros((5, LANES), F32)
        for s in range(self.copies):
            self.v[t, s] = stack(ref[pl.ds(s, 3, stride=self.copies), :], blank, 0)
        self.v[t, self.copies] = stack(ref[3 * self.copies:3 * self.copies + 3, :], blank, 0)

    @staticmethod
    def unit(k):
        return jnp.where(lax.broadcasted_iota(jnp.int32, (8, LANES), 0) == k, 1.0, 0.0)

    def prep(self, t):
        groups = []
        for s in range(self.copies + 1):
            v = self.v[t, s]
            centre = jnp.broadcast_to(jnp.sum(v, axis=1, keepdims=True) * (1.0 / LANES), (8, LANES))
            self.centre[t, s] = centre
            y = v - centre
            norm = jnp.sum(y * y, axis=0, keepdims=True)
            x = y + (self.unit(4) + EPS * self.unit(5)) + norm * self.unit(3)
            if s == self.copies:
                x = x + self.unit(7) * self.cut[t]
            a, b, c = split3(x)
            groups.append(jnp.concatenate([a, a, b, a, b, c, b, c], axis=0))
            if s < self.copies:
                a, b, c = split3(v + self.unit(3))
                p = jnp.concatenate([a, b, c, jnp.zeros_like(a)], axis=0).astype(BF16)
                q = 32 * (s % 2)
                self.point[t, s // 2, q:q + 32, :LANES] = p
                self.point[t, s // 2, q:q + 32, LANES:] = p
        groups.append(jnp.zeros((64, LANES), F32))
        for h in range(self.twos + 1):
            self.left[t, h] = stack(groups[2 * h], groups[2 * h + 1], 0).astype(BF16).T

    def build(self, slot, k, g, j, s):
        y = self.v[j, s] - self.centre[g, s]
        norm = jnp.sum(y * y, axis=0, keepdims=True)
        a, b, c = split3((self.unit(3) + self.unit(5)) - 2.0 * y + norm * self.unit(4))
        q, m = 64 * (s % 2), LANES * (s % 2)
        self.right[slot][k, s // 2, q:q + 64, m:m + LANES] = jnp.concatenate([a, b, a, c, b, a, c, b], axis=0).astype(BF16)

    def squares(self, slot, k, g, h):
        return dot(self.left[g, h], self.right[slot][k, h])

    def get(self, slot, h, k, lanes, shared):
        one = self.d[slot][0, h, k, lanes]
        if not shared:
            return one
        return jnp.where(self.upper(k), one, self.d[slot][1, h, k, lanes])

    @staticmethod
    def upper(k):
        shape = (k.stop - k.start, LANES)
        return lax.broadcasted_iota(jnp.int32, shape, 1) > lax.broadcasted_iota(jnp.int32, shape, 0) + k.start

    def weigh(self, slot, cuts, share, shared, tick):
        total = jnp.zeros((8, LANES), F32)
        for b in range(16):
            k = slice(8 * b, 8 * b + 8)
            d2 = jnp.maximum(self.get(slot, self.twos, k, slice(0, LANES), shared), EPS)
            dist = d2 * lax.rsqrt(d2)
            cut_j = jnp.where(self.upper(k), cuts[0], cuts[1]) if shared else cuts[0]
            cut_i = self.get(slot, self.twos, k, slice(LANES, 2 * LANES), shared)
            w = jnp.where(dist < cut_j, 0.0625, 0.0) + jnp.where(dist < cut_i, 0.0625, 0.0)
            if shared:
                row = lax.broadcasted_iota(jnp.int32, (8, LANES), 0) + 8 * b
                w = jnp.where(lax.broadcasted_iota(jnp.int32, (8, LANES), 1) == row, 0.0, w)
            self.true[slot][k, :] = dist
            self.weight[slot][k, :] = w
            self.minus[slot][k, :] = -w
            total = total + w
            tick()
        self.count[...] += total * share

    def factor(self, slot, share, shared, tick):
        for s in range(self.copies):
            h, m = s // 2, LANES * (s % 2)
            score = jnp.zeros((8, LANES), F32)
            blocks = []
            for q in range(8):
                k = slice(16 * q, 16 * q + 16)
                d2 = jnp.maximum(self.get(slot, h, k, slice(m, m + LANES), shared), EPS)
                r = lax.rsqrt(d2)
                diff = d2 * r - self.true[slot][k, :]
                spread = jnp.abs(diff)
                u = [jnp.tanh(t - spread) for t in HALF_THRESHOLDS]
                w = self.weight[slot][k, :]
                z = w * ((u[0] + u[1]) + (u[2] + u[3]))
                score = score + z[:8] + z[8:]
                slope = ((u[0] * u[0] + u[1] * u[1]) + (u[2] * u[2] + u[3] * u[3])) - 4.0
                f = slope * r * jnp.maximum(jnp.minimum(diff * 1e30, w), self.minus[slot][k, :])
                high = f.astype(BF16)
                low = (f - high.astype(F32)).astype(BF16)
                if shared:
                    blocks.append((high, low))
                else:
                    self.f[slot][0, h, k, m:m + LANES] = high
                    self.f[slot][0, h, LANES + 16 * q:LANES + 16 * q + 16, m:m + LANES] = low
                tick()
            for part, rows in enumerate(zip(*blocks)):
                whole = jnp.concatenate(rows, axis=0)
                mirror = whole.T
                for q in range(8):
                    k = slice(16 * q, 16 * q + 16)
                    upper = self.tri[0, k, :] > 0
                    start = LANES * part + 16 * q
                    self.f[slot][0, h, start:start + 16, m:m + LANES] = jnp.where(upper, whole[k], mirror[k])
                    self.f[slot][1, h, start:start + 16, m:m + LANES] = jnp.where(upper, mirror[k], whole[k])
            self.score[s] += score * share

    @staticmethod
    def fold(z):
        return [z[k:k + 8, m:m + LANES] + z[k + 8:k + 16, m:m + LANES] + z[k + 16:k + 24, m:m + LANES] for k, m in ((0, 0), (32, LANES))]

    def along_j(self, p, f):
        return self.fold(dot(p, f))

    def along_i(self, p, f):
        one = stack(f[:LANES, :LANES], f[LANES:, :LANES], 1)
        two = stack(f[:LANES, LANES:], f[LANES:, LANES:], 1)
        return self.fold(dot_nt(p, stack(one, two, 0)))

    def cross_build(self, item, slot):
        return [functools.partial(self.build, slot, 0, item[0], item[1], s) for s in range(self.copies + 1)]

    def cross_measure(self, item, slot):
        def step(h):
            self.d[slot][0, h] = self.squares(slot, 0, item[0], h)

        return [functools.partial(step, h) for h in [self.twos, *range(self.twos)]]

    def cross_factor(self, item, slot, tick):
        share = item[2].astype(F32) * 0.5
        self.weigh(slot, [self.cut[item[1]]], share, False, tick)
        self.factor(slot, share, False, tick)

    def add(self, t, h, parts):
        for q in range(2):
            self.acc[t, 8 * (2 * h + q):8 * (2 * h + q) + 8, :] += parts[q]

    def put(self, t, h, parts):
        for q in range(2):
            self.acc[t, 8 * (2 * h + q):8 * (2 * h + q) + 8, :] = parts[q]

    def cross_collect(self, item, slot):
        steps = []
        for h in range(self.twos):
            steps.append(lambda h=h: self.add(item[1], h, self.along_j(self.point[item[0], h], self.f[slot][0, h])))
            steps.append(lambda h=h: self.add(item[0], h, self.along_i(self.point[item[1], h], self.f[slot][0, h])))
        return steps

    def self_build(self, item, slot):
        return [functools.partial(self.build, slot, k, item[k], item[k], s) for s in range(self.copies + 1) for k in range(2)]

    def self_measure(self, item, slot):
        def step(h, k):
            self.d[slot][k, h] = self.squares(slot, k, item[k], h)

        return [functools.partial(step, h, k) for h in [self.twos, *range(self.twos)] for k in range(2)]

    def self_factor(self, item, slot, tick):
        self.weigh(slot, [self.cut[item[0]], self.cut[item[1]]], 1.0, True, tick)
        self.factor(slot, 1.0, True, tick)

    def self_collect(self, item, slot):
        steps = []
        for h in range(self.twos):
            for k in range(2):
                steps.append(lambda h=h, k=k: self.put(item[k], h, self.along_j(self.point[item[k], h], self.f[slot][k, h])))
        return steps

    def half(self, kind, items, slot):
        last, now, soon, later = items
        steps = getattr(self, kind + "_collect")(last, 1 - slot)
        steps += getattr(self, kind + "_measure")(soon, 1 - slot)
        steps += getattr(self, kind + "_build")(later, 1 - slot)
        spread(steps, lambda tick: getattr(self, kind + "_factor")(now, slot, tick), 16 + 8 * self.copies)

    def begin_list(self, kind, item, n):
        steps = getattr(self, kind + "_build")(item(0), 0)
        steps += getattr(self, kind + "_measure")(item(0), 0)
        for i in (1, 2):
            steps += getattr(self, kind + "_build")(item(jnp.minimum(i, n - 1)), i % 2)
        for step in steps:
            step()

    def run_list(self, kind, item, n, dummy, beside=lambda i, carry: carry, carry=0):
        def at(p):
            return tuple(jnp.where(p < 0, dummy, z) for z in item(jnp.clip(p, 0, n - 1)))

        def two(i, carry):
            p = 2 * i
            for slot in range(2):
                self.half(kind, [at(p + slot - 1), at(p + slot), at(p + slot + 1), at(p + slot + 3)], slot)
            return beside(i, carry)

        return lax.fori_loop(0, n // 2, two, carry)

    def end_list(self, kind, item, n, dummy):
        def last(i, slot):
            return getattr(self, kind + "_collect")(item(i), slot)

        def odd():
            before = tuple(jnp.where(n > 1, z, dummy) for z in item(jnp.maximum(n - 2, 0)))
            steps = getattr(self, kind + "_collect")(before, 1)
            spread(steps, lambda tick: getattr(self, kind + "_factor")(item(n - 1), 0, tick), 16 + 8 * self.copies)
            for step in last(n - 1, 0):
                step()

        def even():
            for step in last(n - 1, 1):
                step()

        if isinstance(n, int):
            (odd if n % 2 else even)()
        else:
            pl.when(n % 2 == 1)(odd)
            pl.when(n % 2 == 0)(even)

    def scores(self, weight_total):
        rows = [jnp.sum(self.score[s], axis=0, keepdims=True) for s in range(self.copies)]
        rows += [jnp.sum(self.count[...], axis=0, keepdims=True), weight_total]
        total = jnp.zeros((8, LANES), F32)
        for k, x in enumerate(rows):
            total = total + x * self.unit(2 + k)
        return jnp.broadcast_to(jnp.sum(total, axis=1, keepdims=True), (8, LANES))


def self_kernel(base_ref, part_ref, pred_ref, true_ref, kind_ref, *refs, copies, tiles):
    count = len(Engine.shared)
    shared, (items, moment_ref), (x_ref, sum_ref, tri), work = refs[:count], refs[count:count + 2], refs[count + 2:count + 5], refs[count + 5:]
    e = Engine(copies, tiles, shared, work)
    e.tri = tri
    base = base_ref[0]
    rows = 3 * copies
    e.begin_right()
    for ref in [e.score, e.count, x_ref, sum_ref, *(r.at[e.dummy] for r in shared[:5])]:
        ref[...] = jnp.zeros_like(ref)
    row = lax.broadcasted_iota(jnp.int32, (LANES, LANES), 0)
    lane = lax.broadcasted_iota(jnp.int32, (LANES, LANES), 1)
    tri[0] = jnp.where(lane > row, 1.0, 0.0).astype(BF16)

    def append(n, hit, g, j, share):
        items[0, n] = (share * 256 + g) * 256 + j
        return n + hit

    def partner_bits(t):
        bits = 0
        for k in range(1, part_ref.shape[0]):
            bits = bits | lax.shift_left(jnp.int32(1), part_ref[k, t] - (base + t - BAND))
        return lambda offset: lax.shift_right_logical(bits, BAND + offset) & 1

    def scan(i, n):
        for q in range(4):
            t = 4 * i + q
            bits = partner_bits(t)
            for o in range(1, BAND + 1):
                n = append(n, jnp.where(t >= o, bits(-o), 0), jnp.maximum(t - o, 0), t, 2)
        return n

    unroll = next(u for u in (6, 4, 3, 2, 1) if tiles % u == 0)

    @pl.loop(0, tiles // unroll)
    def _(m):
        for q in range(unroll):
            t = m * unroll + q
            sl = pl.ds(pl.multiple_of(t * LANES, LANES), LANES)
            kind = kind_ref[:, sl]
            weight = jnp.where(kind == 1, 5.0, jnp.where(kind == 2, 10.0, 1.0))
            for c in range(3):
                x_ref[q, c * copies:(c + 1) * copies, :] = pred_ref[c, :, sl] * 0.5
            x_ref[q, rows:rows + 3, :] = true_ref[:, sl] * 0.5
            e.place(t, x_ref.at[q])
            e.cut[t] = jnp.where(kind == 1, 15.0, 7.5)
            x = x_ref[q]
            wx = x * weight
            terms = [wx * x[rows + c:rows + c + 1] for c in range(3)] + [wx, wx * x]
            for i, term in enumerate(terms):
                total, error = two_sum(sum_ref[0, i], term)
                sum_ref[0, i] = total
                sum_ref[1, i] += error
            sum_ref[0, 5, 0:1, :] += weight
            e.prep(t)

    blank = jnp.zeros((LANES - 80, LANES), F32)
    high, low = (jnp.concatenate([sum_ref[part, i] for i in range(5)] + [blank], axis=0).T for part in range(2))
    sums = [(high[8 * k:8 * k + 8], low[8 * k:8 * k + 8]) for k in range(16)]
    while len(sums) > 1:
        sums = [pair_add(a, b) for a, b in zip(sums[::2], sums[1::2])]
    sums = sums[0]
    for k in (4, 2, 1):
        sums = pair_add(sums, (roll(sums[0], k, 0), roll(sums[1], k, 0)))
    for part in range(2):
        moment_ref[part] = sums[part] * e.unit(0)
    moment_ref[2] = jnp.broadcast_to(sum_ref[0, 5, 0:1, :], (8, LANES))

    def twin(i):
        return 2 * i, 2 * i + 1

    half = tiles // 2
    e.begin_list("self", twin, half)
    n = e.run_list("self", twin, half, e.dummy, scan, jnp.int32(0))
    for k in range(BAND):
        first, last = partner_bits(k), partner_bits(tiles - 1 - k)
        for o in range(k + 1, BAND + 1):
            n = append(n, first(-o), e.low + BAND + k - o, k, 1)
            n = append(n, last(o), tiles - 1 - k, e.high + o - 1 - k, 1)
    items[0, 0] = jnp.where(n == 0, e.dummy * 257, items[0, 0])
    items[1, 0] = jnp.maximum(n, 1)
    e.end_list("self", twin, half, e.dummy)


def cross_kernel(items, moment_ref, low_ref, high_ref, *refs, copies, tiles):
    count = len(Engine.shared)
    stat_ref, shared, x_ref, work = refs[count], refs[count + 1:2 * count + 1], refs[2 * count + 1], refs[2 * count + 2:]
    e = Engine(copies, tiles, shared, work)
    rows = 3 * copies
    e.begin_right()

    def item(i):
        word = items[0, i]
        return lax.shift_right_logical(word, 8) & 255, word & 255, lax.shift_right_logical(word, 16)

    n = items[1, 0]
    e.begin_list("cross", item, n)
    for i, (ref, start) in enumerate(((low_ref, e.low), (high_ref, e.high))):
        for q in range(BAND):
            t = start + q
            x_ref[BAND * i + q] = ref[:, q * LANES:(q + 1) * LANES]
            e.place(t, x_ref.at[BAND * i + q])
            e.cut[t] = x_ref[BAND * i + q, rows + 3:rows + 4, :]
            e.prep(t)
    e.run_list("cross", item, n, e.dummy)
    e.end_list("cross", item, n, e.dummy)
    stat_ref[0] = moment_ref[0] + e.scores(moment_ref[2, 0:1, :])
    stat_ref[1] = moment_ref[1]


def solve_kernel(stat_ref, other_ref, noise_ref, loss_ref, sum_ref, m_ref, k_ref, s_ref, *, copies, atoms):
    rows = 3 * copies
    stats, error = two_sum(stat_ref[0], other_ref[0])
    low = (stat_ref[1] + other_ref[1]) + error
    for part, x in enumerate((stats, low)):
        s_ref[part] = jnp.broadcast_to(x[0:1], (LANES, LANES)).T

    def per_copy(c, q, scale):
        return tuple(s_ref[part, 16 * q + c * copies:16 * q + (c + 1) * copies, :] * scale for part in range(2))

    def shared(r, q, scale):
        return tuple(s_ref[part, 16 * q + r:16 * q + r + 1, :] * scale for part in range(2))

    def wide(x):
        return tuple(jnp.broadcast_to(v, (copies, LANES)) for v in x)

    weight_sum = jnp.broadcast_to(stats[copies + 3:copies + 4], (copies, LANES))
    count = jnp.broadcast_to(stats[copies + 2:copies + 3], (copies, LANES)) * 16.0
    score = stats[2:copies + 2] * 2.0 + 0.5 * count
    pred_sum = [wide(per_copy(c, 3, 2.0)) for c in range(3)]
    true_sum = [wide(shared(rows + c, 3, 2.0)) for c in range(3)]
    pred_mean = [pair_div(x, weight_sum) for x in pred_sum]
    true_mean = [pair_div(x, weight_sum) for x in true_sum]
    cov = [[pair_add(wide(per_copy(c, d, 4.0)), pair_neg(pair_mul(pred_sum[c], true_mean[d]))) for d in range(3)] for c in range(3)]
    ct = {}
    for d in range(3):
        for e in range(d + 1):
            ct[d, e] = pair_add(wide(shared(rows + d, e, 4.0)), pair_neg(pair_mul(true_sum[d], true_mean[e])))
    var = None
    for c in range(3):
        term = pair_add(wide(per_copy(c, 4, 4.0)), pair_neg(pair_mul(pred_sum[c], pred_mean[c])))
        var = term if var is None else pair_add(var, term)

    x = [[cov[c][d][0] for d in range(3)] for c in range(3)]
    frobenius = jnp.sqrt(sum(x[c][d] * x[c][d] for c in range(3) for d in range(3)))
    x = [[x[c][d] / frobenius for d in range(3)] for c in range(3)]

    def sweep(_, flat):
        x = [flat[0:3], flat[3:6], flat[6:9]]
        gram = {}
        for a in range(3):
            for b in range(a + 1):
                gram[a, b] = gram[b, a] = x[a][0] * x[b][0] + x[a][1] * x[b][1] + x[a][2] * x[b][2]
        for a in range(3):
            for b in range(a + 1):
                gram[a, b] = gram[b, a] = (1.5 if a == b else 0.0) - 0.5 * gram[a, b]
        return tuple(gram[a, 0] * x[0][d] + gram[a, 1] * x[1][d] + gram[a, 2] * x[2][d] for a in range(3) for d in range(3))

    flat = lax.fori_loop(0, SWEEPS, sweep, tuple(v for line in x for v in line), unroll=True)
    x = [flat[0:3], flat[3:6], flat[6:9]]

    square = var
    nothing = jnp.zeros((copies, LANES), F32)
    for c in range(3):
        for d in range(3):
            square = pair_add(square, pair_mul((-2.0 * x[c][d], nothing), cov[c][d]))
    for d in range(3):
        for e in range(d + 1):
            gram = None
            for c in range(3):
                term = two_prod(x[c][d], x[c][e])
                gram = term if gram is None else pair_add(gram, term)
            if d != e:
                gram = (2.0 * gram[0], 2.0 * gram[1])
            square = pair_add(square, pair_mul(gram, ct[d, e]))

    noise = noise_ref[...]
    loss_weight = (noise * noise + SIGMA * SIGMA) / (noise * SIGMA * (noise * SIGMA))
    mean_square = (square[0] + square[1]) / (3.0 * weight_sum)
    loss = loss_weight * mean_square + 1.0 - score / count
    for s in range(copies):
        loss_ref[s] = loss[s, 0]
    sum_ref[...] = jnp.broadcast_to(jnp.sum(loss, axis=0, keepdims=True), (8, LANES))

    grad_scale = 16.0 * atoms
    for c in range(3):
        for d in range(3):
            m_ref[3 * c + d] = x[c][d]
        m_ref[9 + c] = pred_mean[c][0]
        k_ref[c:c + 1, :] = true_mean[c][0][0:1]
    m_ref[12] = grad_scale * 2.0 * loss_weight / (3.0 * weight_sum)
    m_ref[13] = grad_scale / count


def gradient_kernel(m_ref, k_ref, pred_ref, true_ref, kind_ref, acc_ref, grad_ref, *, copies, tiles):
    for t in range(tiles):
        sl = slice(t * LANES, (t + 1) * LANES)
        kind = kind_ref[:, sl]
        weight = jnp.where(kind == 1, 5.0, jnp.where(kind == 2, 10.0, 1.0))
        centred = true_ref[:, sl] - k_ref[0:3, :]
        factor_sum = 0.5 * acc_ref[t, pl.ds(3, copies, stride=8), :]
        for c in range(3):
            target = m_ref[3 * c] * centred[0:1] + m_ref[3 * c + 1] * centred[1:2] + m_ref[3 * c + 2] * centred[2:3] + m_ref[9 + c]
            pred = pred_ref[c, :, sl]
            pull = pred * factor_sum - acc_ref[t, pl.ds(c, copies, stride=8), :]
            grad_ref[c, :, sl] = m_ref[12] * weight * (pred - target) - m_ref[13] * pull


def pack_kernel(pred_hbm, true_hbm, kind_hbm, part_hbm, noise_hbm, first_ref, last_ref, pred_ref, true_ref, kind_ref, part_ref, noise_ref, noise_smem, sems, *, copies, tiles):
    span = BAND * LANES
    moves = [
        pltpu.make_async_copy(source, target, sems.at[i])
        for i, (source, target) in enumerate(
            ((pred_hbm, pred_ref), (true_hbm, true_ref), (kind_hbm, kind_ref), (part_hbm, part_ref), (noise_hbm, noise_smem))
        )
    ]
    for move in moves:
        move.start()
    for move in moves:
        move.wait()
    for ref, start in ((first_ref, 0), (last_ref, tiles * LANES - span)):
        sl = slice(start, start + span)
        for c in range(3):
            ref[c * copies:(c + 1) * copies, :] = pred_ref[c, :, sl] * 0.5
        ref[3 * copies:3 * copies + 3, :] = true_ref[:, sl] * 0.5
        ref[3 * copies + 3:3 * copies + 4, :] = jnp.where(kind_ref[:, sl] == 1, 15.0, 7.5)
    row = lax.broadcasted_iota(jnp.int32, (copies, LANES), 0)
    noise = jnp.zeros((copies, LANES), F32)
    for s in range(copies):
        noise = jnp.where(row == s, noise_smem[s], noise)
    noise_ref[...] = noise


VMEM = pl.BlockSpec(memory_space=pltpu.VMEM)
SMEM = pl.BlockSpec(memory_space=pltpu.SMEM)
PARAMS = pltpu.CompilerParams(vmem_limit_bytes=40 * 2**20)
SMALL = pltpu.CompilerParams(vmem_limit_bytes=4 * 2**20)


def swap(x, axis, step):
    return lax.ppermute(x, axis, [(i, i ^ step) for i in range(lax.axis_size(axis))])


def shards(coords_pred, coords_true, atom_kind, partners, noise_level):
    copies, _, local = coords_pred.shape
    tiles = partners.shape[0]
    rows = 3 * copies
    size = lax.axis_size("res")
    kind = atom_kind[None]
    coords_pred = jnp.transpose(coords_pred, (1, 0, 2))
    partners = partners.T
    base = (lax.axis_index("res") * tiles)[None].astype(jnp.int32)
    stats_shape = jax.ShapeDtypeStruct((2, 8, LANES), F32)

    block = jax.ShapeDtypeStruct((rows + 4, BAND * LANES), F32)
    same = [jax.ShapeDtypeStruct(x.shape, x.dtype) for x in (coords_pred, coords_true, kind, partners)]
    first, last, coords_pred, coords_true, kind, partners, noise = pl.pallas_call(
        functools.partial(pack_kernel, copies=copies, tiles=tiles),
        in_specs=[pl.BlockSpec(memory_space=pltpu.HBM)] * 5,
        out_specs=[VMEM] * 7,
        out_shape=[block, block, *same, jax.ShapeDtypeStruct((copies, LANES), F32)],
        scratch_shapes=[pltpu.SMEM((copies,), F32), pltpu.SemaphoreType.DMA((5,))],
        compiler_params=SMALL,
        name="pack",
    )(*(pltpu.with_memory_space_constraint(x, pltpu.HBM) for x in (coords_pred, coords_true, kind, partners, noise_level)))
    forward = [(i, i + 1) for i in range(size - 1)]
    low = lax.ppermute(last, "res", forward)
    high = lax.ppermute(first, "res", [(b, a) for a, b in forward])

    shared_shapes = Engine.shared_shapes(tiles, copies)
    count = len(shared_shapes)
    x_shape = pltpu.VMEM((6, 16, LANES), F32)
    *shared, items, moments = pl.pallas_call(
        functools.partial(self_kernel, copies=copies, tiles=tiles),
        in_specs=[SMEM, SMEM] + [VMEM] * 3,
        out_specs=[VMEM] * count + [SMEM, VMEM],
        out_shape=[*shared_shapes, jax.ShapeDtypeStruct((2, LANES), jnp.int32), jax.ShapeDtypeStruct((3, 8, LANES), F32)],
        scratch_shapes=[x_shape, pltpu.VMEM((2, 6, 16, LANES), F32), pltpu.VMEM((1, LANES, LANES), BF16), *Engine.work_shapes(copies, 2)],
        compiler_params=PARAMS,
        cost_estimate=pl.CostEstimate(flops=10**8, bytes_accessed=10**6, transcendentals=10**7),
        name="self_tiles",
    )(base, partners, coords_pred, coords_true, kind)
    stats, *shared = pl.pallas_call(
        functools.partial(cross_kernel, copies=copies, tiles=tiles),
        in_specs=[SMEM] + [VMEM] * (3 + count),
        out_specs=[VMEM] * (1 + count),
        out_shape=[stats_shape, *shared_shapes],
        input_output_aliases={4 + i: 1 + i for i in range(count)},
        scratch_shapes=[x_shape, *Engine.work_shapes(copies, 1)],
        compiler_params=PARAMS,
        name="cross_tiles",
    )(items, moments, low, high, *shared)

    step = 1
    while True:
        other = swap(stats, "res", step)
        step *= 2
        if step == size:
            break
        total, error = two_sum(stats[0], other[0])
        stats = jnp.stack([total, (stats[1] + other[1]) + error])

    copy_loss, total, maps, centre = pl.pallas_call(
        functools.partial(solve_kernel, copies=copies, atoms=local * size),
        in_specs=[VMEM] * 3,
        out_specs=[SMEM] + [VMEM] * 3,
        out_shape=[
            jax.ShapeDtypeStruct((copies,), F32),
            jax.ShapeDtypeStruct((8, LANES), F32),
            jax.ShapeDtypeStruct((14, copies, LANES), F32),
            jax.ShapeDtypeStruct((8, LANES), F32),
        ],
        scratch_shapes=[pltpu.VMEM((2, LANES, LANES), F32)],
        compiler_params=SMALL,
        name="solve",
    )(stats, other, noise)
    step = 1
    while step < lax.axis_size("samp"):
        total = total + swap(total, "samp", step)
        step *= 2
    mean_loss = total[0, 0] / (copies * lax.axis_size("samp"))
    grad = pl.pallas_call(
        functools.partial(gradient_kernel, copies=copies, tiles=tiles),
        in_specs=[VMEM] * 6,
        out_specs=VMEM,
        out_shape=jax.ShapeDtypeStruct((3, copies, local), F32),
        cost_estimate=pl.CostEstimate(flops=10**6, bytes_accessed=10**6, transcendentals=0),
        compiler_params=SMALL,
        name="gradient",
    )(maps, centre, coords_pred, coords_true, kind, shared[Engine.shared.index("acc")])
    return copy_loss, mean_loss, jnp.transpose(grad, (1, 0, 2))


def solution(mesh):
    in_specs = (P("samp", None, "res"), P(None, "res"), P("res"), P("res", None), P("samp"))
    out_specs = (P("samp"), P(), P("samp", None, "res"))
    return jax.shard_map(shards, mesh=mesh, in_specs=in_specs, out_specs=out_specs, check_vma=False)
```

```python
import functools

import jax
import jax.numpy as jnp
from jax import lax
from jax.experimental import pallas as pl
from jax.experimental.pallas import tpu as pltpu
from jax.sharding import PartitionSpec as P

LANES = 128
BAND = 2
SWEEPS = 20
SIGMA = 16.0
HALF_THRESHOLDS = (0.25, 0.5, 1.0, 2.0)
EPS = 0.25e-6
F32 = jnp.float32
BF16 = jnp.bfloat16


def roll(x, shift, axis=1):
    return pltpu.roll(x, shift, axis)


def two_sum(a, b):
    s = a + b
    t = s - a
    return s, (a - (s - t)) + (b - t)


def two_prod(a, b):
    def halves(x):
        t = x * 4097.0
        h = t - (t - x)
        return h, x - h

    p = a * b
    ah, al = halves(a)
    bh, bl = halves(b)
    return p, ((ah * bh - p) + ah * bl + al * bh) + al * bl


def pair_add(x, y):
    s, e = two_sum(x[0], y[0])
    return two_sum(s, e + (x[1] + y[1]))


def pair_neg(x):
    return -x[0], -x[1]


def pair_mul(x, y):
    p, e = two_prod(x[0], y[0])
    return two_sum(p, e + (x[0] * y[1] + x[1] * y[0]))


def pair_div(x, w):
    q = x[0] / w
    p, e = two_prod(q, w)
    return two_sum(q, (((x[0] - p) - e) + x[1]) / w)


def dot(a, b):
    return jnp.dot(a, b, preferred_element_type=F32)


def dot_nt(a, b):
    return lax.dot_general(a, b, (((1,), (1,)), ((), ())), preferred_element_type=F32)


def split3(x):
    a = x.astype(BF16).astype(F32)
    rest = x - a
    b = rest.astype(BF16).astype(F32)
    return a, b, (rest - b).astype(BF16).astype(F32)


def stack(a, b, axis):
    return jnp.concatenate([a, b], axis=axis)


def spread(steps, work, ticks):
    state = [0, 0]

    def tick():
        state[0] += 1
        while state[1] < len(steps) and state[1] * ticks * 3 < state[0] * len(steps) * 4:
            steps[state[1]]()
            state[1] += 1

    work(tick)
    for step in steps[state[1]:]:
        step()


class Engine:
    shared = ("v", "cut", "centre", "left", "point", "acc", "score", "count")
    work = ("true", "weight", "minus", "right", "d", "f")

    def __init__(self, copies, tiles, shared, work):
        self.copies = copies
        self.twos = copies // 2
        self.low, self.high, self.dummy = tiles, tiles + BAND, tiles + 2 * BAND
        for name, ref in zip(self.shared + self.work, (*shared, *work)):
            setattr(self, name, ref)

    @staticmethod
    def shared_shapes(tiles, copies):
        n, twos = tiles + 2 * BAND + 1, copies // 2
        return [
            jax.ShapeDtypeStruct(shape, dtype)
            for shape, dtype in (
                ((n, copies + 1, 8, LANES), F32),
                ((n, 1, LANES), F32),
                ((n, copies + 1, 8, LANES), F32),
                ((n, twos + 1, LANES, LANES), BF16),
                ((n, twos, 64, 2 * LANES), BF16),
                ((n, copies * 8, LANES), F32),
                ((copies, 8, LANES), F32),
                ((8, LANES), F32),
            )
        ]

    @staticmethod
    def work_shapes(copies, parts):
        twos = copies // 2
        return [[pltpu.VMEM((LANES, LANES), F32)] * 2] * 3 + [
            [pltpu.VMEM((parts, twos + 1, LANES, 2 * LANES), BF16)] * 2,
            [pltpu.VMEM((parts, twos + 1, LANES, 2 * LANES), F32)] * 2,
            [pltpu.VMEM((parts, twos, 2 * LANES, 2 * LANES), BF16)] * 2,
        ]

    def begin_right(self):
        pick = jnp.where(lax.broadcasted_iota(jnp.int32, (LANES, LANES), 0) == 7, 1.0, 0.0).astype(BF16)
        blank = jnp.zeros((64, LANES), BF16)
        for ref in self.right:
            for k in range(ref.shape[0]):
                for h in range(self.twos + 1):
                    ref[k, h, 64:, :LANES] = blank
                    ref[k, h, :64, LANES:] = blank
                ref[k, self.twos, :, LANES:] = pick

    def place(self, t, ref):
        blank = jnp.zeros((5, LANES), F32)
        for s in range(self.copies):
            self.v[t, s] = stack(ref[pl.ds(s, 3, stride=self.copies), :], blank, 0)
        self.v[t, self.copies] = stack(ref[3 * self.copies:3 * self.copies + 3, :], blank, 0)

    @staticmethod
    def unit(k):
        return jnp.where(lax.broadcasted_iota(jnp.int32, (8, LANES), 0) == k, 1.0, 0.0)

    def prep(self, t):
        groups = []
        for s in range(self.copies + 1):
            v = self.v[t, s]
            centre = jnp.broadcast_to(jnp.sum(v, axis=1, keepdims=True) * (1.0 / LANES), (8, LANES))
            self.centre[t, s] = centre
            y = v - centre
            norm = jnp.sum(y * y, axis=0, keepdims=True)
            x = y + (self.unit(4) + EPS * self.unit(5)) + norm * self.unit(3)
            if s == self.copies:
                x = x + self.unit(7) * self.cut[t]
            a, b, c = split3(x)
            groups.append(jnp.concatenate([a, a, b, a, b, c, b, c], axis=0))
            if s < self.copies:
                a, b, c = split3(v + self.unit(3))
                p = jnp.concatenate([a, b, c, jnp.zeros_like(a)], axis=0).astype(BF16)
                q = 32 * (s % 2)
                self.point[t, s // 2, q:q + 32, :LANES] = p
                self.point[t, s // 2, q:q + 32, LANES:] = p
        groups.append(jnp.zeros((64, LANES), F32))
        for h in range(self.twos + 1):
            self.left[t, h] = stack(groups[2 * h], groups[2 * h + 1], 0).astype(BF16).T

    def build(self, slot, k, g, j, s):
        y = self.v[j, s] - self.centre[g, s]
        norm = jnp.sum(y * y, axis=0, keepdims=True)
        a, b, c = split3((self.unit(3) + self.unit(5)) - 2.0 * y + norm * self.unit(4))
        q, m = 64 * (s % 2), LANES * (s % 2)
        self.right[slot][k, s // 2, q:q + 64, m:m + LANES] = jnp.concatenate([a, b, a, c, b, a, c, b], axis=0).astype(BF16)

    def squares(self, slot, k, g, h):
        return dot(self.left[g, h], self.right[slot][k, h])

    def get(self, slot, h, k, lanes, shared):
        one = self.d[slot][0, h, k, lanes]
        if not shared:
            return one
        return jnp.where(self.upper(k), one, self.d[slot][1, h, k, lanes])

    @staticmethod
    def upper(k):
        shape = (k.stop - k.start, LANES)
        return lax.broadcasted_iota(jnp.int32, shape, 1) > lax.broadcasted_iota(jnp.int32, shape, 0) + k.start

    def weigh(self, slot, cuts, share, shared, tick):
        total = jnp.zeros((8, LANES), F32)
        for b in range(16):
            k = slice(8 * b, 8 * b + 8)
            d2 = jnp.maximum(self.get(slot, self.twos, k, slice(0, LANES), shared), EPS)
            dist = d2 * lax.rsqrt(d2)
            cut_j = jnp.where(self.upper(k), cuts[0], cuts[1]) if shared else cuts[0]
            cut_i = self.get(slot, self.twos, k, slice(LANES, 2 * LANES), shared)
            w = jnp.where(dist < cut_j, 0.0625, 0.0) + jnp.where(dist < cut_i, 0.0625, 0.0)
            if shared:
                row = lax.broadcasted_iota(jnp.int32, (8, LANES), 0) + 8 * b
                w = jnp.where(lax.broadcasted_iota(jnp.int32, (8, LANES), 1) == row, 0.0, w)
            self.true[slot][k, :] = dist
            self.weight[slot][k, :] = w
            self.minus[slot][k, :] = -w
            total = total + w
            tick()
        self.count[...] += total * share

    def factor(self, slot, share, shared, tick):
        for s in range(self.copies):
            h, m = s // 2, LANES * (s % 2)
            score = jnp.zeros((8, LANES), F32)
            blocks = []
            for q in range(8):
                k = slice(16 * q, 16 * q + 16)
                d2 = jnp.maximum(self.get(slot, h, k, slice(m, m + LANES), shared), EPS)
                r = lax.rsqrt(d2)
                diff = d2 * r - self.true[slot][k, :]
                spread = jnp.abs(diff)
                u = [jnp.tanh(t - spread) for t in HALF_THRESHOLDS]
                w = self.weight[slot][k, :]
                z = w * ((u[0] + u[1]) + (u[2] + u[3]))
                score = score + z[:8] + z[8:]
                slope = ((u[0] * u[0] + u[1] * u[1]) + (u[2] * u[2] + u[3] * u[3])) - 4.0
                f = slope * r * jnp.maximum(jnp.minimum(diff * 1e30, w), self.minus[slot][k, :])
                high = f.astype(BF16)
                low = (f - high.astype(F32)).astype(BF16)
                if shared:
                    blocks.append((high, low))
                else:
                    self.f[slot][0, h, k, m:m + LANES] = high
                    self.f[slot][0, h, LANES + 16 * q:LANES + 16 * q + 16, m:m + LANES] = low
                tick()
            for part, rows in enumerate(zip(*blocks)):
                whole = jnp.concatenate(rows, axis=0)
                mirror = whole.T
                for q in range(8):
                    k = slice(16 * q, 16 * q + 16)
                    upper = self.tri[0, k, :] > 0
                    start = LANES * part + 16 * q
                    self.f[slot][0, h, start:start + 16, m:m + LANES] = jnp.where(upper, whole[k], mirror[k])
                    self.f[slot][1, h, start:start + 16, m:m + LANES] = jnp.where(upper, mirror[k], whole[k])
            self.score[s] += score * share

    @staticmethod
    def fold(z):
        return [z[k:k + 8, m:m + LANES] + z[k + 8:k + 16, m:m + LANES] + z[k + 16:k + 24, m:m + LANES] for k, m in ((0, 0), (32, LANES))]

    def along_j(self, p, f):
        return self.fold(dot(p, f))

    def along_i(self, p, f):
        one = stack(f[:LANES, :LANES], f[LANES:, :LANES], 1)
        two = stack(f[:LANES, LANES:], f[LANES:, LANES:], 1)
        return self.fold(dot_nt(p, stack(one, two, 0)))

    def cross_build(self, item, slot):
        return [functools.partial(self.build, slot, 0, item[0], item[1], s) for s in range(self.copies + 1)]

    def cross_measure(self, item, slot):
        def step(h):
            self.d[slot][0, h] = self.squares(slot, 0, item[0], h)

        return [functools.partial(step, h) for h in [self.twos, *range(self.twos)]]

    def cross_factor(self, item, slot, tick):
        share = item[2].astype(F32) * 0.5
        self.weigh(slot, [self.cut[item[1]]], share, False, tick)
        self.factor(slot, share, False, tick)

    def add(self, t, h, parts):
        for q in range(2):
            self.acc[t, 8 * (2 * h + q):8 * (2 * h + q) + 8, :] += parts[q]

    def put(self, t, h, parts):
        for q in range(2):
            self.acc[t, 8 * (2 * h + q):8 * (2 * h + q) + 8, :] = parts[q]

    def cross_collect(self, item, slot):
        steps = []
        for h in range(self.twos):
            steps.append(lambda h=h: self.add(item[1], h, self.along_j(self.point[item[0], h], self.f[slot][0, h])))
            steps.append(lambda h=h: self.add(item[0], h, self.along_i(self.point[item[1], h], self.f[slot][0, h])))
        return steps

    def self_build(self, item, slot):
        return [functools.partial(self.build, slot, k, item[k], item[k], s) for s in range(self.copies + 1) for k in range(2)]

    def self_measure(self, item, slot):
        def step(h, k):
            self.d[slot][k, h] = self.squares(slot, k, item[k], h)

        return [functools.partial(step, h, k) for h in [self.twos, *range(self.twos)] for k in range(2)]

    def self_factor(self, item, slot, tick):
        self.weigh(slot, [self.cut[item[0]], self.cut[item[1]]], 1.0, True, tick)
        self.factor(slot, 1.0, True, tick)

    def self_collect(self, item, slot):
        steps = []
        for h in range(self.twos):
            for k in range(2):
                steps.append(lambda h=h, k=k: self.put(item[k], h, self.along_j(self.point[item[k], h], self.f[slot][k, h])))
        return steps

    def half(self, kind, items, slot):
        last, now, soon, later = items
        steps = getattr(self, kind + "_collect")(last, 1 - slot)
        steps += getattr(self, kind + "_measure")(soon, 1 - slot)
        steps += getattr(self, kind + "_build")(later, 1 - slot)
        spread(steps, lambda tick: getattr(self, kind + "_factor")(now, slot, tick), 16 + 8 * self.copies)

    def begin_list(self, kind, item, n):
        steps = getattr(self, kind + "_build")(item(0), 0)
        steps += getattr(self, kind + "_measure")(item(0), 0)
        for i in (1, 2):
            steps += getattr(self, kind + "_build")(item(jnp.minimum(i, n - 1)), i % 2)
        for step in steps:
            step()

    def run_list(self, kind, item, n, dummy):
        def at(p):
            return tuple(jnp.where(p < 0, dummy, z) for z in item(jnp.clip(p, 0, n - 1)))

        @pl.loop(0, n // 2)
        def _(i):
            p = 2 * i
            for slot in range(2):
                self.half(kind, [at(p + slot - 1), at(p + slot), at(p + slot + 1), at(p + slot + 3)], slot)

    def end_list(self, kind, item, n, dummy):
        def last(i, slot):
            return getattr(self, kind + "_collect")(item(i), slot)

        def odd():
            before = tuple(jnp.where(n > 1, z, dummy) for z in item(jnp.maximum(n - 2, 0)))
            steps = getattr(self, kind + "_collect")(before, 1)
            spread(steps, lambda tick: getattr(self, kind + "_factor")(item(n - 1), 0, tick), 16 + 8 * self.copies)
            for step in last(n - 1, 0):
                step()

        def even():
            for step in last(n - 1, 1):
                step()

        if isinstance(n, int):
            (odd if n % 2 else even)()
        else:
            pl.when(n % 2 == 1)(odd)
            pl.when(n % 2 == 0)(even)

    def scores(self, weight_total):
        rows = [jnp.sum(self.score[s], axis=0, keepdims=True) for s in range(self.copies)]
        rows += [jnp.sum(self.count[...], axis=0, keepdims=True), weight_total]
        total = jnp.zeros((8, LANES), F32)
        for k, x in enumerate(rows):
            total = total + x * self.unit(2 + k)
        return jnp.broadcast_to(jnp.sum(total, axis=1, keepdims=True), (8, LANES))


def self_kernel(base_ref, part_ref, pred_ref, true_ref, kind_ref, *refs, copies, tiles):
    count = len(Engine.shared)
    shared, (items, moment_ref), (x_ref, sum_ref, tri), work = refs[:count], refs[count:count + 2], refs[count + 2:count + 5], refs[count + 5:]
    e = Engine(copies, tiles, shared, work)
    e.tri = tri
    base = base_ref[0]
    rows = 3 * copies
    e.begin_right()
    for ref in [e.score, e.count, x_ref, sum_ref, *(r.at[e.dummy] for r in shared[:5])]:
        ref[...] = jnp.zeros_like(ref)
    row = lax.broadcasted_iota(jnp.int32, (LANES, LANES), 0)
    lane = lax.broadcasted_iota(jnp.int32, (LANES, LANES), 1)
    tri[0] = jnp.where(lane > row, 1.0, 0.0).astype(BF16)

    place = lax.broadcasted_iota(jnp.int32, (1, LANES), 1)

    def append(state, hit, g, j, share):
        n, row = state
        return n + hit, jnp.where(place == n, (share * 256 + g) * 256 + j, row)

    def partner_bits(t):
        bits = 0
        for k in range(1, part_ref.shape[0]):
            bits = bits | lax.shift_left(jnp.int32(1), (part_ref[k, t] - base) - (t - BAND))
        return lambda offset: lax.shift_right_logical(bits, BAND + offset) & 1

    unroll = next(u for u in (6, 4, 3, 2, 1) if tiles % u == 0)

    @pl.loop(0, tiles // unroll)
    def _(m):
        for q in range(unroll):
            t = m * unroll + q
            sl = pl.ds(pl.multiple_of(t * LANES, LANES), LANES)
            kind = kind_ref[:, sl]
            weight = jnp.where(kind == 1, 5.0, jnp.where(kind == 2, 10.0, 1.0))
            for c in range(3):
                x_ref[q, c * copies:(c + 1) * copies, :] = pred_ref[c, :, sl] * 0.5
            x_ref[q, rows:rows + 3, :] = true_ref[:, sl] * 0.5
            e.place(t, x_ref.at[q])
            e.cut[t] = jnp.where(kind == 1, 15.0, 7.5)
            x = x_ref[q]
            wx = x * weight
            terms = [wx * x[rows + c:rows + c + 1] for c in range(3)] + [wx, wx * x]
            for i, term in enumerate(terms):
                total, error = two_sum(sum_ref[0, i], term)
                sum_ref[0, i] = total
                sum_ref[1, i] += error
            sum_ref[0, 5, 0:1, :] += weight
            e.prep(t)

    blank = jnp.zeros((LANES - 80, LANES), F32)
    high, low = (jnp.concatenate([sum_ref[part, i] for i in range(5)] + [blank], axis=0).T for part in range(2))
    sums = [(high[8 * k:8 * k + 8], low[8 * k:8 * k + 8]) for k in range(16)]
    while len(sums) > 1:
        sums = [pair_add(a, b) for a, b in zip(sums[::2], sums[1::2])]
    sums = sums[0]
    for k in (4, 2, 1):
        sums = pair_add(sums, (roll(sums[0], k, 0), roll(sums[1], k, 0)))
    for part in range(2):
        moment_ref[part] = sums[part] * e.unit(0)
    moment_ref[2] = jnp.broadcast_to(sum_ref[0, 5, 0:1, :], (8, LANES))

    def twin(i):
        return 2 * i, 2 * i + 1

    half = tiles // 2
    e.begin_list("self", twin, half)
    e.run_list("self", twin, half, e.dummy)

    state = jnp.int32(0), jnp.zeros((1, LANES), jnp.int32)
    edges = []
    for t in range(tiles):
        bits = partner_bits(t)
        for o in range(1, BAND + 1):
            if t >= o:
                state = append(state, bits(-o), t - o, t, 2)
            else:
                edges.append((bits(-o), e.low + BAND + t - o, t, 1))
            if t + o >= tiles:
                edges.append((bits(o), t, e.high + t + o - tiles, 1))
    for edge in edges:
        state = append(state, *edge)
    n, row = state
    row = jnp.where((place == 0) & (n == 0), e.dummy * 257, row)
    items[...] = jnp.where(place == LANES - 1, jnp.maximum(n, 1), row)
    e.end_list("self", twin, half, e.dummy)


def cross_kernel(items, moment_ref, low_ref, high_ref, *refs, copies, tiles):
    count = len(Engine.shared)
    stat_ref, shared, x_ref, work = refs[count], refs[count + 1:2 * count + 1], refs[2 * count + 1], refs[2 * count + 2:]
    e = Engine(copies, tiles, shared, work)
    rows = 3 * copies
    e.begin_right()

    def item(i):
        word = items[0, i]
        return lax.shift_right_logical(word, 8) & 255, word & 255, lax.shift_right_logical(word, 16)

    n = items[0, LANES - 1]
    e.begin_list("cross", item, n)
    for i, (ref, start) in enumerate(((low_ref, e.low), (high_ref, e.high))):
        for q in range(BAND):
            t = start + q
            x_ref[BAND * i + q] = ref[:, q * LANES:(q + 1) * LANES]
            e.place(t, x_ref.at[BAND * i + q])
            e.cut[t] = x_ref[BAND * i + q, rows + 3:rows + 4, :]
            e.prep(t)
    e.run_list("cross", item, n, e.dummy)
    e.end_list("cross", item, n, e.dummy)
    stat_ref[0] = moment_ref[0] + e.scores(moment_ref[2, 0:1, :])
    stat_ref[1] = moment_ref[1]


def solve_kernel(stat_ref, other_ref, noise_ref, loss_ref, sum_ref, m_ref, k_ref, s_ref, *, copies, atoms):
    rows = 3 * copies
    stats, error = two_sum(stat_ref[0], other_ref[0])
    low = (stat_ref[1] + other_ref[1]) + error
    for part, x in enumerate((stats, low)):
        s_ref[part] = jnp.broadcast_to(x[0:1], (LANES, LANES)).T

    def per_copy(c, q, scale):
        return tuple(s_ref[part, 16 * q + c * copies:16 * q + (c + 1) * copies, :] * scale for part in range(2))

    def shared(r, q, scale):
        return tuple(s_ref[part, 16 * q + r:16 * q + r + 1, :] * scale for part in range(2))

    def wide(x):
        return tuple(jnp.broadcast_to(v, (copies, LANES)) for v in x)

    weight_sum = jnp.broadcast_to(stats[copies + 3:copies + 4], (copies, LANES))
    count = jnp.broadcast_to(stats[copies + 2:copies + 3], (copies, LANES)) * 16.0
    score = stats[2:copies + 2] * 2.0 + 0.5 * count
    pred_sum = [wide(per_copy(c, 3, 2.0)) for c in range(3)]
    true_sum = [wide(shared(rows + c, 3, 2.0)) for c in range(3)]
    pred_mean = [pair_div(x, weight_sum) for x in pred_sum]
    true_mean = [pair_div(x, weight_sum) for x in true_sum]
    cov = [[pair_add(wide(per_copy(c, d, 4.0)), pair_neg(pair_mul(pred_sum[c], true_mean[d]))) for d in range(3)] for c in range(3)]
    ct = {}
    for d in range(3):
        for e in range(d + 1):
            ct[d, e] = pair_add(wide(shared(rows + d, e, 4.0)), pair_neg(pair_mul(true_sum[d], true_mean[e])))
    var = None
    for c in range(3):
        term = pair_add(wide(per_copy(c, 4, 4.0)), pair_neg(pair_mul(pred_sum[c], pred_mean[c])))
        var = term if var is None else pair_add(var, term)

    x = [[cov[c][d][0] for d in range(3)] for c in range(3)]
    frobenius = jnp.sqrt(sum(x[c][d] * x[c][d] for c in range(3) for d in range(3)))
    x = [[x[c][d] / frobenius for d in range(3)] for c in range(3)]

    def sweep(_, flat):
        x = [flat[0:3], flat[3:6], flat[6:9]]
        gram = {}
        for a in range(3):
            for b in range(a + 1):
                gram[a, b] = gram[b, a] = x[a][0] * x[b][0] + x[a][1] * x[b][1] + x[a][2] * x[b][2]
        for a in range(3):
            for b in range(a + 1):
                gram[a, b] = gram[b, a] = (1.5 if a == b else 0.0) - 0.5 * gram[a, b]
        return tuple(gram[a, 0] * x[0][d] + gram[a, 1] * x[1][d] + gram[a, 2] * x[2][d] for a in range(3) for d in range(3))

    flat = lax.fori_loop(0, SWEEPS, sweep, tuple(v for line in x for v in line), unroll=True)
    x = [flat[0:3], flat[3:6], flat[6:9]]

    square = var
    nothing = jnp.zeros((copies, LANES), F32)
    for c in range(3):
        for d in range(3):
            square = pair_add(square, pair_mul((-2.0 * x[c][d], nothing), cov[c][d]))
    for d in range(3):
        for e in range(d + 1):
            gram = None
            for c in range(3):
                term = two_prod(x[c][d], x[c][e])
                gram = term if gram is None else pair_add(gram, term)
            if d != e:
                gram = (2.0 * gram[0], 2.0 * gram[1])
            square = pair_add(square, pair_mul(gram, ct[d, e]))

    noise = noise_ref[...]
    loss_weight = (noise * noise + SIGMA * SIGMA) / (noise * SIGMA * (noise * SIGMA))
    mean_square = (square[0] + square[1]) / (3.0 * weight_sum)
    loss = loss_weight * mean_square + 1.0 - score / count
    for s in range(copies):
        loss_ref[s] = loss[s, 0]
    sum_ref[...] = jnp.broadcast_to(jnp.sum(loss, axis=0, keepdims=True), (8, LANES))

    grad_scale = 16.0 * atoms
    for c in range(3):
        for d in range(3):
            m_ref[3 * c + d] = x[c][d]
        m_ref[9 + c] = pred_mean[c][0]
        k_ref[c:c + 1, :] = true_mean[c][0][0:1]
    m_ref[12] = grad_scale * 2.0 * loss_weight / (3.0 * weight_sum)
    m_ref[13] = grad_scale / count


def gradient_kernel(m_ref, k_ref, pred_ref, true_ref, kind_ref, acc_ref, grad_ref, *, copies, tiles):
    for t in range(tiles):
        sl = slice(t * LANES, (t + 1) * LANES)
        kind = kind_ref[:, sl]
        weight = jnp.where(kind == 1, 5.0, jnp.where(kind == 2, 10.0, 1.0))
        centred = true_ref[:, sl] - k_ref[0:3, :]
        factor_sum = 0.5 * acc_ref[t, pl.ds(3, copies, stride=8), :]
        for c in range(3):
            target = m_ref[3 * c] * centred[0:1] + m_ref[3 * c + 1] * centred[1:2] + m_ref[3 * c + 2] * centred[2:3] + m_ref[9 + c]
            pred = pred_ref[c, :, sl]
            pull = pred * factor_sum - acc_ref[t, pl.ds(c, copies, stride=8), :]
            grad_ref[c, :, sl] = m_ref[12] * weight * (pred - target) - m_ref[13] * pull


def pack_kernel(pred_hbm, true_hbm, kind_hbm, part_hbm, noise_hbm, first_ref, last_ref, pred_ref, true_ref, kind_ref, part_ref, noise_ref, noise_smem, sems, *, copies, tiles):
    span = BAND * LANES
    moves = [
        pltpu.make_async_copy(source, target, sems.at[i])
        for i, (source, target) in enumerate(
            ((pred_hbm, pred_ref), (true_hbm, true_ref), (kind_hbm, kind_ref), (part_hbm, part_ref), (noise_hbm, noise_smem))
        )
    ]
    for move in moves:
        move.start()
    for move in moves:
        move.wait()
    for ref, start in ((first_ref, 0), (last_ref, tiles * LANES - span)):
        sl = slice(start, start + span)
        for c in range(3):
            ref[c * copies:(c + 1) * copies, :] = pred_ref[c, :, sl] * 0.5
        ref[3 * copies:3 * copies + 3, :] = true_ref[:, sl] * 0.5
        ref[3 * copies + 3:3 * copies + 4, :] = jnp.where(kind_ref[:, sl] == 1, 15.0, 7.5)
    row = lax.broadcasted_iota(jnp.int32, (copies, LANES), 0)
    noise = jnp.zeros((copies, LANES), F32)
    for s in range(copies):
        noise = jnp.where(row == s, noise_smem[s], noise)
    noise_ref[...] = noise


VMEM = pl.BlockSpec(memory_space=pltpu.VMEM)
SMEM = pl.BlockSpec(memory_space=pltpu.SMEM)
PARAMS = pltpu.CompilerParams(vmem_limit_bytes=40 * 2**20)
SMALL = pltpu.CompilerParams(vmem_limit_bytes=4 * 2**20)


def swap(x, axis, step):
    return lax.ppermute(x, axis, [(i, i ^ step) for i in range(lax.axis_size(axis))])


def shards(coords_pred, coords_true, atom_kind, partners, noise_level):
    copies, _, local = coords_pred.shape
    tiles = partners.shape[0]
    rows = 3 * copies
    size = lax.axis_size("res")
    kind = atom_kind[None]
    coords_pred = jnp.transpose(coords_pred, (1, 0, 2))
    partners = partners.T
    base = (lax.axis_index("res") * tiles)[None].astype(jnp.int32)
    stats_shape = jax.ShapeDtypeStruct((2, 8, LANES), F32)

    block = jax.ShapeDtypeStruct((rows + 4, BAND * LANES), F32)
    same = [jax.ShapeDtypeStruct(x.shape, x.dtype) for x in (coords_pred, coords_true, kind, partners)]
    first, last, coords_pred, coords_true, kind, partners, noise = pl.pallas_call(
        functools.partial(pack_kernel, copies=copies, tiles=tiles),
        in_specs=[pl.BlockSpec(memory_space=pltpu.HBM)] * 5,
        out_specs=[VMEM] * 7,
        out_shape=[block, block, *same, jax.ShapeDtypeStruct((copies, LANES), F32)],
        scratch_shapes=[pltpu.SMEM((copies,), F32), pltpu.SemaphoreType.DMA((5,))],
        compiler_params=SMALL,
        name="pack",
    )(*(pltpu.with_memory_space_constraint(x, pltpu.HBM) for x in (coords_pred, coords_true, kind, partners, noise_level)))
    forward = [(i, i + 1) for i in range(size - 1)]
    low = lax.ppermute(last, "res", forward)
    high = lax.ppermute(first, "res", [(b, a) for a, b in forward])

    shared_shapes = Engine.shared_shapes(tiles, copies)
    count = len(shared_shapes)
    x_shape = pltpu.VMEM((6, 16, LANES), F32)
    *shared, items, moments = pl.pallas_call(
        functools.partial(self_kernel, copies=copies, tiles=tiles),
        in_specs=[SMEM, SMEM] + [VMEM] * 3,
        out_specs=[VMEM] * (count + 2),
        out_shape=[*shared_shapes, jax.ShapeDtypeStruct((1, LANES), jnp.int32), jax.ShapeDtypeStruct((3, 8, LANES), F32)],
        scratch_shapes=[x_shape, pltpu.VMEM((2, 6, 16, LANES), F32), pltpu.VMEM((1, LANES, LANES), BF16), *Engine.work_shapes(copies, 2)],
        compiler_params=PARAMS,
        cost_estimate=pl.CostEstimate(flops=10**8, bytes_accessed=10**6, transcendentals=10**7),
        name="self_tiles",
    )(base, partners, coords_pred, coords_true, kind)
    stats, *shared = pl.pallas_call(
        functools.partial(cross_kernel, copies=copies, tiles=tiles),
        in_specs=[SMEM] + [VMEM] * (3 + count),
        out_specs=[VMEM] * (1 + count),
        out_shape=[stats_shape, *shared_shapes],
        input_output_aliases={4 + i: 1 + i for i in range(count)},
        scratch_shapes=[x_shape, *Engine.work_shapes(copies, 1)],
        compiler_params=PARAMS,
        name="cross_tiles",
    )(items, moments, low, high, *shared)

    step = 1
    while True:
        other = swap(stats, "res", step)
        step *= 2
        if step == size:
            break
        total, error = two_sum(stats[0], other[0])
        stats = jnp.stack([total, (stats[1] + other[1]) + error])

    copy_loss, total, maps, centre = pl.pallas_call(
        functools.partial(solve_kernel, copies=copies, atoms=local * size),
        in_specs=[VMEM] * 3,
        out_specs=[SMEM] + [VMEM] * 3,
        out_shape=[
            jax.ShapeDtypeStruct((copies,), F32),
            jax.ShapeDtypeStruct((8, LANES), F32),
            jax.ShapeDtypeStruct((14, copies, LANES), F32),
            jax.ShapeDtypeStruct((8, LANES), F32),
        ],
        scratch_shapes=[pltpu.VMEM((2, LANES, LANES), F32)],
        compiler_params=SMALL,
        name="solve",
    )(stats, other, noise)
    step = 1
    while step < lax.axis_size("samp"):
        total = total + swap(total, "samp", step)
        step *= 2
    mean_loss = total[0, 0] / (copies * lax.axis_size("samp"))
    grad = pl.pallas_call(
        functools.partial(gradient_kernel, copies=copies, tiles=tiles),
        in_specs=[VMEM] * 6,
        out_specs=VMEM,
        out_shape=jax.ShapeDtypeStruct((3, copies, local), F32),
        cost_estimate=pl.CostEstimate(flops=10**6, bytes_accessed=10**6, transcendentals=0),
        compiler_params=SMALL,
        name="gradient",
    )(maps, centre, coords_pred, coords_true, kind, shared[Engine.shared.index("acc")])
    return copy_loss, mean_loss, jnp.transpose(grad, (1, 0, 2))


def solution(mesh):
    in_specs = (P("samp", None, "res"), P(None, "res"), P("res"), P("res", None), P("samp"))
    out_specs = (P("samp"), P(), P("samp", None, "res"))
    return jax.shard_map(shards, mesh=mesh, in_specs=in_specs, out_specs=out_specs, check_vma=False)
```

```python
import functools

import jax
import jax.numpy as jnp
from jax import lax
from jax.experimental import pallas as pl
from jax.experimental.pallas import tpu as pltpu
from jax.sharding import PartitionSpec as P

LANES = 128
BAND = 2
SWEEPS = 20
SIGMA = 16.0
HALF_THRESHOLDS = (0.25, 0.5, 1.0, 2.0)
EPS = 0.25e-6
F32 = jnp.float32
BF16 = jnp.bfloat16


def roll(x, shift, axis=1):
    return pltpu.roll(x, shift, axis)


def two_sum(a, b):
    s = a + b
    t = s - a
    return s, (a - (s - t)) + (b - t)


def two_prod(a, b):
    def halves(x):
        t = x * 4097.0
        h = t - (t - x)
        return h, x - h

    p = a * b
    ah, al = halves(a)
    bh, bl = halves(b)
    return p, ((ah * bh - p) + ah * bl + al * bh) + al * bl


def pair_add(x, y):
    s, e = two_sum(x[0], y[0])
    return two_sum(s, e + (x[1] + y[1]))


def pair_neg(x):
    return -x[0], -x[1]


def pair_mul(x, y):
    p, e = two_prod(x[0], y[0])
    return two_sum(p, e + (x[0] * y[1] + x[1] * y[0]))


def pair_div(x, w):
    q = x[0] / w
    p, e = two_prod(q, w)
    return two_sum(q, (((x[0] - p) - e) + x[1]) / w)


def dot(a, b):
    return jnp.dot(a, b, preferred_element_type=F32)


def dot_nt(a, b):
    return lax.dot_general(a, b, (((1,), (1,)), ((), ())), preferred_element_type=F32)


def split3(x):
    a = x.astype(BF16).astype(F32)
    rest = x - a
    b = rest.astype(BF16).astype(F32)
    return a, b, (rest - b).astype(BF16).astype(F32)


def stack(a, b, axis):
    return jnp.concatenate([a, b], axis=axis)


def spread(steps, work, ticks):
    state = [0, 0]

    def tick():
        state[0] += 1
        while state[1] < len(steps) and state[1] * ticks * 3 < state[0] * len(steps) * 4:
            steps[state[1]]()
            state[1] += 1

    work(tick)
    for step in steps[state[1]:]:
        step()


class Engine:
    shared = ("v", "cut", "centre", "left", "point", "acc", "score", "count")
    work = ("true", "weight", "minus", "right", "d", "f")

    def __init__(self, copies, tiles, shared, work):
        self.copies = copies
        self.twos = copies // 2
        self.low, self.high, self.dummy = tiles, tiles + BAND, tiles + 2 * BAND
        for name, ref in zip(self.shared + self.work, (*shared, *work)):
            setattr(self, name, ref)

    @staticmethod
    def shared_shapes(tiles, copies):
        n, twos = tiles + 2 * BAND + 1, copies // 2
        return [
            jax.ShapeDtypeStruct(shape, dtype)
            for shape, dtype in (
                ((n, copies + 1, 8, LANES), F32),
                ((n, 1, LANES), F32),
                ((n, copies + 1, 8, LANES), F32),
                ((n, twos + 1, LANES, LANES), BF16),
                ((n, twos, 64, 2 * LANES), BF16),
                ((n, copies * 8, LANES), F32),
                ((copies, 8, LANES), F32),
                ((8, LANES), F32),
            )
        ]

    @staticmethod
    def work_shapes(copies, parts):
        twos = copies // 2
        return [[pltpu.VMEM((LANES, LANES), F32)] * 2] * 3 + [
            [pltpu.VMEM((parts, twos + 1, LANES, 2 * LANES), BF16)] * 2,
            [pltpu.VMEM((parts, twos + 1, LANES, 2 * LANES), F32)] * 2,
            [pltpu.VMEM((parts, twos, 2 * LANES, 2 * LANES), BF16)] * 2,
        ]

    def begin_right(self):
        pick = jnp.where(lax.broadcasted_iota(jnp.int32, (LANES, LANES), 0) == 7, 1.0, 0.0).astype(BF16)
        blank = jnp.zeros((64, LANES), BF16)
        for ref in self.right:
            for k in range(ref.shape[0]):
                for h in range(self.twos + 1):
                    ref[k, h, 64:, :LANES] = blank
                    ref[k, h, :64, LANES:] = blank
                ref[k, self.twos, :, LANES:] = pick

    def place(self, t, ref):
        blank = jnp.zeros((5, LANES), F32)
        for s in range(self.copies):
            self.v[t, s] = stack(ref[pl.ds(s, 3, stride=self.copies), :], blank, 0)
        self.v[t, self.copies] = stack(ref[3 * self.copies:3 * self.copies + 3, :], blank, 0)

    @staticmethod
    def unit(k):
        return jnp.where(lax.broadcasted_iota(jnp.int32, (8, LANES), 0) == k, 1.0, 0.0)

    def prep(self, t):
        groups = []
        for s in range(self.copies + 1):
            v = self.v[t, s]
            centre = jnp.broadcast_to(jnp.sum(v, axis=1, keepdims=True) * (1.0 / LANES), (8, LANES))
            self.centre[t, s] = centre
            y = v - centre
            norm = jnp.sum(y * y, axis=0, keepdims=True)
            x = y + (self.unit(4) + EPS * self.unit(5)) + norm * self.unit(3)
            if s == self.copies:
                x = x + self.unit(7) * self.cut[t]
            a, b, c = split3(x)
            groups.append(jnp.concatenate([a, a, b, a, b, c, b, c], axis=0))
            if s < self.copies:
                a, b, c = split3(v + self.unit(3))
                p = jnp.concatenate([a, b, c, jnp.zeros_like(a)], axis=0).astype(BF16)
                q = 32 * (s % 2)
                self.point[t, s // 2, q:q + 32, :LANES] = p
                self.point[t, s // 2, q:q + 32, LANES:] = p
        groups.append(jnp.zeros((64, LANES), F32))
        for h in range(self.twos + 1):
            self.left[t, h] = stack(groups[2 * h], groups[2 * h + 1], 0).astype(BF16).T

    def build(self, slot, k, g, j, s):
        y = self.v[j, s] - self.centre[g, s]
        norm = jnp.sum(y * y, axis=0, keepdims=True)
        a, b, c = split3((self.unit(3) + self.unit(5)) - 2.0 * y + norm * self.unit(4))
        q, m = 64 * (s % 2), LANES * (s % 2)
        self.right[slot][k, s // 2, q:q + 64, m:m + LANES] = jnp.concatenate([a, b, a, c, b, a, c, b], axis=0).astype(BF16)

    def squares(self, slot, k, g, h):
        return dot(self.left[g, h], self.right[slot][k, h])

    def get(self, slot, h, k, lanes, shared):
        one = self.d[slot][0, h, k, lanes]
        if not shared:
            return one
        return jnp.where(self.upper(k), one, self.d[slot][1, h, k, lanes])

    @staticmethod
    def upper(k):
        shape = (k.stop - k.start, LANES)
        return lax.broadcasted_iota(jnp.int32, shape, 1) > lax.broadcasted_iota(jnp.int32, shape, 0) + k.start

    def weigh(self, slot, cuts, share, shared, tick):
        total = jnp.zeros((8, LANES), F32)
        for b in range(16):
            k = slice(8 * b, 8 * b + 8)
            d2 = jnp.maximum(self.get(slot, self.twos, k, slice(0, LANES), shared), EPS)
            dist = d2 * lax.rsqrt(d2)
            cut_j = jnp.where(self.upper(k), cuts[0], cuts[1]) if shared else cuts[0]
            cut_i = self.get(slot, self.twos, k, slice(LANES, 2 * LANES), shared)
            w = jnp.where(dist < cut_j, 0.0625, 0.0) + jnp.where(dist < cut_i, 0.0625, 0.0)
            if shared:
                row = lax.broadcasted_iota(jnp.int32, (8, LANES), 0) + 8 * b
                w = jnp.where(lax.broadcasted_iota(jnp.int32, (8, LANES), 1) == row, 0.0, w)
            self.true[slot][k, :] = dist
            self.weight[slot][k, :] = w
            self.minus[slot][k, :] = -w
            total = total + w
            tick()
        self.count[...] += total * share

    def factor(self, slot, share, shared, tick):
        for s in range(self.copies):
            h, m = s // 2, LANES * (s % 2)
            score = jnp.zeros((8, LANES), F32)
            blocks = []
            for q in range(8):
                k = slice(16 * q, 16 * q + 16)
                d2 = jnp.maximum(self.get(slot, h, k, slice(m, m + LANES), shared), EPS)
                r = lax.rsqrt(d2)
                diff = d2 * r - self.true[slot][k, :]
                spread = jnp.abs(diff)
                u = [jnp.tanh(t - spread) for t in HALF_THRESHOLDS]
                w = self.weight[slot][k, :]
                z = w * ((u[0] + u[1]) + (u[2] + u[3]))
                score = score + z[:8] + z[8:]
                slope = ((u[0] * u[0] + u[1] * u[1]) + (u[2] * u[2] + u[3] * u[3])) - 4.0
                f = slope * r * jnp.maximum(jnp.minimum(diff * 1e30, w), self.minus[slot][k, :])
                high = f.astype(BF16)
                low = (f - high.astype(F32)).astype(BF16)
                if shared:
                    blocks.append((high, low))
                else:
                    self.f[slot][0, h, k, m:m + LANES] = high
                    self.f[slot][0, h, LANES + 16 * q:LANES + 16 * q + 16, m:m + LANES] = low
                tick()
            for part, rows in enumerate(zip(*blocks)):
                whole = jnp.concatenate(rows, axis=0)
                mirror = whole.T
                for q in range(8):
                    k = slice(16 * q, 16 * q + 16)
                    upper = self.tri[0, k, :] > 0
                    start = LANES * part + 16 * q
                    self.f[slot][0, h, start:start + 16, m:m + LANES] = jnp.where(upper, whole[k], mirror[k])
                    self.f[slot][1, h, start:start + 16, m:m + LANES] = jnp.where(upper, mirror[k], whole[k])
            self.score[s] += score * share

    @staticmethod
    def fold(z):
        return [z[k:k + 8, m:m + LANES] + z[k + 8:k + 16, m:m + LANES] + z[k + 16:k + 24, m:m + LANES] for k, m in ((0, 0), (32, LANES))]

    def along_j(self, p, f):
        return self.fold(dot(p, f))

    def along_i(self, p, f):
        one = stack(f[:LANES, :LANES], f[LANES:, :LANES], 1)
        two = stack(f[:LANES, LANES:], f[LANES:, LANES:], 1)
        return self.fold(dot_nt(p, stack(one, two, 0)))

    def cross_build(self, item, slot):
        return [functools.partial(self.build, slot, 0, item[0], item[1], s) for s in range(self.copies + 1)]

    def cross_measure(self, item, slot):
        def step(h):
            self.d[slot][0, h] = self.squares(slot, 0, item[0], h)

        return [functools.partial(step, h) for h in [self.twos, *range(self.twos)]]

    def cross_factor(self, item, slot, tick):
        share = item[2].astype(F32) * 0.5
        self.weigh(slot, [self.cut[item[1]]], share, False, tick)
        self.factor(slot, share, False, tick)

    def add(self, t, h, parts):
        for q in range(2):
            self.acc[t, 8 * (2 * h + q):8 * (2 * h + q) + 8, :] += parts[q]

    def put(self, t, h, parts):
        for q in range(2):
            self.acc[t, 8 * (2 * h + q):8 * (2 * h + q) + 8, :] = parts[q]

    def cross_collect(self, item, slot):
        steps = []
        for h in range(self.twos):
            steps.append(lambda h=h: self.add(item[1], h, self.along_j(self.point[item[0], h], self.f[slot][0, h])))
            steps.append(lambda h=h: self.add(item[0], h, self.along_i(self.point[item[1], h], self.f[slot][0, h])))
        return steps

    def self_build(self, item, slot):
        return [functools.partial(self.build, slot, k, item[k], item[k], s) for s in range(self.copies + 1) for k in range(2)]

    def self_measure(self, item, slot):
        def step(h, k):
            self.d[slot][k, h] = self.squares(slot, k, item[k], h)

        return [functools.partial(step, h, k) for h in [self.twos, *range(self.twos)] for k in range(2)]

    def self_factor(self, item, slot, tick):
        self.weigh(slot, [self.cut[item[0]], self.cut[item[1]]], 1.0, True, tick)
        self.factor(slot, 1.0, True, tick)

    def self_collect(self, item, slot):
        steps = []
        for h in range(self.twos):
            for k in range(2):
                steps.append(lambda h=h, k=k: self.put(item[k], h, self.along_j(self.point[item[k], h], self.f[slot][k, h])))
        return steps

    def half(self, kind, items, slot):
        last, now, soon, later = items
        steps = getattr(self, kind + "_collect")(last, 1 - slot)
        steps += getattr(self, kind + "_measure")(soon, 1 - slot)
        steps += getattr(self, kind + "_build")(later, 1 - slot)
        spread(steps, lambda tick: getattr(self, kind + "_factor")(now, slot, tick), 16 + 8 * self.copies)

    def begin_list(self, kind, item, n):
        steps = getattr(self, kind + "_build")(item(0), 0)
        steps += getattr(self, kind + "_measure")(item(0), 0)
        for i in (1, 2):
            steps += getattr(self, kind + "_build")(item(jnp.minimum(i, n - 1)), i % 2)
        for step in steps:
            step()

    def run_list(self, kind, item, n, dummy):
        def at(p):
            return tuple(jnp.where(p < 0, dummy, z) for z in item(jnp.clip(p, 0, n - 1)))

        @pl.loop(0, n // 2)
        def _(i):
            p = 2 * i
            for slot in range(2):
                self.half(kind, [at(p + slot - 1), at(p + slot), at(p + slot + 1), at(p + slot + 3)], slot)

    def end_list(self, kind, item, n, dummy):
        def last(i, slot):
            return getattr(self, kind + "_collect")(item(i), slot)

        def odd():
            before = tuple(jnp.where(n > 1, z, dummy) for z in item(jnp.maximum(n - 2, 0)))
            steps = getattr(self, kind + "_collect")(before, 1)
            spread(steps, lambda tick: getattr(self, kind + "_factor")(item(n - 1), 0, tick), 16 + 8 * self.copies)
            for step in last(n - 1, 0):
                step()

        def even():
            for step in last(n - 1, 1):
                step()

        if isinstance(n, int):
            (odd if n % 2 else even)()
        else:
            pl.when(n % 2 == 1)(odd)
            pl.when(n % 2 == 0)(even)

    def scores(self, weight_total):
        rows = [jnp.sum(self.score[s], axis=0, keepdims=True) for s in range(self.copies)]
        rows += [jnp.sum(self.count[...], axis=0, keepdims=True), weight_total]
        total = jnp.zeros((8, LANES), F32)
        for k, x in enumerate(rows):
            total = total + x * self.unit(2 + k)
        return jnp.broadcast_to(jnp.sum(total, axis=1, keepdims=True), (8, LANES))


def self_kernel(base_ref, part_ref, pred_ref, true_ref, kind_ref, *refs, copies, tiles):
    count = len(Engine.shared)
    shared, (items, moment_ref), (x_ref, sum_ref, tri), work = refs[:count], refs[count:count + 2], refs[count + 2:count + 5], refs[count + 5:]
    e = Engine(copies, tiles, shared, work)
    e.tri = tri
    base = base_ref[0]
    rows = 3 * copies
    e.begin_right()
    for ref in [e.score, e.count, x_ref, sum_ref, *(r.at[e.dummy] for r in shared[:5])]:
        ref[...] = jnp.zeros_like(ref)
    row = lax.broadcasted_iota(jnp.int32, (LANES, LANES), 0)
    lane = lax.broadcasted_iota(jnp.int32, (LANES, LANES), 1)
    tri[0] = jnp.where(lane > row, 1.0, 0.0).astype(BF16)

    place = lax.broadcasted_iota(jnp.int32, (1, LANES), 1)

    def append(state, hit, g, j, share):
        n, row = state
        return n + hit, jnp.where(place == n, (share * 256 + g) * 256 + j, row)

    def partner_bits(t):
        bits = 0
        for k in range(1, part_ref.shape[0]):
            bits = bits | lax.shift_left(jnp.int32(1), (part_ref[k, t] - base) - (t - BAND))
        return lambda offset: lax.shift_right_logical(bits, BAND + offset) & 1

    unroll = next(u for u in (6, 4, 3, 2, 1) if tiles % u == 0)

    @pl.loop(0, tiles // unroll)
    def _(m):
        for q in range(unroll):
            t = m * unroll + q
            sl = pl.ds(pl.multiple_of(t * LANES, LANES), LANES)
            kind = kind_ref[:, sl]
            weight = jnp.where(kind == 1, 5.0, jnp.where(kind == 2, 10.0, 1.0))
            for c in range(3):
                x_ref[q, c * copies:(c + 1) * copies, :] = pred_ref[c, :, sl] * 0.5
            x_ref[q, rows:rows + 3, :] = true_ref[:, sl] * 0.5
            e.place(t, x_ref.at[q])
            e.cut[t] = jnp.where(kind == 1, 15.0, 7.5)
            x = x_ref[q]
            wx = x * weight
            terms = [wx * x[rows + c:rows + c + 1] for c in range(3)] + [wx, wx * x]
            for i, term in enumerate(terms):
                total, error = two_sum(sum_ref[0, i], term)
                sum_ref[0, i] = total
                sum_ref[1, i] += error
            sum_ref[0, 5, 0:1, :] += weight
            e.prep(t)

    blank = jnp.zeros((LANES - 80, LANES), F32)
    high, low = (jnp.concatenate([sum_ref[part, i] for i in range(5)] + [blank], axis=0).T for part in range(2))
    sums = [(high[8 * k:8 * k + 8], low[8 * k:8 * k + 8]) for k in range(16)]
    while len(sums) > 1:
        sums = [pair_add(a, b) for a, b in zip(sums[::2], sums[1::2])]
    sums = sums[0]
    for k in (4, 2, 1):
        sums = pair_add(sums, (roll(sums[0], k, 0), roll(sums[1], k, 0)))
    for part in range(2):
        moment_ref[part] = sums[part] * e.unit(0)
    moment_ref[2] = jnp.broadcast_to(sum_ref[0, 5, 0:1, :], (8, LANES))

    def twin(i):
        return 2 * i, 2 * i + 1

    half = tiles // 2
    e.begin_list("self", twin, half)
    e.run_list("self", twin, half, e.dummy)

    state = jnp.int32(0), jnp.zeros((1, LANES), jnp.int32)
    edges = []
    for t in range(tiles):
        bits = partner_bits(t)
        for o in range(1, BAND + 1):
            if t >= o:
                state = append(state, bits(-o), t - o, t, 2)
            else:
                edges.append((bits(-o), e.low + BAND + t - o, t, 1))
            if t + o >= tiles:
                edges.append((bits(o), t, e.high + t + o - tiles, 1))
    for edge in edges:
        state = append(state, *edge)
    n, row = state
    row = jnp.where((place == 0) & (n == 0), e.dummy * 257, row)
    items[...] = jnp.where(place == LANES - 1, jnp.maximum(n, 1), row)
    e.end_list("self", twin, half, e.dummy)


def cross_kernel(items, moment_ref, low_ref, high_ref, *refs, copies, tiles):
    count = len(Engine.shared)
    stat_ref, shared, x_ref, work = refs[count], refs[count + 1:2 * count + 1], refs[2 * count + 1], refs[2 * count + 2:]
    e = Engine(copies, tiles, shared, work)
    rows = 3 * copies
    e.begin_right()

    def item(i):
        word = items[0, i]
        return lax.shift_right_logical(word, 8) & 255, word & 255, lax.shift_right_logical(word, 16)

    n = items[0, LANES - 1]
    e.begin_list("cross", item, n)
    for i, (ref, start) in enumerate(((low_ref, e.low), (high_ref, e.high))):
        for q in range(BAND):
            t = start + q
            x_ref[BAND * i + q] = ref[:, q * LANES:(q + 1) * LANES]
            e.place(t, x_ref.at[BAND * i + q])
            e.cut[t] = x_ref[BAND * i + q, rows + 3:rows + 4, :]
            e.prep(t)
    e.run_list("cross", item, n, e.dummy)
    e.end_list("cross", item, n, e.dummy)
    stat_ref[0] = moment_ref[0] + e.scores(moment_ref[2, 0:1, :])
    stat_ref[1] = moment_ref[1]


def solve_kernel(stat_ref, other_ref, noise_ref, loss_ref, sum_ref, m_ref, k_ref, s_ref, *, copies, atoms):
    rows = 3 * copies
    stats, error = two_sum(stat_ref[0], other_ref[0])
    low = (stat_ref[1] + other_ref[1]) + error
    for part, x in enumerate((stats, low)):
        s_ref[part] = jnp.broadcast_to(x[0:1], (LANES, LANES)).T

    def per_copy(c, q, scale):
        return tuple(s_ref[part, 16 * q + c * copies:16 * q + (c + 1) * copies, :] * scale for part in range(2))

    def shared(r, q, scale):
        return tuple(s_ref[part, 16 * q + r:16 * q + r + 1, :] * scale for part in range(2))

    def wide(x):
        return tuple(jnp.broadcast_to(v, (copies, LANES)) for v in x)

    weight_sum = jnp.broadcast_to(stats[copies + 3:copies + 4], (copies, LANES))
    count = jnp.broadcast_to(stats[copies + 2:copies + 3], (copies, LANES)) * 16.0
    score = stats[2:copies + 2] * 2.0 + 0.5 * count
    pred_sum = [wide(per_copy(c, 3, 2.0)) for c in range(3)]
    true_sum = [wide(shared(rows + c, 3, 2.0)) for c in range(3)]
    pred_mean = [pair_div(x, weight_sum) for x in pred_sum]
    true_mean = [pair_div(x, weight_sum) for x in true_sum]
    cov = [[pair_add(wide(per_copy(c, d, 4.0)), pair_neg(pair_mul(pred_sum[c], true_mean[d]))) for d in range(3)] for c in range(3)]
    ct = {}
    for d in range(3):
        for e in range(d + 1):
            ct[d, e] = pair_add(wide(shared(rows + d, e, 4.0)), pair_neg(pair_mul(true_sum[d], true_mean[e])))
    var = None
    for c in range(3):
        term = pair_add(wide(per_copy(c, 4, 4.0)), pair_neg(pair_mul(pred_sum[c], pred_mean[c])))
        var = term if var is None else pair_add(var, term)

    x = [[cov[c][d][0] for d in range(3)] for c in range(3)]
    frobenius = jnp.sqrt(sum(x[c][d] * x[c][d] for c in range(3) for d in range(3)))
    x = [[x[c][d] / frobenius for d in range(3)] for c in range(3)]

    def sweep(_, flat):
        x = [flat[0:3], flat[3:6], flat[6:9]]
        gram = {}
        for a in range(3):
            for b in range(a + 1):
                gram[a, b] = gram[b, a] = x[a][0] * x[b][0] + x[a][1] * x[b][1] + x[a][2] * x[b][2]
        for a in range(3):
            for b in range(a + 1):
                gram[a, b] = gram[b, a] = (1.5 if a == b else 0.0) - 0.5 * gram[a, b]
        return tuple(gram[a, 0] * x[0][d] + gram[a, 1] * x[1][d] + gram[a, 2] * x[2][d] for a in range(3) for d in range(3))

    flat = lax.fori_loop(0, SWEEPS, sweep, tuple(v for line in x for v in line), unroll=True)
    x = [flat[0:3], flat[3:6], flat[6:9]]

    square = var
    nothing = jnp.zeros((copies, LANES), F32)
    for c in range(3):
        for d in range(3):
            square = pair_add(square, pair_mul((-2.0 * x[c][d], nothing), cov[c][d]))
    for d in range(3):
        for e in range(d + 1):
            gram = None
            for c in range(3):
                term = two_prod(x[c][d], x[c][e])
                gram = term if gram is None else pair_add(gram, term)
            if d != e:
                gram = (2.0 * gram[0], 2.0 * gram[1])
            square = pair_add(square, pair_mul(gram, ct[d, e]))

    noise = noise_ref[...]
    loss_weight = (noise * noise + SIGMA * SIGMA) / (noise * SIGMA * (noise * SIGMA))
    mean_square = (square[0] + square[1]) / (3.0 * weight_sum)
    loss = loss_weight * mean_square + 1.0 - score / count
    for s in range(copies):
        loss_ref[s] = loss[s, 0]
    sum_ref[...] = jnp.broadcast_to(jnp.sum(loss, axis=0, keepdims=True), (8, LANES))

    grad_scale = 16.0 * atoms
    for c in range(3):
        for d in range(3):
            m_ref[3 * c + d] = x[c][d]
        m_ref[9 + c] = pred_mean[c][0]
    k_ref[...] = sum(true_mean[c][0][0:1] * Engine.unit(c) for c in range(3))
    m_ref[12] = grad_scale * 2.0 * loss_weight / (3.0 * weight_sum)
    m_ref[13] = grad_scale / count


def gradient_kernel(m_ref, k_ref, pred_ref, true_ref, kind_ref, acc_ref, grad_ref, *, copies, tiles):
    for t in range(tiles):
        sl = slice(t * LANES, (t + 1) * LANES)
        kind = kind_ref[:, sl]
        weight = jnp.where(kind == 1, 5.0, jnp.where(kind == 2, 10.0, 1.0))
        centred = true_ref[:, sl] - k_ref[0:3, :]
        factor_sum = 0.5 * acc_ref[t, pl.ds(3, copies, stride=8), :]
        for c in range(3):
            target = m_ref[3 * c] * centred[0:1] + m_ref[3 * c + 1] * centred[1:2] + m_ref[3 * c + 2] * centred[2:3] + m_ref[9 + c]
            pred = pred_ref[c, :, sl]
            pull = pred * factor_sum - acc_ref[t, pl.ds(c, copies, stride=8), :]
            grad_ref[c, :, sl] = m_ref[12] * weight * (pred - target) - m_ref[13] * pull


def pack_kernel(pred_hbm, true_hbm, kind_hbm, part_hbm, noise_hbm, first_ref, last_ref, pred_ref, true_ref, kind_ref, part_ref, noise_ref, noise_smem, sems, *, copies, tiles):
    span = BAND * LANES
    moves = [
        pltpu.make_async_copy(source, target, sems.at[i])
        for i, (source, target) in enumerate(
            ((pred_hbm, pred_ref), (true_hbm, true_ref), (kind_hbm, kind_ref), (part_hbm, part_ref), (noise_hbm, noise_smem))
        )
    ]
    for move in moves:
        move.start()
    for move in moves:
        move.wait()
    for ref, start in ((first_ref, 0), (last_ref, tiles * LANES - span)):
        sl = slice(start, start + span)
        cut = jnp.where(kind_ref[:, sl] == 1, 15.0, 7.5)
        ref[...] = jnp.concatenate([pred_ref[c, :, sl] * 0.5 for c in range(3)] + [true_ref[:, sl] * 0.5, cut], axis=0)
    row = lax.broadcasted_iota(jnp.int32, (copies, LANES), 0)
    noise = jnp.zeros((copies, LANES), F32)
    for s in range(copies):
        noise = jnp.where(row == s, noise_smem[s], noise)
    noise_ref[...] = noise


VMEM = pl.BlockSpec(memory_space=pltpu.VMEM)
SMEM = pl.BlockSpec(memory_space=pltpu.SMEM)
PARAMS = pltpu.CompilerParams(vmem_limit_bytes=40 * 2**20)
SMALL = pltpu.CompilerParams(vmem_limit_bytes=4 * 2**20)


def swap(x, axis, step):
    return lax.ppermute(x, axis, [(i, i ^ step) for i in range(lax.axis_size(axis))])


def shards(coords_pred, coords_true, atom_kind, partners, noise_level):
    copies, _, local = coords_pred.shape
    tiles = partners.shape[0]
    rows = 3 * copies
    size = lax.axis_size("res")
    kind = atom_kind[None]
    coords_pred = jnp.transpose(coords_pred, (1, 0, 2))
    partners = partners.T
    base = (lax.axis_index("res") * tiles)[None].astype(jnp.int32)
    stats_shape = jax.ShapeDtypeStruct((2, 8, LANES), F32)

    block = jax.ShapeDtypeStruct((rows + 4, BAND * LANES), F32)
    same = [jax.ShapeDtypeStruct(x.shape, x.dtype) for x in (coords_pred, coords_true, kind, partners)]
    first, last, coords_pred, coords_true, kind, partners, noise = pl.pallas_call(
        functools.partial(pack_kernel, copies=copies, tiles=tiles),
        in_specs=[pl.BlockSpec(memory_space=pltpu.HBM)] * 5,
        out_specs=[VMEM] * 7,
        out_shape=[block, block, *same, jax.ShapeDtypeStruct((copies, LANES), F32)],
        scratch_shapes=[pltpu.SMEM((copies,), F32), pltpu.SemaphoreType.DMA((5,))],
        compiler_params=SMALL,
        name="pack",
    )(*(pltpu.with_memory_space_constraint(x, pltpu.HBM) for x in (coords_pred, coords_true, kind, partners, noise_level)))
    forward = [(i, i + 1) for i in range(size - 1)]
    low = lax.ppermute(last, "res", forward)
    high = lax.ppermute(first, "res", [(b, a) for a, b in forward])

    shared_shapes = Engine.shared_shapes(tiles, copies)
    count = len(shared_shapes)
    x_shape = pltpu.VMEM((8, 16, LANES), F32)
    *shared, items, moments = pl.pallas_call(
        functools.partial(self_kernel, copies=copies, tiles=tiles),
        in_specs=[SMEM, SMEM] + [VMEM] * 3,
        out_specs=[VMEM] * (count + 2),
        out_shape=[*shared_shapes, jax.ShapeDtypeStruct((1, LANES), jnp.int32), jax.ShapeDtypeStruct((3, 8, LANES), F32)],
        scratch_shapes=[x_shape, pltpu.VMEM((2, 6, 16, LANES), F32), pltpu.VMEM((1, LANES, LANES), BF16), *Engine.work_shapes(copies, 2)],
        compiler_params=PARAMS,
        cost_estimate=pl.CostEstimate(flops=10**8, bytes_accessed=10**6, transcendentals=10**7),
        name="self_tiles",
    )(base, partners, coords_pred, coords_true, kind)
    stats, *shared = pl.pallas_call(
        functools.partial(cross_kernel, copies=copies, tiles=tiles),
        in_specs=[SMEM] + [VMEM] * (3 + count),
        out_specs=[VMEM] * (1 + count),
        out_shape=[stats_shape, *shared_shapes],
        input_output_aliases={4 + i: 1 + i for i in range(count)},
        scratch_shapes=[x_shape, *Engine.work_shapes(copies, 1)],
        compiler_params=PARAMS,
        name="cross_tiles",
    )(items, moments, low, high, *shared)

    step = 1
    while True:
        other = swap(stats, "res", step)
        step *= 2
        if step == size:
            break
        total, error = two_sum(stats[0], other[0])
        stats = jnp.stack([total, (stats[1] + other[1]) + error])

    copy_loss, total, maps, centre = pl.pallas_call(
        functools.partial(solve_kernel, copies=copies, atoms=local * size),
        in_specs=[VMEM] * 3,
        out_specs=[SMEM] + [VMEM] * 3,
        out_shape=[
            jax.ShapeDtypeStruct((copies,), F32),
            jax.ShapeDtypeStruct((8, LANES), F32),
            jax.ShapeDtypeStruct((14, copies, LANES), F32),
            jax.ShapeDtypeStruct((8, LANES), F32),
        ],
        scratch_shapes=[pltpu.VMEM((2, LANES, LANES), F32)],
        compiler_params=SMALL,
        name="solve",
    )(stats, other, noise)
    step = 1
    while step < lax.axis_size("samp"):
        total = total + swap(total, "samp", step)
        step *= 2
    mean_loss = total[0, 0] / (copies * lax.axis_size("samp"))
    grad = pl.pallas_call(
        functools.partial(gradient_kernel, copies=copies, tiles=tiles),
        in_specs=[VMEM] * 6,
        out_specs=VMEM,
        out_shape=jax.ShapeDtypeStruct((3, copies, local), F32),
        cost_estimate=pl.CostEstimate(flops=10**6, bytes_accessed=10**6, transcendentals=0),
        compiler_params=SMALL,
        name="gradient",
    )(maps, centre, coords_pred, coords_true, kind, shared[Engine.shared.index("acc")])
    return copy_loss, mean_loss, jnp.transpose(grad, (1, 0, 2))


def solution(mesh):
    in_specs = (P("samp", None, "res"), P(None, "res"), P("res"), P("res", None), P("samp"))
    out_specs = (P("samp"), P(), P("samp", None, "res"))
    return jax.shard_map(shards, mesh=mesh, in_specs=in_specs, out_specs=out_specs, check_vma=False)
```

```python
import functools

import jax
import jax.numpy as jnp
from jax import lax
from jax.experimental import pallas as pl
from jax.experimental.pallas import tpu as pltpu
from jax.sharding import PartitionSpec as P

LANES = 128
BAND = 2
SWEEPS = 20
SIGMA = 16.0
HALF_THRESHOLDS = (0.25, 0.5, 1.0, 2.0)
EPS = 0.25e-6
F32 = jnp.float32
BF16 = jnp.bfloat16


def roll(x, shift, axis=1):
    return pltpu.roll(x, shift, axis)


def two_sum(a, b):
    s = a + b
    t = s - a
    return s, (a - (s - t)) + (b - t)


def two_prod(a, b):
    def halves(x):
        t = x * 4097.0
        h = t - (t - x)
        return h, x - h

    p = a * b
    ah, al = halves(a)
    bh, bl = halves(b)
    return p, ((ah * bh - p) + ah * bl + al * bh) + al * bl


def pair_add(x, y):
    s, e = two_sum(x[0], y[0])
    return two_sum(s, e + (x[1] + y[1]))


def pair_neg(x):
    return -x[0], -x[1]


def pair_mul(x, y):
    p, e = two_prod(x[0], y[0])
    return two_sum(p, e + (x[0] * y[1] + x[1] * y[0]))


def pair_div(x, w):
    q = x[0] / w
    p, e = two_prod(q, w)
    return two_sum(q, (((x[0] - p) - e) + x[1]) / w)


def dot(a, b):
    return jnp.dot(a, b, preferred_element_type=F32)


def dot_nt(a, b):
    return lax.dot_general(a, b, (((1,), (1,)), ((), ())), preferred_element_type=F32)


def split3(x):
    a = x.astype(BF16).astype(F32)
    rest = x - a
    b = rest.astype(BF16).astype(F32)
    return a, b, (rest - b).astype(BF16).astype(F32)


def stack(a, b, axis):
    return jnp.concatenate([a, b], axis=axis)


def spread(steps, work, ticks):
    state = [0, 0]

    def tick():
        state[0] += 1
        while state[1] < len(steps) and state[1] * ticks * 3 < state[0] * len(steps) * 4:
            steps[state[1]]()
            state[1] += 1

    work(tick)
    for step in steps[state[1]:]:
        step()


class Engine:
    shared = ("v", "cut", "centre", "left", "point", "acc", "score", "count")
    work = ("true", "weight", "minus", "right", "d", "f")

    def __init__(self, copies, tiles, shared, work):
        self.copies = copies
        self.twos = copies // 2
        self.low, self.high, self.dummy = tiles, tiles + BAND, tiles + 2 * BAND
        for name, ref in zip(self.shared + self.work, (*shared, *work)):
            setattr(self, name, ref)

    @staticmethod
    def shared_shapes(tiles, copies):
        n, twos = tiles + 2 * BAND + 1, copies // 2
        return [
            jax.ShapeDtypeStruct(shape, dtype)
            for shape, dtype in (
                ((n, copies + 1, 8, LANES), F32),
                ((n, 1, LANES), F32),
                ((n, copies + 1, 8, LANES), F32),
                ((n, twos + 1, LANES, LANES), BF16),
                ((n, twos, 64, 2 * LANES), BF16),
                ((n, copies * 8, LANES), F32),
                ((copies, 8, LANES), F32),
                ((8, LANES), F32),
            )
        ]

    @staticmethod
    def work_shapes(copies, parts):
        twos = copies // 2
        return [[pltpu.VMEM((LANES, LANES), F32)] * 2] * 3 + [
            [pltpu.VMEM((parts, twos + 1, LANES, 2 * LANES), BF16)] * 2,
            [pltpu.VMEM((parts, twos + 1, LANES, 2 * LANES), F32)] * 2,
            [pltpu.VMEM((parts, twos, 2 * LANES, 2 * LANES), BF16)] * 2,
        ]

    def begin_right(self):
        pick = jnp.where(lax.broadcasted_iota(jnp.int32, (LANES, LANES), 0) == 7, 1.0, 0.0).astype(BF16)
        blank = jnp.zeros((64, LANES), BF16)
        for ref in self.right:
            for k in range(ref.shape[0]):
                for h in range(self.twos + 1):
                    ref[k, h, 64:, :LANES] = blank
                    ref[k, h, :64, LANES:] = blank
                ref[k, self.twos, :, LANES:] = pick

    def place(self, t, ref):
        blank = jnp.zeros((5, LANES), F32)
        for s in range(self.copies):
            self.v[t, s] = stack(ref[pl.ds(s, 3, stride=self.copies), :], blank, 0)
        self.v[t, self.copies] = stack(ref[3 * self.copies:3 * self.copies + 3, :], blank, 0)

    @staticmethod
    def unit(k):
        return jnp.where(lax.broadcasted_iota(jnp.int32, (8, LANES), 0) == k, 1.0, 0.0)

    def prep(self, t):
        groups = []
        for s in range(self.copies + 1):
            v = self.v[t, s]
            centre = jnp.broadcast_to(jnp.sum(v, axis=1, keepdims=True) * (1.0 / LANES), (8, LANES))
            self.centre[t, s] = centre
            y = v - centre
            norm = jnp.sum(y * y, axis=0, keepdims=True)
            x = (self.unit(4) + EPS * self.unit(5)) - 2.0 * y + norm * self.unit(3)
            if s == self.copies:
                x = x + self.unit(7) * self.cut[t]
            a, b, c = split3(x)
            groups.append(jnp.concatenate([a, a, b, a, b, c, b, c], axis=0))
            if s < self.copies:
                a, b, c = split3(v + self.unit(3))
                p = jnp.concatenate([a, b, c, jnp.zeros_like(a)], axis=0).astype(BF16)
                q = 32 * (s % 2)
                self.point[t, s // 2, q:q + 32, :LANES] = p
                self.point[t, s // 2, q:q + 32, LANES:] = p
        groups.append(jnp.zeros((64, LANES), F32))
        for h in range(self.twos + 1):
            self.left[t, h] = stack(groups[2 * h], groups[2 * h + 1], 0).astype(BF16).T

    def build(self, slot, k, g, j, s):
        y = self.v[j, s] - self.centre[g, s]
        norm = jnp.sum(y * y, axis=0, keepdims=True)
        a, b, c = split3(y + (self.unit(3) + self.unit(5)) + norm * self.unit(4))
        q, m = 64 * (s % 2), LANES * (s % 2)
        self.right[slot][k, s // 2, q:q + 64, m:m + LANES] = jnp.concatenate([a, b, a, c, b, a, c, b], axis=0).astype(BF16)

    def squares(self, slot, k, g, h):
        return dot(self.left[g, h], self.right[slot][k, h])

    def get(self, slot, h, k, lanes, shared):
        one = self.d[slot][0, h, k, lanes]
        if not shared:
            return one
        return jnp.where(self.upper(k), one, self.d[slot][1, h, k, lanes])

    @staticmethod
    def upper(k):
        shape = (k.stop - k.start, LANES)
        return lax.broadcasted_iota(jnp.int32, shape, 1) > lax.broadcasted_iota(jnp.int32, shape, 0) + k.start

    def weigh(self, slot, cuts, share, shared, tick):
        total = jnp.zeros((8, LANES), F32)
        for b in range(16):
            k = slice(8 * b, 8 * b + 8)
            d2 = jnp.maximum(self.get(slot, self.twos, k, slice(0, LANES), shared), EPS)
            dist = d2 * lax.rsqrt(d2)
            cut_j = jnp.where(self.upper(k), cuts[0], cuts[1]) if shared else cuts[0]
            cut_i = self.get(slot, self.twos, k, slice(LANES, 2 * LANES), shared)
            w = jnp.where(dist < cut_j, 0.0625, 0.0) + jnp.where(dist < cut_i, 0.0625, 0.0)
            if shared:
                row = lax.broadcasted_iota(jnp.int32, (8, LANES), 0) + 8 * b
                w = jnp.where(lax.broadcasted_iota(jnp.int32, (8, LANES), 1) == row, 0.0, w)
            self.true[slot][k, :] = dist
            self.weight[slot][k, :] = w
            self.minus[slot][k, :] = -w
            total = total + w
            tick()
        self.count[...] += total * share

    def factor(self, slot, share, shared, tick):
        for s in range(self.copies):
            h, m = s // 2, LANES * (s % 2)
            score = jnp.zeros((8, LANES), F32)
            blocks = []
            for q in range(8):
                k = slice(16 * q, 16 * q + 16)
                d2 = jnp.maximum(self.get(slot, h, k, slice(m, m + LANES), shared), EPS)
                r = lax.rsqrt(d2)
                diff = d2 * r - self.true[slot][k, :]
                spread = jnp.abs(diff)
                u = [jnp.tanh(t - spread) for t in HALF_THRESHOLDS]
                w = self.weight[slot][k, :]
                z = w * ((u[0] + u[1]) + (u[2] + u[3]))
                score = score + z[:8] + z[8:]
                slope = ((u[0] * u[0] + u[1] * u[1]) + (u[2] * u[2] + u[3] * u[3])) - 4.0
                f = slope * r * jnp.maximum(jnp.minimum(diff * 1e30, w), self.minus[slot][k, :])
                high = f.astype(BF16)
                low = (f - high.astype(F32)).astype(BF16)
                if shared:
                    blocks.append((high, low))
                else:
                    self.f[slot][0, h, k, m:m + LANES] = high
                    self.f[slot][0, h, LANES + 16 * q:LANES + 16 * q + 16, m:m + LANES] = low
                tick()
            for part, rows in enumerate(zip(*blocks)):
                whole = jnp.concatenate(rows, axis=0)
                mirror = whole.T
                for q in range(8):
                    k = slice(16 * q, 16 * q + 16)
                    upper = self.tri[0, k, :] > 0
                    start = LANES * part + 16 * q
                    self.f[slot][0, h, start:start + 16, m:m + LANES] = jnp.where(upper, whole[k], mirror[k])
                    self.f[slot][1, h, start:start + 16, m:m + LANES] = jnp.where(upper, mirror[k], whole[k])
            self.score[s] += score * share

    @staticmethod
    def fold(z):
        return [z[k:k + 8, m:m + LANES] + z[k + 8:k + 16, m:m + LANES] + z[k + 16:k + 24, m:m + LANES] for k, m in ((0, 0), (32, LANES))]

    def along_j(self, p, f):
        return self.fold(dot(p, f))

    def along_i(self, p, f):
        one = stack(f[:LANES, :LANES], f[LANES:, :LANES], 1)
        two = stack(f[:LANES, LANES:], f[LANES:, LANES:], 1)
        return self.fold(dot_nt(p, stack(one, two, 0)))

    def cross_build(self, item, slot):
        return [functools.partial(self.build, slot, 0, item[0], item[1], s) for s in range(self.copies + 1)]

    def cross_measure(self, item, slot):
        def step(h):
            self.d[slot][0, h] = self.squares(slot, 0, item[0], h)

        return [functools.partial(step, h) for h in [self.twos, *range(self.twos)]]

    def cross_factor(self, item, slot, tick):
        share = item[2].astype(F32) * 0.5
        self.weigh(slot, [self.cut[item[1]]], share, False, tick)
        self.factor(slot, share, False, tick)

    def add(self, t, h, parts):
        for q in range(2):
            self.acc[t, 8 * (2 * h + q):8 * (2 * h + q) + 8, :] += parts[q]

    def put(self, t, h, parts):
        for q in range(2):
            self.acc[t, 8 * (2 * h + q):8 * (2 * h + q) + 8, :] = parts[q]

    def cross_collect(self, item, slot):
        steps = []
        for h in range(self.twos):
            steps.append(lambda h=h: self.add(item[1], h, self.along_j(self.point[item[0], h], self.f[slot][0, h])))
            steps.append(lambda h=h: self.add(item[0], h, self.along_i(self.point[item[1], h], self.f[slot][0, h])))
        return steps

    def self_build(self, item, slot):
        return [functools.partial(self.build, slot, k, item[k], item[k], s) for s in range(self.copies + 1) for k in range(2)]

    def self_measure(self, item, slot):
        def step(h, k):
            self.d[slot][k, h] = self.squares(slot, k, item[k], h)

        return [functools.partial(step, h, k) for h in [self.twos, *range(self.twos)] for k in range(2)]

    def self_factor(self, item, slot, tick):
        self.weigh(slot, [self.cut[item[0]], self.cut[item[1]]], 1.0, True, tick)
        self.factor(slot, 1.0, True, tick)

    def self_collect(self, item, slot):
        steps = []
        for h in range(self.twos):
            for k in range(2):
                steps.append(lambda h=h, k=k: self.put(item[k], h, self.along_j(self.point[item[k], h], self.f[slot][k, h])))
        return steps

    def half(self, kind, items, slot):
        last, now, soon, later = items
        steps = getattr(self, kind + "_collect")(last, 1 - slot)
        steps += getattr(self, kind + "_measure")(soon, 1 - slot)
        steps += getattr(self, kind + "_build")(later, 1 - slot)
        spread(steps, lambda tick: getattr(self, kind + "_factor")(now, slot, tick), 16 + 8 * self.copies)

    def begin_list(self, kind, item, n):
        steps = getattr(self, kind + "_build")(item(0), 0)
        steps += getattr(self, kind + "_measure")(item(0), 0)
        for i in (1, 2):
            steps += getattr(self, kind + "_build")(item(jnp.minimum(i, n - 1)), i % 2)
        for step in steps:
            step()

    def run_list(self, kind, item, n, dummy):
        def at(p):
            return tuple(jnp.where(p < 0, dummy, z) for z in item(jnp.clip(p, 0, n - 1)))

        run = 4 if isinstance(n, int) and n % 4 == 0 else 2

        @pl.loop(0, n // run)
        def _(i):
            for k in range(run):
                p = run * i + k
                self.half(kind, [at(p - 1), at(p), at(p + 1), at(p + 3)], k % 2)

    def end_list(self, kind, item, n, dummy):
        def last(i, slot):
            return getattr(self, kind + "_collect")(item(i), slot)

        def odd():
            before = tuple(jnp.where(n > 1, z, dummy) for z in item(jnp.maximum(n - 2, 0)))
            steps = getattr(self, kind + "_collect")(before, 1)
            spread(steps, lambda tick: getattr(self, kind + "_factor")(item(n - 1), 0, tick), 16 + 8 * self.copies)
            for step in last(n - 1, 0):
                step()

        def even():
            for step in last(n - 1, 1):
                step()

        if isinstance(n, int):
            (odd if n % 2 else even)()
        else:
            pl.when(n % 2 == 1)(odd)
            pl.when(n % 2 == 0)(even)

    def scores(self, weight_total):
        rows = [jnp.sum(self.score[s], axis=0, keepdims=True) for s in range(self.copies)]
        rows += [jnp.sum(self.count[...], axis=0, keepdims=True), weight_total]
        total = jnp.zeros((8, LANES), F32)
        for k, x in enumerate(rows):
            total = total + x * self.unit(2 + k)
        return jnp.broadcast_to(jnp.sum(total, axis=1, keepdims=True), (8, LANES))


def self_kernel(base_ref, part_ref, pred_ref, true_ref, kind_ref, *refs, copies, tiles):
    count = len(Engine.shared)
    shared, (items, moment_ref), (x_ref, sum_ref, tri), work = refs[:count], refs[count:count + 2], refs[count + 2:count + 5], refs[count + 5:]
    e = Engine(copies, tiles, shared, work)
    e.tri = tri
    base = base_ref[0]
    rows = 3 * copies
    e.begin_right()
    for ref in [e.score, e.count, x_ref, sum_ref, *(r.at[e.dummy] for r in shared[:5])]:
        ref[...] = jnp.zeros_like(ref)
    row = lax.broadcasted_iota(jnp.int32, (LANES, LANES), 0)
    lane = lax.broadcasted_iota(jnp.int32, (LANES, LANES), 1)
    tri[0] = jnp.where(lane > row, 1.0, 0.0).astype(BF16)

    place = lax.broadcasted_iota(jnp.int32, (1, LANES), 1)

    def append(state, hit, g, j, share):
        n, row = state
        return n + hit, jnp.where(place == n, (share * 256 + g) * 256 + j, row)

    def partner_bits(t):
        bits = 0
        for k in range(1, part_ref.shape[0]):
            bits = bits | lax.shift_left(jnp.int32(1), (part_ref[k, t] - base) - (t - BAND))
        return lambda offset: lax.shift_right_logical(bits, BAND + offset) & 1

    unroll = next(u for u in (12, 6, 4, 3, 2, 1) if tiles % u == 0)

    @pl.loop(0, tiles // unroll)
    def _(m):
        for q in range(unroll):
            t = m * unroll + q
            sl = pl.ds(pl.multiple_of(t * LANES, LANES), LANES)
            kind = kind_ref[:, sl]
            weight = jnp.where(kind == 1, 5.0, jnp.where(kind == 2, 10.0, 1.0))
            for c in range(3):
                x_ref[q, c * copies:(c + 1) * copies, :] = pred_ref[c, :, sl] * 0.5
            x_ref[q, rows:rows + 3, :] = true_ref[:, sl] * 0.5
            e.place(t, x_ref.at[q])
            e.cut[t] = jnp.where(kind == 1, 15.0, 7.5)
            x = x_ref[q]
            wx = x * weight
            terms = [wx * x[rows + c:rows + c + 1] for c in range(3)] + [wx, wx * x]
            for i, term in enumerate(terms):
                total, error = two_sum(sum_ref[0, i], term)
                sum_ref[0, i] = total
                sum_ref[1, i] += error
            sum_ref[0, 5, 0:1, :] += weight
            e.prep(t)

    blank = jnp.zeros((LANES - 80, LANES), F32)
    high, low = (jnp.concatenate([sum_ref[part, i] for i in range(5)] + [blank], axis=0).T for part in range(2))
    sums = [(high[8 * k:8 * k + 8], low[8 * k:8 * k + 8]) for k in range(16)]
    while len(sums) > 1:
        sums = [pair_add(a, b) for a, b in zip(sums[::2], sums[1::2])]
    sums = sums[0]
    for k in (4, 2, 1):
        sums = pair_add(sums, (roll(sums[0], k, 0), roll(sums[1], k, 0)))
    for part in range(2):
        moment_ref[part] = sums[part] * e.unit(0)
    moment_ref[2] = jnp.broadcast_to(sum_ref[0, 5, 0:1, :], (8, LANES))

    def twin(i):
        return 2 * i, 2 * i + 1

    half = tiles // 2
    e.begin_list("self", twin, half)
    e.run_list("self", twin, half, e.dummy)

    state = jnp.int32(0), jnp.zeros((1, LANES), jnp.int32)
    edges = []
    for t in range(tiles):
        bits = partner_bits(t)
        for o in range(1, BAND + 1):
            if t >= o:
                state = append(state, bits(-o), t - o, t, 2)
            else:
                edges.append((bits(-o), e.low + BAND + t - o, t, 1))
            if t + o >= tiles:
                edges.append((bits(o), t, e.high + t + o - tiles, 1))
    for edge in edges:
        state = append(state, *edge)
    n, row = state
    row = jnp.where((place == 0) & (n == 0), e.dummy * 257, row)
    items[...] = jnp.where(place == LANES - 1, jnp.maximum(n, 1), row)
    e.end_list("self", twin, half, e.dummy)


def cross_kernel(items, moment_ref, low_ref, high_ref, *refs, copies, tiles):
    count = len(Engine.shared)
    stat_ref, shared, x_ref, work = refs[count], refs[count + 1:2 * count + 1], refs[2 * count + 1], refs[2 * count + 2:]
    e = Engine(copies, tiles, shared, work)
    rows = 3 * copies
    e.begin_right()

    def item(i):
        word = items[0, i]
        return lax.shift_right_logical(word, 8) & 255, word & 255, lax.shift_right_logical(word, 16)

    n = items[0, LANES - 1]
    e.begin_list("cross", item, n)
    for i, (ref, start) in enumerate(((low_ref, e.low), (high_ref, e.high))):
        for q in range(BAND):
            t = start + q
            x_ref[BAND * i + q] = ref[:, q * LANES:(q + 1) * LANES]
            e.place(t, x_ref.at[BAND * i + q])
            e.cut[t] = x_ref[BAND * i + q, rows + 3:rows + 4, :]
            e.prep(t)
    e.run_list("cross", item, n, e.dummy)
    e.end_list("cross", item, n, e.dummy)
    stat_ref[0] = moment_ref[0] + e.scores(moment_ref[2, 0:1, :])
    stat_ref[1] = moment_ref[1]


def solve_kernel(stat_ref, other_ref, noise_ref, loss_ref, sum_ref, m_ref, k_ref, s_ref, *, copies, atoms):
    rows = 3 * copies
    stats, error = two_sum(stat_ref[0], other_ref[0])
    low = (stat_ref[1] + other_ref[1]) + error
    for part, x in enumerate((stats, low)):
        s_ref[part] = jnp.broadcast_to(x[0:1], (LANES, LANES)).T

    def per_copy(c, q, scale):
        return tuple(s_ref[part, 16 * q + c * copies:16 * q + (c + 1) * copies, :] * scale for part in range(2))

    def shared(r, q, scale):
        return tuple(s_ref[part, 16 * q + r:16 * q + r + 1, :] * scale for part in range(2))

    def wide(x):
        return tuple(jnp.broadcast_to(v, (copies, LANES)) for v in x)

    weight_sum = jnp.broadcast_to(stats[copies + 3:copies + 4], (copies, LANES))
    count = jnp.broadcast_to(stats[copies + 2:copies + 3], (copies, LANES)) * 16.0
    score = stats[2:copies + 2] * 2.0 + 0.5 * count
    pred_sum = [wide(per_copy(c, 3, 2.0)) for c in range(3)]
    true_sum = [wide(shared(rows + c, 3, 2.0)) for c in range(3)]
    pred_mean = [pair_div(x, weight_sum) for x in pred_sum]
    true_mean = [pair_div(x, weight_sum) for x in true_sum]
    cov = [[pair_add(wide(per_copy(c, d, 4.0)), pair_neg(pair_mul(pred_sum[c], true_mean[d]))) for d in range(3)] for c in range(3)]
    ct = {}
    for d in range(3):
        for e in range(d + 1):
            ct[d, e] = pair_add(wide(shared(rows + d, e, 4.0)), pair_neg(pair_mul(true_sum[d], true_mean[e])))
    var = None
    for c in range(3):
        term = pair_add(wide(per_copy(c, 4, 4.0)), pair_neg(pair_mul(pred_sum[c], pred_mean[c])))
        var = term if var is None else pair_add(var, term)

    x = [[cov[c][d][0] for d in range(3)] for c in range(3)]
    frobenius = jnp.sqrt(sum(x[c][d] * x[c][d] for c in range(3) for d in range(3)))
    x = [[x[c][d] / frobenius for d in range(3)] for c in range(3)]

    def sweep(_, flat):
        x = [flat[0:3], flat[3:6], flat[6:9]]
        gram = {}
        for a in range(3):
            for b in range(a + 1):
                gram[a, b] = gram[b, a] = x[a][0] * x[b][0] + x[a][1] * x[b][1] + x[a][2] * x[b][2]
        for a in range(3):
            for b in range(a + 1):
                gram[a, b] = gram[b, a] = (1.5 if a == b else 0.0) - 0.5 * gram[a, b]
        return tuple(gram[a, 0] * x[0][d] + gram[a, 1] * x[1][d] + gram[a, 2] * x[2][d] for a in range(3) for d in range(3))

    flat = lax.fori_loop(0, SWEEPS, sweep, tuple(v for line in x for v in line), unroll=True)
    x = [flat[0:3], flat[3:6], flat[6:9]]

    square = var
    nothing = jnp.zeros((copies, LANES), F32)
    for c in range(3):
        for d in range(3):
            square = pair_add(square, pair_mul((-2.0 * x[c][d], nothing), cov[c][d]))
    for d in range(3):
        for e in range(d + 1):
            gram = None
            for c in range(3):
                term = two_prod(x[c][d], x[c][e])
                gram = term if gram is None else pair_add(gram, term)
            if d != e:
                gram = (2.0 * gram[0], 2.0 * gram[1])
            square = pair_add(square, pair_mul(gram, ct[d, e]))

    noise = noise_ref[...]
    loss_weight = (noise * noise + SIGMA * SIGMA) / (noise * SIGMA * (noise * SIGMA))
    mean_square = (square[0] + square[1]) / (3.0 * weight_sum)
    loss = loss_weight * mean_square + 1.0 - score / count
    for s in range(copies):
        loss_ref[s] = loss[s, 0]
    sum_ref[...] = jnp.broadcast_to(jnp.sum(loss, axis=0, keepdims=True), (8, LANES))

    grad_scale = 16.0 * atoms
    for c in range(3):
        for d in range(3):
            m_ref[3 * c + d] = x[c][d]
        m_ref[9 + c] = pred_mean[c][0]
    k_ref[...] = sum(true_mean[c][0][0:1] * Engine.unit(c) for c in range(3))
    m_ref[12] = grad_scale * 2.0 * loss_weight / (3.0 * weight_sum)
    m_ref[13] = grad_scale / count


def gradient_kernel(m_ref, k_ref, pred_ref, true_ref, kind_ref, acc_ref, grad_ref, *, copies, tiles):
    for t in range(tiles):
        sl = slice(t * LANES, (t + 1) * LANES)
        kind = kind_ref[:, sl]
        weight = jnp.where(kind == 1, 5.0, jnp.where(kind == 2, 10.0, 1.0))
        centred = true_ref[:, sl] - k_ref[0:3, :]
        factor_sum = 0.5 * acc_ref[t, pl.ds(3, copies, stride=8), :]
        for c in range(3):
            target = m_ref[3 * c] * centred[0:1] + m_ref[3 * c + 1] * centred[1:2] + m_ref[3 * c + 2] * centred[2:3] + m_ref[9 + c]
            pred = pred_ref[c, :, sl]
            pull = pred * factor_sum - acc_ref[t, pl.ds(c, copies, stride=8), :]
            grad_ref[c, :, sl] = m_ref[12] * weight * (pred - target) - m_ref[13] * pull


def pack_kernel(pred_hbm, true_hbm, kind_hbm, part_hbm, noise_hbm, first_ref, last_ref, pred_ref, true_ref, kind_ref, part_ref, noise_ref, noise_smem, sems, *, copies, tiles):
    span = BAND * LANES
    moves = [
        pltpu.make_async_copy(source, target, sems.at[i])
        for i, (source, target) in enumerate(
            ((pred_hbm, pred_ref), (true_hbm, true_ref), (kind_hbm, kind_ref), (part_hbm, part_ref), (noise_hbm, noise_smem))
        )
    ]
    for move in moves:
        move.start()
    for move in moves:
        move.wait()
    for ref, start in ((first_ref, 0), (last_ref, tiles * LANES - span)):
        sl = slice(start, start + span)
        cut = jnp.where(kind_ref[:, sl] == 1, 15.0, 7.5)
        ref[...] = jnp.concatenate([pred_ref[c, :, sl] * 0.5 for c in range(3)] + [true_ref[:, sl] * 0.5, cut], axis=0)
    row = lax.broadcasted_iota(jnp.int32, (copies, LANES), 0)
    noise = jnp.zeros((copies, LANES), F32)
    for s in range(copies):
        noise = jnp.where(row == s, noise_smem[s], noise)
    noise_ref[...] = noise


VMEM = pl.BlockSpec(memory_space=pltpu.VMEM)
SMEM = pl.BlockSpec(memory_space=pltpu.SMEM)
PARAMS = pltpu.CompilerParams(vmem_limit_bytes=40 * 2**20)
SMALL = pltpu.CompilerParams(vmem_limit_bytes=4 * 2**20)


def swap(x, axis, step):
    return lax.ppermute(x, axis, [(i, i ^ step) for i in range(lax.axis_size(axis))])


def shards(coords_pred, coords_true, atom_kind, partners, noise_level):
    copies, _, local = coords_pred.shape
    tiles = partners.shape[0]
    rows = 3 * copies
    size = lax.axis_size("res")
    kind = atom_kind[None]
    coords_pred = jnp.transpose(coords_pred, (1, 0, 2))
    partners = partners.T
    base = (lax.axis_index("res") * tiles)[None].astype(jnp.int32)
    stats_shape = jax.ShapeDtypeStruct((2, 8, LANES), F32)

    block = jax.ShapeDtypeStruct((rows + 4, BAND * LANES), F32)
    same = [jax.ShapeDtypeStruct(x.shape, x.dtype) for x in (coords_pred, coords_true, kind, partners)]
    first, last, coords_pred, coords_true, kind, partners, noise = pl.pallas_call(
        functools.partial(pack_kernel, copies=copies, tiles=tiles),
        in_specs=[pl.BlockSpec(memory_space=pltpu.HBM)] * 5,
        out_specs=[VMEM] * 7,
        out_shape=[block, block, *same, jax.ShapeDtypeStruct((copies, LANES), F32)],
        scratch_shapes=[pltpu.SMEM((copies,), F32), pltpu.SemaphoreType.DMA((5,))],
        compiler_params=SMALL,
        name="pack",
    )(*(pltpu.with_memory_space_constraint(x, pltpu.HBM) for x in (coords_pred, coords_true, kind, partners, noise_level)))
    forward = [(i, i + 1) for i in range(size - 1)]
    low = lax.ppermute(last, "res", forward)
    high = lax.ppermute(first, "res", [(b, a) for a, b in forward])

    shared_shapes = Engine.shared_shapes(tiles, copies)
    count = len(shared_shapes)
    x_shape = pltpu.VMEM((14, 16, LANES), F32)
    *shared, items, moments = pl.pallas_call(
        functools.partial(self_kernel, copies=copies, tiles=tiles),
        in_specs=[SMEM, SMEM] + [VMEM] * 3,
        out_specs=[VMEM] * (count + 2),
        out_shape=[*shared_shapes, jax.ShapeDtypeStruct((1, LANES), jnp.int32), jax.ShapeDtypeStruct((3, 8, LANES), F32)],
        scratch_shapes=[x_shape, pltpu.VMEM((2, 6, 16, LANES), F32), pltpu.VMEM((1, LANES, LANES), BF16), *Engine.work_shapes(copies, 2)],
        compiler_params=PARAMS,
        cost_estimate=pl.CostEstimate(flops=10**8, bytes_accessed=10**6, transcendentals=10**7),
        name="self_tiles",
    )(base, partners, coords_pred, coords_true, kind)
    stats, *shared = pl.pallas_call(
        functools.partial(cross_kernel, copies=copies, tiles=tiles),
        in_specs=[SMEM] + [VMEM] * (3 + count),
        out_specs=[VMEM] * (1 + count),
        out_shape=[stats_shape, *shared_shapes],
        input_output_aliases={4 + i: 1 + i for i in range(count)},
        scratch_shapes=[x_shape, *Engine.work_shapes(copies, 1)],
        compiler_params=PARAMS,
        name="cross_tiles",
    )(items, moments, low, high, *shared)

    step = 1
    while True:
        other = swap(stats, "res", step)
        step *= 2
        if step == size:
            break
        total, error = two_sum(stats[0], other[0])
        stats = jnp.stack([total, (stats[1] + other[1]) + error])

    copy_loss, total, maps, centre = pl.pallas_call(
        functools.partial(solve_kernel, copies=copies, atoms=local * size),
        in_specs=[VMEM] * 3,
        out_specs=[SMEM] + [VMEM] * 3,
        out_shape=[
            jax.ShapeDtypeStruct((copies,), F32),
            jax.ShapeDtypeStruct((8, LANES), F32),
            jax.ShapeDtypeStruct((14, copies, LANES), F32),
            jax.ShapeDtypeStruct((8, LANES), F32),
        ],
        scratch_shapes=[pltpu.VMEM((2, LANES, LANES), F32)],
        compiler_params=SMALL,
        name="solve",
    )(stats, other, noise)
    step = 1
    while step < lax.axis_size("samp"):
        total = total + swap(total, "samp", step)
        step *= 2
    mean_loss = total[0, 0] / (copies * lax.axis_size("samp"))
    grad = pl.pallas_call(
        functools.partial(gradient_kernel, copies=copies, tiles=tiles),
        in_specs=[VMEM] * 6,
        out_specs=VMEM,
        out_shape=jax.ShapeDtypeStruct((3, copies, local), F32),
        cost_estimate=pl.CostEstimate(flops=10**6, bytes_accessed=10**6, transcendentals=0),
        compiler_params=SMALL,
        name="gradient",
    )(maps, centre, coords_pred, coords_true, kind, shared[Engine.shared.index("acc")])
    return copy_loss, mean_loss, jnp.transpose(grad, (1, 0, 2))


def solution(mesh):
    in_specs = (P("samp", None, "res"), P(None, "res"), P("res"), P("res", None), P("samp"))
    out_specs = (P("samp"), P(), P("samp", None, "res"))
    return jax.shard_map(shards, mesh=mesh, in_specs=in_specs, out_specs=out_specs, check_vma=False)
```
